512 devices in a mesh: row: 16 (over y, x_lo), col: 32 (over x_hi, z, core).
Axes of the slice: x: 4 (x_hi: 2, x_lo: 2; x = x_hi * 2 + x_lo), y: 8, z: 8, core: 2. Of those that a mesh axis runs over, the one named last changes fastest.
Arguments:
- tokens: float32 [128, 512, 128], P('row', 'col'), may hold values from -6 to 6
- cotangent: float32 [128, 512, 128], P('row', 'col'), may hold values from -6 to 6
- conv_weight: float32 [3, 3, 128], replicated, may hold values from -1 to 1
- w_query: float32 [128, 128], replicated, may hold values from -8 to 8, as said below
- w_key: float32 [128, 128], replicated, may hold values from -0.5 to 0.5
- w_value: float32 [128, 128], replicated, may hold values from -0.5 to 0.5
- w_out: float32 [128, 128], replicated, may hold values from -0.5 to 0.5
Outputs:
- output: float32 [128, 512, 128], P('row', 'col')
- d_tokens: float32 [128, 512, 128], P('row', 'col')
- g_conv: float32 [3, 3, 128], replicated
- g_query: float32 [128, 128], replicated
- g_key: float32 [128, 128], replicated
- g_value: float32 [128, 128], replicated
- g_out: float32 [128, 128], replicated
The draws below stay inside these ranges and needn't reach their ends.
Inputs may be any that keep to these rules, and one draw needn't show every extreme that they name: `w_query`: A real matrix of independent entries.
All inputs are finite; a program needn't handle non-finite values.
Results may differ from the reference program's by a relative error of at most 0.0003.
Values sent between devices are 32-bit elements; how exact they have to be, the bound alone decides.
No kernel may reach another device: no remote copies, remote signals or barrier semaphores. Data moves between devices by JAX's collectives and lax.ppermute only.
A program may use at most 64 MiB of HBM per device.

```python
import jax
import jax.numpy as jnp
from jax import lax

C = 128
HEADS = 2
POOL = 32
NR = 128
NC = 512


def draw_w_query(key, part):
    key = jax.random.fold_in(key, 11)
    edge_value = (3.0 / C) ** 0.5
    return jax.random.uniform(key, (C, C), jnp.float32, -edge_value, edge_value)


def levels(key, shape, shards, low, largest):
    loudness = 1.0
    for dim, blocks in shards:
        draws = jax.random.uniform(jax.random.fold_in(jax.random.fold_in(key, 6), dim), (blocks,), jnp.float32, low / len(shards), largest / len(shards))
        loudness = loudness * jnp.repeat(jnp.exp(draws), shape[dim] // blocks).reshape((-1,) + (1,) * (len(shape) - 1 - dim))
    return loudness


def centred(own_key, shape, scale, limit, shards=(), kind=jnp.bfloat16):
    result = scale * jax.random.normal(own_key, shape, jnp.float32)
    if shards:
        result = result * levels(own_key, shape, shards, -0.22, 0.18)
    return jnp.clip(result, -limit, limit).astype(kind)


def setup_inputs(seed: int = 0) -> dict:
    key_list = jax.random.split(jax.random.key(seed), 8)
    return {
        "tokens": centred(key_list[0], (NR, NC, C), 1.0, 6.0, ((0, 16), (1, 32)), jnp.float32),
        "cotangent": centred(key_list[1], (NR, NC, C), 1.0, 6.0, ((0, 16), (1, 32)), jnp.float32),
        "conv_weight": centred(key_list[2], (3, 3, C), 0.25, 1.0, (), jnp.float32),
        "w_query": draw_w_query(jax.random.fold_in(key_list[7], 71), 0),
        "w_key": centred(key_list[4], (C, C), C ** -0.5, 0.5, (), jnp.float32),
        "w_value": centred(key_list[5], (C, C), C ** -0.5, 0.5, (), jnp.float32),
        "w_out": centred(key_list[6], (C, C), C ** -0.5, 0.5, (), jnp.float32),
    }


def product(left, right):
    return jnp.dot(left, right, precision=lax.Precision.HIGHEST, preferred_element_type=jnp.float32)

def normalize(values_in):
    average = lax.optimization_barrier(jnp.mean(values_in, -1, keepdims=True))
    centered = values_in - average
    inv_std = lax.rsqrt(lax.optimization_barrier(jnp.mean(centered * centered, -1, keepdims=True)) + 1e-06)
    return (centered * inv_std, inv_std)

def norm_back(gradient, normed, inv_std):
    return inv_std * (gradient - lax.optimization_barrier(jnp.mean(gradient, -1, keepdims=True)) - normed * lax.optimization_barrier(jnp.mean(gradient * normed, -1, keepdims=True)))

def conv_apply(tokens, padded, conv_weight):
    tile_rows, tile_cols = (tokens.shape[0], tokens.shape[1])
    total = tokens
    for offset_r in range(3):
        for offset_c in range(3):
            total = total + conv_weight[offset_r, offset_c] * padded[offset_r:offset_r + tile_rows, offset_c:offset_c + tile_cols]
    return total

def conv_back(gradient, padded_grad, conv_weight):
    tile_rows, tile_cols = (gradient.shape[0], gradient.shape[1])
    total = gradient
    for offset_r in range(3):
        for offset_c in range(3):
            total = total + conv_weight[offset_r, offset_c] * padded_grad[2 - offset_r:2 - offset_r + tile_rows, 2 - offset_c:2 - offset_c + tile_cols]
    return total

def conv_weight_grad(gradient, padded):
    tile_rows, tile_cols = (gradient.shape[0], gradient.shape[1])
    outer = []
    for offset_r in range(3):
        inner = []
        for offset_c in range(3):
            inner.append(lax.optimization_barrier(jnp.sum(padded[offset_r:offset_r + tile_rows, offset_c:offset_c + tile_cols] * gradient, axis=(0, 1))))
        outer.append(jnp.stack(inner))
    return jnp.stack(outer)

def attend(normed_blk, grad_blk, w_query, w_out, key_rows, values):
    channels = key_rows.shape[1]
    head_width = channels // HEADS
    score_scale = head_width ** (-0.5)
    query_rows = product(normed_blk, w_query)
    d_att = product(grad_blk, w_out.T)
    att_parts, dq_parts, dk_parts, dv_parts = ([], [], [], [])
    for head_index in range(HEADS):
        low = head_index * head_width
        query_h = query_rows[:, low:low + head_width]
        key_h = key_rows[:, low:low + head_width]
        value_h = values[:, low:low + head_width]
        d_out_h = d_att[:, low:low + head_width]
        scores = product(query_h, key_h.T) * score_scale
        highest = lax.optimization_barrier(jnp.max(scores, -1, keepdims=True))
        weights = jnp.exp(scores - highest)
        probs = weights / lax.optimization_barrier(jnp.sum(weights, -1, keepdims=True))
        att_parts.append(product(probs, value_h))
        d_probs = product(d_out_h, value_h.T)
        d_scores = probs * (d_probs - lax.optimization_barrier(jnp.sum(d_probs * probs, -1, keepdims=True)))
        dq_parts.append(product(d_scores, key_h) * score_scale)
        dk_parts.append(product(d_scores.T, query_h) * score_scale)
        dv_parts.append(product(probs.T, d_out_h))
    return (jnp.concatenate(att_parts, 1), jnp.concatenate(dq_parts, 1), jnp.concatenate(dk_parts, 1), jnp.concatenate(dv_parts, 1))

def reference(tokens, cotangent, conv_weight, w_query, w_key, w_value, w_out):
    tile_rows, tile_cols, channels = tokens.shape
    padded = jnp.pad(tokens, ((1, 1), (1, 1), (0, 0)))
    mixed_tokens = conv_apply(tokens, padded, conv_weight)
    normed, inv_std = normalize(mixed_tokens)
    win_r = tile_rows // POOL
    win_c = tile_cols // POOL
    pooled = normed.reshape(POOL, win_r, POOL, win_c, channels).mean(axis=(1, 3)).reshape(POOL * POOL, channels)
    pooled_n, pooled_inv = normalize(pooled)
    key_rows = product(pooled_n, w_key)
    values = product(pooled_n, w_value)
    tok_count = tile_rows * tile_cols
    block_rows = min(1024, tok_count)
    flat_n = normed.reshape(tok_count // block_rows, block_rows, channels)
    flat_g = cotangent.reshape(tok_count // block_rows, block_rows, channels)

    def block_step(totals, inputs):
        d_keys, d_values, grad_out, grad_query = totals
        normed_blk, grad_blk = inputs
        att, d_query, part_k, part_v = attend(normed_blk, grad_blk, w_query, w_out, key_rows, values)
        totals = (d_keys + part_k, d_values + part_v, grad_out + product(att.T, grad_blk), grad_query + product(normed_blk.T, d_query))
        return (totals, (product(att, w_out), product(d_query, w_query.T)))
    empty_keys = jnp.zeros((POOL * POOL, channels), jnp.float32)
    empty_square = jnp.zeros((channels, channels), jnp.float32)
    totals, (att_out, d_normed) = lax.scan(block_step, (empty_keys, empty_keys, empty_square, empty_square), (flat_n, flat_g))
    d_keys, d_values, grad_out, grad_query = totals
    output = mixed_tokens + att_out.reshape(tile_rows, tile_cols, channels)
    d_pooled = norm_back(product(d_keys, w_key.T) + product(d_values, w_value.T), pooled_n, pooled_inv)
    spread = d_pooled.reshape(POOL, 1, POOL, 1, channels) / float(win_r * win_c)
    spread = jnp.broadcast_to(spread, (POOL, win_r, POOL, win_c, channels)).reshape(tile_rows, tile_cols, channels)
    d_normed = d_normed.reshape(tile_rows, tile_cols, channels) + spread
    d_mixed = cotangent + norm_back(d_normed, normed, inv_std)
    padded_grad = jnp.pad(d_mixed, ((1, 1), (1, 1), (0, 0)))
    d_tokens = conv_back(d_mixed, padded_grad, conv_weight)
    grad_conv = conv_weight_grad(d_mixed, padded)
    root = float(tok_count) ** (-0.5)
    grad_key = product(pooled_n.T, d_keys) / float(POOL)
    grad_value = product(pooled_n.T, d_values) / float(POOL)
    return (output, d_tokens, grad_conv * root, grad_query * root, grad_key, grad_value, grad_out * root)
```

```python
import jax
import jax.numpy as jnp
from jax import lax
from jax.experimental import pallas as pl
from jax.experimental.pallas import tpu as pltpu
from jax.sharding import Mesh, PartitionSpec as P

HEADS = 2
POOL = 32
ROW = ("y", "xl")
COL = ("xh", "z", "c")
CHIPS = ("xl", "y", "xh", "z")
FAR = ("y", "xh", "z")
NEAR = ("xl", "c")
HALO = 64


def product(left, right, dims=((1,), (0,))):
    return lax.dot_general(
        left,
        right,
        (dims, ((), ())),
        precision=lax.Precision.HIGHEST,
        preferred_element_type=jnp.float32,
    )


def normalize(values_in):
    average = jnp.mean(values_in, -1, keepdims=True)
    centered = values_in - average
    inv_std = lax.rsqrt(jnp.mean(centered * centered, -1, keepdims=True) + 1e-06)
    return (centered * inv_std, inv_std)


def norm_back(gradient, normed, inv_std):
    return inv_std * (
        gradient
        - jnp.mean(gradient, -1, keepdims=True)
        - normed * jnp.mean(gradient * normed, -1, keepdims=True)
    )


def neighbours(low_side, high_side, axis):
    peers = lax.axis_size(axis)
    up = [(i, i + 1) for i in range(peers - 1)]
    down = [(i + 1, i) for i in range(peers - 1)]
    return lax.ppermute(high_side, axis, up), lax.ppermute(low_side, axis, down)


def halo(tokens, cotangent):
    cols = tokens.shape[1]
    low = jnp.concatenate([tokens[:2], cotangent[:1]])
    high = jnp.concatenate([tokens[-2:], cotangent[-1:]])
    before, after = neighbours(low, high, ROW)
    tall_t = jnp.concatenate([before[:2], tokens, after[:2]])
    tall_g = jnp.concatenate([before[2:], cotangent, after[2:]])
    rows_t, rows_g = tall_t.shape[0], tall_g.shape[0]

    def side(first_t, first_g):
        part_t = tall_t[:, first_t : first_t + 2].reshape(2 * rows_t, -1)
        return jnp.concatenate([part_t, tall_g[:, first_g]])

    before, after = neighbours(side(0, 0), side(cols - 2, cols - 1), COL)

    def parts(received):
        return (
            received[: 2 * rows_t].reshape(rows_t, 2, -1),
            received[2 * rows_t :].reshape(rows_g, 1, -1),
        )

    (before_t, before_g), (after_t, after_g) = parts(before), parts(after)
    return (
        jnp.concatenate([before_t, tall_t, after_t], 1),
        jnp.concatenate([before_g, tall_g, after_g], 1),
    )


def ring(extended):
    rows, cols, channels = extended.shape
    used = 2 * cols + 2 * (rows - 2)
    return jnp.concatenate(
        [
            extended[0],
            extended[-1],
            extended[1:-1, 0],
            extended[1:-1, -1],
            jnp.zeros((HALO - used, channels), extended.dtype),
        ]
    )


def attention(keys, normed, normed_ring, grad, grad_ring, w_query, w_key, w_value, w_out):
    channels = keys.shape[1]
    count = normed.shape[0]
    width = channels // HEADS
    scale = width ** (-0.5)
    tokens_t = jnp.concatenate([normed, normed_ring]).T
    grads_t = jnp.concatenate([grad, grad_ring]).T
    query_t = product(w_query, tokens_t, ((0,), (0,)))
    d_att_t = product(w_out, grads_t)
    to_keys, to_values = [], []
    for head in range(HEADS):
        part = slice(head * width, (head + 1) * width)
        to_keys.append(product(w_key[:, part], query_t[part]) * scale)
        to_values.append(product(w_value[:, part], d_att_t[part]))
    inner = [x[:, :count] for x in to_keys], [x[:, :count] for x in to_values]
    outer = [x[:, count:] for x in to_keys], [x[:, count:] for x in to_values]
    query_keys = jnp.concatenate(inner[0] + outer[0], 1)
    d_att_values = jnp.concatenate(inner[1] + outer[1], 1)
    scores = product(keys, query_keys)
    weights = jnp.exp(scores - jnp.max(scores, 0, keepdims=True))
    probs = weights * (1.0 / jnp.sum(weights, 0, keepdims=True))
    d_probs = product(keys, d_att_values)
    att_keys = product(keys, probs, ((0,), (0,)))
    d_scores = probs * (d_probs - jnp.sum(d_probs * probs, 0, keepdims=True))
    d_query_keys = product(keys, d_scores, ((0,), (0,)))
    wide = HEADS * count
    both = ((1,), (1,))
    d_pooled_sum = product(d_scores[:, :wide], query_keys[:, :wide], both) + product(
        probs[:, :wide], d_att_values[:, :wide], both
    )
    att_t, dq_t, dq_ring_t, g_key, g_value = [], [], [], [], []
    ring_count = normed_ring.shape[0]
    for head in range(HEADS):
        part = slice(head * width, (head + 1) * width)
        own = slice(head * count, (head + 1) * count)
        far = slice(wide + head * ring_count, wide + (head + 1) * ring_count)
        att_t.append(product(w_value[:, part], att_keys[:, own], ((0,), (0,))))
        dq_t.append(product(w_key[:, part], d_query_keys[:, own], ((0,), (0,))) * scale)
        dq_ring_t.append(product(w_key[:, part], d_query_keys[:, far], ((0,), (0,))) * scale)
        g_key.append(product(d_query_keys[:, own], query_t[part, :count], both) * scale)
        g_value.append(product(att_keys[:, own], d_att_t[part, :count], both))
    att_t, dq_t, dq_ring_t = (jnp.concatenate(x) for x in (att_t, dq_t, dq_ring_t))
    att_out = product(att_t, w_out, ((0,), (0,)))
    d_normed = product(dq_t, w_query, ((0,), (1,)))
    d_normed_ring = product(dq_ring_t, w_query, ((0,), (1,)))
    g_query = product(tokens_t[:, :count], dq_t, both)
    g_out = product(att_t, grads_t[:, :count], both)
    weight_grads = jnp.concatenate(
        [g_query, jnp.concatenate(g_key, 1), jnp.concatenate(g_value, 1), g_out]
    )
    return att_out, d_pooled_sum, weight_grads, d_normed, d_normed_ring


def body(tokens, cotangent, conv_weight, w_query, w_key, w_value, w_out):
    tile_rows, tile_cols, channels = tokens.shape
    count = tile_rows * tile_cols
    row_count = lax.axis_size(ROW)
    col_count = lax.axis_size(COL)
    win_r = tile_rows * row_count // POOL
    win_c = tile_cols * col_count // POOL
    cells = tile_rows // win_r
    chips = lax.axis_size(CHIPS)
    far_count = lax.axis_size(FAR)

    padded_t, padded_g = halo(tokens, cotangent)
    ext_r, ext_c = tile_rows + 2, tile_cols + 2
    mixed = padded_t[1 : 1 + ext_r, 1 : 1 + ext_c]
    for i in range(3):
        for j in range(3):
            mixed = mixed + conv_weight[i, j] * padded_t[i : i + ext_r, j : j + ext_c]
    normed_ext, inv_ext = normalize(mixed)
    normed, inv_std = normed_ext[1:-1, 1:-1], inv_ext[1:-1, 1:-1]
    pooled = jnp.mean(normed.reshape(cells, win_r, win_c, channels), axis=(1, 2))
    pooled_n, pooled_inv = normalize(pooled)

    spread = jnp.broadcast_to(pooled_n[None], (chips, cells, channels))
    spread = lax.all_to_all(spread, CHIPS, 0, 0, tiled=True)
    keys = lax.all_gather(spread, "c", axis=0, tiled=True).reshape(-1, channels)

    normed_ring, inv_ring, grad_ring = ring(normed_ext), ring(inv_ext), ring(padded_g)
    flat_n = normed.reshape(count, channels)
    att_out, d_sum, weight_grads, d_normed, d_normed_ring = attention(
        keys,
        flat_n,
        normed_ring,
        cotangent.reshape(count, channels),
        grad_ring,
        w_query,
        w_key,
        w_value,
        w_out,
    )
    output = mixed[1:-1, 1:-1] + att_out.reshape(tokens.shape)

    sums = jnp.concatenate(
        [
            d_sum.reshape(2 * chips, cells, channels),
            weight_grads.reshape(2 * chips, 1, channels),
        ],
        1,
    )
    sums = lax.all_to_all(sums, "c", 0, 0, tiled=True)
    sums = sums[:chips] + sums[chips:]
    sums = jnp.sum(lax.all_to_all(sums, CHIPS, 0, 0, tiled=True), 0)
    d_pooled = norm_back(sums[:cells], pooled_n, pooled_inv) / float(win_r * win_c)

    d_tile = d_normed.reshape(cells, win_r, tile_cols, channels) + d_pooled[:, None, None]
    d_mixed = cotangent + norm_back(d_tile.reshape(tokens.shape), normed, inv_std)
    g_conv = [
        jnp.sum(padded_t[1 + i : 1 + i + tile_rows, 1 + j : 1 + j + tile_cols] * d_mixed, (0, 1))
        for i in range(3)
        for j in range(3)
    ]

    share = jnp.concatenate([d_pooled, sums[cells:], jnp.stack(g_conv)])
    share = jnp.broadcast_to(share[None], (far_count,) + share.shape)
    share = lax.all_to_all(share, FAR, 0, 0, tiled=True)
    kept = cells + 1
    conv_part = jnp.sum(share[:, kept:], 0)
    conv_part = jnp.concatenate([conv_part, jnp.zeros((7, channels), jnp.float32)])
    share = jnp.concatenate(
        [
            share[:, :cells].reshape(far_count * cells, channels),
            share[:, cells],
            conv_part,
        ]
    )
    near = lax.all_gather(share, NEAR, axis=0)
    pools = near[:, : far_count * cells].reshape(2, 2, 8, 2, 8, cells, channels)
    weights = near[:, far_count * cells : far_count * kept]
    g_conv = jnp.sum(near[:, far_count * kept :], 0)[:9].reshape(3, 3, channels)

    row, col = lax.axis_index(ROW), lax.axis_index(COL)

    def owner(d_row, d_col):
        r = jnp.clip(row + d_row, 0, row_count - 1)
        k = jnp.clip(col + d_col, 0, col_count - 1)
        start = (r % 2, k % 2, r // 2, k // 16, (k // 2) % 8, 0, 0)
        return lax.dynamic_slice(pools, start, (1,) * 5 + (cells, channels)).reshape(
            cells, channels
        )

    def line(d_row, cell):
        return jnp.concatenate(
            [
                owner(d_row, -1)[cell][None],
                jnp.broadcast_to(owner(d_row, 0)[cell][None], (tile_cols, channels)),
                owner(d_row, 1)[cell][None],
            ]
        )

    def column(d_col):
        return jnp.repeat(owner(0, d_col), win_r, axis=0)

    top, bottom = line(-1, cells - 1), line(1, 0)
    left, right = column(-1), column(1)
    used = 2 * ext_c + 2 * tile_rows
    d_ring = d_normed_ring[:used] + jnp.concatenate([top, bottom, left, right])
    d_ring = grad_ring[:used] + norm_back(d_ring, normed_ring[:used], inv_ring[:used])
    top, bottom = d_ring[:ext_c], d_ring[ext_c : 2 * ext_c]
    left = d_ring[2 * ext_c : 2 * ext_c + tile_rows]
    right = d_ring[2 * ext_c + tile_rows :]
    left, right = jnp.where(col > 0, left, 0.0), jnp.where(col < col_count - 1, right, 0.0)
    at = lax.broadcasted_iota(jnp.int32, (ext_c, 1), 0)
    inside = ((at > 0) | (col > 0)) & ((at < ext_c - 1) | (col < col_count - 1))
    top = jnp.where(inside & (row > 0), top, 0.0)
    bottom = jnp.where(inside & (row < row_count - 1), bottom, 0.0)
    padded_d = jnp.concatenate([left[:, None], d_mixed, right[:, None]], 1)
    padded_d = jnp.concatenate([top[None], padded_d, bottom[None]])
    d_tokens = d_mixed
    for i in range(3):
        for j in range(3):
            d_tokens = (
                d_tokens
                + conv_weight[i, j] * padded_d[2 - i : 2 - i + tile_rows, 2 - j : 2 - j + tile_cols]
            )
    root = float(count * row_count * col_count) ** (-0.5)
    g_query, g_value, g_key, g_out = (weights[k] for k in range(4))
    return (
        output,
        d_tokens,
        g_conv * root,
        g_query * root,
        g_key / float(POOL),
        g_value / float(POOL),
        g_out * root,
    )


def solution(mesh):
    fine = Mesh(mesh.devices.reshape(8, 2, 2, 8, 2), ("y", "xl", "xh", "z", "c"))
    tile = P(ROW, COL, None)
    return jax.shard_map(
        body,
        mesh=fine,
        in_specs=(tile, tile, P(), P(), P(), P(), P()),
        out_specs=(tile, tile, P(), P(), P(), P(), P()),
        check_vma=False,
    )
```

```python
import jax
import jax.numpy as jnp
from jax import lax
from jax.experimental import pallas as pl
from jax.experimental.pallas import tpu as pltpu
from jax.sharding import Mesh, PartitionSpec as P

HEADS = 2
POOL = 32
ROW = ("y", "xl")
COL = ("xh", "z", "c")
CHIP_COL = ("xh", "z")
CHIPS = CHIP_COL + ROW
HALO = 64


def product(left, right, dims=((1,), (0,)), precision=lax.Precision.HIGH):
    return lax.dot_general(
        left, right, (dims, ((), ())), precision=precision, preferred_element_type=jnp.float32
    )


def exact(left, right, dims=((1,), (0,))):
    return product(left, right, dims, lax.Precision.HIGHEST)


def normalize(values_in):
    average = jnp.mean(values_in, -1, keepdims=True)
    centered = values_in - average
    inv_std = lax.rsqrt(jnp.mean(centered * centered, -1, keepdims=True) + 1e-06)
    return (centered * inv_std, inv_std)


def norm_back(gradient, normed, inv_std):
    return inv_std * (
        gradient
        - jnp.mean(gradient, -1, keepdims=True)
        - normed * jnp.mean(gradient * normed, -1, keepdims=True)
    )


def neighbours(low_side, high_side, axis):
    peers = lax.axis_size(axis)
    up = [(i, i + 1) for i in range(peers - 1)]
    down = [(i + 1, i) for i in range(peers - 1)]
    return lax.ppermute(high_side, axis, up), lax.ppermute(low_side, axis, down)


def halo(tokens, cotangent):
    cols = tokens.shape[1]
    low = jnp.concatenate([tokens[:2], cotangent[:1]])
    high = jnp.concatenate([tokens[-2:], cotangent[-1:]])
    before, after = neighbours(low, high, ROW)
    tall_t = jnp.concatenate([before[:2], tokens, after[:2]])
    tall_g = jnp.concatenate([before[2:], cotangent, after[2:]])
    rows_t, rows_g = tall_t.shape[0], tall_g.shape[0]

    def side(first_t, first_g):
        part_t = tall_t[:, first_t : first_t + 2].reshape(2 * rows_t, -1)
        return jnp.concatenate([part_t, tall_g[:, first_g]])

    before, after = neighbours(side(0, 0), side(cols - 2, cols - 1), COL)

    def parts(received):
        return (
            received[: 2 * rows_t].reshape(rows_t, 2, -1),
            received[2 * rows_t :].reshape(rows_g, 1, -1),
        )

    (before_t, before_g), (after_t, after_g) = parts(before), parts(after)
    return (
        jnp.concatenate([before_t, tall_t, after_t], 1),
        jnp.concatenate([before_g, tall_g, after_g], 1),
    )


def ring(extended):
    rows, cols, channels = extended.shape
    used = 2 * cols + 2 * (rows - 2)
    return jnp.concatenate(
        [
            extended[0],
            extended[-1],
            extended[1:-1, 0],
            extended[1:-1, -1],
            jnp.zeros((HALO - used, channels), extended.dtype),
        ]
    )


def attention(keys, normed, normed_ring, grad, grad_ring, w_query, w_key, w_value, w_out):
    channels = keys.shape[1]
    count = normed.shape[0]
    width = channels // HEADS
    scale = width ** (-0.5)
    tokens_t = jnp.concatenate([normed, normed_ring]).T
    grads_t = jnp.concatenate([grad, grad_ring]).T
    query_t = exact(w_query, tokens_t, ((0,), (0,)))
    d_att_t = product(w_out, grads_t)
    to_keys, to_values = [], []
    for head in range(HEADS):
        part = slice(head * width, (head + 1) * width)
        to_keys.append(exact(w_key[:, part], query_t[part]) * scale)
        to_values.append(product(w_value[:, part], d_att_t[part]))
    inner = [x[:, :count] for x in to_keys], [x[:, :count] for x in to_values]
    outer = [x[:, count:] for x in to_keys], [x[:, count:] for x in to_values]
    query_keys = jnp.concatenate(inner[0] + outer[0], 1)
    d_att_values = jnp.concatenate(inner[1] + outer[1], 1)
    scores = exact(keys, query_keys)
    weights = jnp.exp(scores - jnp.max(scores, 0, keepdims=True))
    probs = weights * (1.0 / jnp.sum(weights, 0, keepdims=True))
    d_probs = product(keys, d_att_values)
    att_keys = product(keys, probs, ((0,), (0,)))
    d_scores = probs * (d_probs - jnp.sum(d_probs * probs, 0, keepdims=True))
    d_query_keys = product(keys, d_scores, ((0,), (0,)))
    wide = HEADS * count
    both = ((1,), (1,))
    d_pooled_sum = product(d_scores[:, :wide], query_keys[:, :wide], both) + product(
        probs[:, :wide], d_att_values[:, :wide], both
    )
    att_t, dq_t, dq_ring_t, g_key, g_value = [], [], [], [], []
    ring_count = normed_ring.shape[0]
    for head in range(HEADS):
        part = slice(head * width, (head + 1) * width)
        own = slice(head * count, (head + 1) * count)
        far = slice(wide + head * ring_count, wide + (head + 1) * ring_count)
        att_t.append(product(w_value[:, part], att_keys[:, own], ((0,), (0,))))
        dq_t.append(product(w_key[:, part], d_query_keys[:, own], ((0,), (0,))) * scale)
        dq_ring_t.append(product(w_key[:, part], d_query_keys[:, far], ((0,), (0,))) * scale)
        g_key.append(product(d_query_keys[:, own], query_t[part, :count], both) * scale)
        g_value.append(product(att_keys[:, own], d_att_t[part, :count], both))
    att_t, dq_t, dq_ring_t = (jnp.concatenate(x) for x in (att_t, dq_t, dq_ring_t))
    att_out = product(att_t, w_out, ((0,), (0,)))
    d_normed = product(dq_t, w_query, ((0,), (1,)))
    d_normed_ring = product(dq_ring_t, w_query, ((0,), (1,)))
    g_query = product(tokens_t[:, :count], dq_t, both)
    g_out = product(att_t, grads_t[:, :count], both)
    weight_grads = jnp.concatenate(
        [g_query, jnp.concatenate(g_key, 1), jnp.concatenate(g_value, 1), g_out]
    )
    return att_out, d_pooled_sum, weight_grads, d_normed, d_normed_ring


def body(tokens, cotangent, conv_weight, w_query, w_key, w_value, w_out):
    tile_rows, tile_cols, channels = tokens.shape
    count = tile_rows * tile_cols
    row_count = lax.axis_size(ROW)
    col_count = lax.axis_size(COL)
    win_r = tile_rows * row_count // POOL
    win_c = tile_cols * col_count // POOL
    cells = tile_rows // win_r
    chips = lax.axis_size(CHIPS)
    lines = lax.axis_size(CHIP_COL)

    padded_t, padded_g = halo(tokens, cotangent)
    ext_r, ext_c = tile_rows + 2, tile_cols + 2
    mixed = padded_t[1 : 1 + ext_r, 1 : 1 + ext_c]
    for i in range(3):
        for j in range(3):
            mixed = mixed + conv_weight[i, j] * padded_t[i : i + ext_r, j : j + ext_c]
    normed_ext, inv_ext = normalize(mixed)
    normed, inv_std = normed_ext[1:-1, 1:-1], inv_ext[1:-1, 1:-1]
    pooled = jnp.mean(normed.reshape(cells, win_r, win_c, channels), axis=(1, 2))
    pooled_n, pooled_inv = normalize(pooled)

    spread = jnp.broadcast_to(pooled_n[None], (chips, cells, channels))
    spread = lax.all_to_all(spread, CHIPS, 0, 0, tiled=True)
    keys = lax.all_gather(spread, "c", axis=0, tiled=True).reshape(-1, channels)

    normed_ring, inv_ring, grad_ring = ring(normed_ext), ring(inv_ext), ring(padded_g)
    flat_n = normed.reshape(count, channels)
    att_out, d_sum, weight_grads, d_normed, d_normed_ring = attention(
        keys,
        flat_n,
        normed_ring,
        cotangent.reshape(count, channels),
        grad_ring,
        w_query,
        w_key,
        w_value,
        w_out,
    )
    output = mixed[1:-1, 1:-1] + att_out.reshape(tokens.shape)

    sums = jnp.concatenate(
        [
            d_sum.reshape(2 * chips, 1, cells * channels),
            weight_grads.reshape(2 * chips, 1, channels),
        ],
        2,
    )
    sums = lax.all_to_all(sums, "c", 0, 0, tiled=True)
    sums = sums[:chips] + sums[chips:]
    sums = jnp.sum(lax.all_to_all(sums, CHIPS, 0, 0, tiled=True), 0)
    sums = sums.reshape(cells + 1, channels)
    d_pooled = norm_back(sums[:cells], pooled_n, pooled_inv) / float(win_r * win_c)

    d_tile = d_normed.reshape(cells, win_r, tile_cols, channels) + d_pooled[:, None, None]
    d_mixed = cotangent + norm_back(d_tile.reshape(tokens.shape), normed, inv_std)
    g_conv = [
        jnp.sum(padded_t[1 + i : 1 + i + tile_rows, 1 + j : 1 + j + tile_cols] * d_mixed, (0, 1))
        for i in range(3)
        for j in range(3)
    ]

    row, col = lax.axis_index(ROW), lax.axis_index(COL)
    share = jnp.concatenate(
        [d_pooled, sums[cells:], jnp.stack(g_conv), jnp.zeros((4, channels), jnp.float32)]
    )
    share = jnp.broadcast_to(share[None], (row_count,) + share.shape)
    share = lax.all_to_all(share, ROW, 0, 0, tiled=True)
    near_rows = jnp.pad(share[:, :cells], ((1, 1), (0, 0), (0, 0)))
    near_rows = lax.dynamic_slice_in_dim(near_rows, row, 3, 0).reshape(3 * cells, channels)
    g_conv = jnp.sum(share[:, cells + 1 : cells + 10], 0)
    share = jnp.concatenate(
        [share[:, cells], g_conv, near_rows, jnp.zeros((1, channels), jnp.float32)]
    )
    share = jnp.broadcast_to(share[None], (lines,) + share.shape)
    share = lax.all_to_all(share, CHIP_COL, 0, 0, tiled=True)
    near = lax.all_gather(share, "c", axis=0)
    weights = near[:, :, :row_count].reshape(4, channels, channels)
    g_conv = jnp.sum(near[:, :, row_count : row_count + 9], (0, 1)).reshape(3, 3, channels)

    def owner(d_row, d_col):
        k = jnp.clip(col + d_col, 0, col_count - 1)
        start = (k % 2, k // 2, row_count + 9 + (d_row + 1) * cells, 0)
        return lax.dynamic_slice(near, start, (1, 1, cells, channels)).reshape(cells, channels)

    def line(d_row, cell):
        return jnp.concatenate(
            [
                owner(d_row, -1)[cell][None],
                jnp.broadcast_to(owner(d_row, 0)[cell][None], (tile_cols, channels)),
                owner(d_row, 1)[cell][None],
            ]
        )

    def column(d_col):
        return jnp.repeat(owner(0, d_col), win_r, axis=0)

    top, bottom = line(-1, cells - 1), line(1, 0)
    left, right = column(-1), column(1)
    used = 2 * ext_c + 2 * tile_rows
    d_ring = d_normed_ring[:used] + jnp.concatenate([top, bottom, left, right])
    d_ring = grad_ring[:used] + norm_back(d_ring, normed_ring[:used], inv_ring[:used])
    top, bottom = d_ring[:ext_c], d_ring[ext_c : 2 * ext_c]
    left = d_ring[2 * ext_c : 2 * ext_c + tile_rows]
    right = d_ring[2 * ext_c + tile_rows :]
    left, right = jnp.where(col > 0, left, 0.0), jnp.where(col < col_count - 1, right, 0.0)
    at = lax.broadcasted_iota(jnp.int32, (ext_c, 1), 0)
    inside = ((at > 0) | (col > 0)) & ((at < ext_c - 1) | (col < col_count - 1))
    top = jnp.where(inside & (row > 0), top, 0.0)
    bottom = jnp.where(inside & (row < row_count - 1), bottom, 0.0)
    padded_d = jnp.concatenate([left[:, None], d_mixed, right[:, None]], 1)
    padded_d = jnp.concatenate([top[None], padded_d, bottom[None]])
    d_tokens = d_mixed
    for i in range(3):
        for j in range(3):
            d_tokens = (
                d_tokens
                + conv_weight[i, j] * padded_d[2 - i : 2 - i + tile_rows, 2 - j : 2 - j + tile_cols]
            )
    root = float(count * row_count * col_count) ** (-0.5)
    g_query, g_key, g_value, g_out = (weights[k] for k in range(4))
    return (
        output,
        d_tokens,
        g_conv * root,
        g_query * root,
        g_key / float(POOL),
        g_value / float(POOL),
        g_out * root,
    )


def solution(mesh):
    fine = Mesh(mesh.devices.reshape(8, 2, 2, 8, 2), ("y", "xl", "xh", "z", "c"))
    tile = P(ROW, COL, None)
    return jax.shard_map(
        body,
        mesh=fine,
        in_specs=(tile, tile, P(), P(), P(), P(), P()),
        out_specs=(tile, tile, P(), P(), P(), P(), P()),
        check_vma=False,
    )
```

```python
import functools

import jax
import jax.numpy as jnp
from jax import lax
from jax.experimental import pallas as pl
from jax.experimental.pallas import tpu as pltpu
from jax.sharding import Mesh, PartitionSpec as P

HEADS = 2
POOL = 32
ROW = ("y", "xl")
COL = ("xh", "z", "c")
CHIP_COL = ("xh", "z")
CHIPS = CHIP_COL + ROW
ROWS, COLS, CHANNELS = 8, 16, 128
CELLS, WIN_ROWS = 2, 4
COUNT = ROWS * COLS
WIDE = COLS + 2
USED = 2 * WIDE + 2 * ROWS
RING = 64
WIDTH = CHANNELS // HEADS
SCALE = WIDTH ** (-0.5)
BOTH = ((1,), (1,))
FIRST = ((0,), (0,))


def product(left, right, dims=((1,), (0,)), precision=lax.Precision.HIGHEST):
    return lax.dot_general(
        left, right, (dims, ((), ())), precision=precision, preferred_element_type=jnp.float32
    )


def normalize(values_in):
    average = jnp.mean(values_in, -1, keepdims=True)
    centered = values_in - average
    inv_std = lax.rsqrt(jnp.mean(centered * centered, -1, keepdims=True) + 1e-06)
    return (centered * inv_std, inv_std)


def norm_back(gradient, normed, inv_std):
    return inv_std * (
        gradient
        - jnp.mean(gradient, -1, keepdims=True)
        - normed * jnp.mean(gradient * normed, -1, keepdims=True)
    )


def f32(*shape):
    return jax.ShapeDtypeStruct(shape, jnp.float32)


def call(kernel, outs, *args, scratch=(), scalars=0, flops=1 << 20):
    in_vmem = pl.BlockSpec(memory_space=pltpu.VMEM)
    specs = [pl.BlockSpec(memory_space=pltpu.SMEM)] * scalars + [in_vmem] * (len(args) - scalars)
    return pl.pallas_call(
        kernel,
        out_shape=outs,
        in_specs=specs,
        out_specs=[in_vmem] * len(outs),
        scratch_shapes=[pltpu.VMEM(shape, jnp.float32) for shape in scratch],
        compiler_params=pltpu.CompilerParams(vmem_limit_bytes=48 << 20),
        cost_estimate=pl.CostEstimate(flops=flops, bytes_accessed=1 << 20, transcendentals=0),
    )(*args)


def neighbours(low_side, high_side, axis):
    peers = lax.axis_size(axis)
    up = [(i, i + 1) for i in range(peers - 1)]
    down = [(i + 1, i) for i in range(peers - 1)]
    return lax.ppermute(high_side, axis, up), lax.ppermute(low_side, axis, down)


def mix_kernel(
    tokens, grad, above, below, before, after, weight,
    message, pooled_out, padded, mixed_out, normed_out, inv_out, grad_out,
    normed_ext, inv_ext, mixed_ext,
):
    padded[2 : 2 + ROWS, 2 : 2 + COLS] = tokens[...]
    padded[0:2, 2 : 2 + COLS] = above[0:2]
    padded[2 + ROWS : 4 + ROWS, 2 : 2 + COLS] = below[0:2]
    tall = ROWS + 4
    for r in range(tall):
        for k in range(2):
            at = k * tall + r
            padded[r, k : k + 1] = before[at : at + 1]
            padded[r, 2 + COLS + k : 3 + COLS + k] = after[at : at + 1]
    mixed = padded[1 : ROWS + 3, 1 : 1 + WIDE]
    for i in range(3):
        for j in range(3):
            mixed = mixed + weight[i, j : j + 1][None] * padded[i : i + ROWS + 2, j : j + WIDE]
    normed, inv_std = normalize(mixed)
    mixed_ext[:, 0:WIDE] = mixed
    normed_ext[:, 0:WIDE] = normed
    inv_ext[:, 0:WIDE] = jnp.broadcast_to(inv_std, normed.shape)
    inner = normed_ext[1 : 1 + ROWS, 1 : 1 + COLS]
    for cell in range(CELLS):
        window = jnp.sum(inner[cell * WIN_ROWS : (cell + 1) * WIN_ROWS], 0)
        pooled = jnp.sum(window, 0, keepdims=True) * (1.0 / (WIN_ROWS * COLS))
        pooled_n, pooled_inv = normalize(pooled)
        pooled_out[cell : cell + 1] = pooled_n
        pooled_out[CELLS + cell : CELLS + cell + 1] = jnp.broadcast_to(pooled_inv, pooled_n.shape)
    message[...] = jnp.broadcast_to(pooled_out[0:CELLS][None], message.shape)
    mixed_out[...] = mixed_ext[1 : 1 + ROWS, 1 : 1 + COLS]
    for ext, out in ((normed_ext, normed_out), (inv_ext, inv_out)):
        out[0:COUNT] = ext[1 : 1 + ROWS, 1 : 1 + COLS].reshape(COUNT, CHANNELS)
        out[COUNT : COUNT + WIDE] = ext[0, 0:WIDE]
        out[COUNT + WIDE : COUNT + 2 * WIDE] = ext[ROWS + 1, 0:WIDE]
        for r in range(ROWS):
            left = COUNT + 2 * WIDE + r
            out[left : left + 1] = ext[1 + r, 0:1]
            out[left + ROWS : left + ROWS + 1] = ext[1 + r, WIDE - 1 : WIDE]
        out[COUNT + USED :] = jnp.zeros((RING - USED, CHANNELS), jnp.float32)
    low = 2 * tall
    high = low + ROWS + 1
    grad_out[0:COUNT] = grad[...].reshape(COUNT, CHANNELS)
    for start, middle, at in ((COUNT, above, low), (COUNT + WIDE, below, high)):
        grad_out[start : start + 1] = before[at : at + 1]
        grad_out[start + 1 : start + 1 + COLS] = middle[2]
        grad_out[start + 1 + COLS : start + WIDE] = after[at : at + 1]
    left = COUNT + 2 * WIDE
    grad_out[left : left + ROWS] = before[low + 1 : high]
    grad_out[left + ROWS : left + 2 * ROWS] = after[low + 1 : high]
    grad_out[COUNT + USED :] = jnp.zeros((RING - USED, CHANNELS), jnp.float32)


def halves(value):
    high = value.astype(jnp.bfloat16)
    return high, (value - high.astype(jnp.float32)).astype(jnp.bfloat16)


def three_pass(left, right, dims=((1,), (0,))):
    (left_high, left_low), (right_high, right_low) = left, right
    part = functools.partial(product, dims=dims, precision=lax.Precision.DEFAULT)
    return part(left_high, right_high) + (part(left_high, right_low) + part(left_low, right_high))


def attend_kernel(
    core, keys_ref, to_keys, to_values, query_t, d_att_t, normed_t, grad_t, w_key, w_value,
    own_out, mate_out, att_out, dq_out, ring_out,
):
    own = core[0] * (keys_ref.shape[0] // 2)
    mate = keys_ref.shape[0] // 2 - own
    quarter = keys_ref.shape[0] // 4
    keys = jnp.concatenate(
        [
            keys_ref[pl.ds(start, quarter, stride=2)]
            for start in (own, own + 1, mate, mate + 1)
        ]
    )
    wide = HEADS * COUNT
    query_keys, d_att_values = to_keys[...], to_values[...]
    scores = product(keys, query_keys)
    weights = jnp.exp(scores - jnp.max(scores, 0, keepdims=True))
    probs = weights * (1.0 / jnp.sum(weights, 0, keepdims=True))
    keys_split = halves(keys)
    keys_t = halves(keys.T)
    values_split = halves(d_att_values)
    d_probs = three_pass(keys_split, values_split)
    d_scores = probs * (d_probs - jnp.sum(d_probs * probs, 0, keepdims=True))
    probs_split, d_split = halves(probs), halves(d_scores)
    att_keys = three_pass(keys_t, probs_split)
    d_query_keys = three_pass(keys_t, d_split)

    def inner(pair):
        return tuple(x[:, :wide] for x in pair)

    sums = three_pass(inner(d_split), inner(halves(query_keys)), BOTH) + three_pass(
        inner(probs_split), inner(values_split), BOTH
    )
    upper = lax.broadcasted_iota(jnp.int32, (CHANNELS, CHANNELS), 0) < WIDTH
    left = lax.broadcasted_iota(jnp.int32, (CHANNELS, CHANNELS), 1) < WIDTH

    def heads(first, second, mask=upper):
        return jnp.where(mask, first, second)

    z0, z1 = att_keys[:, :COUNT], att_keys[:, COUNT:wide]
    y0, y1 = d_query_keys[:, :COUNT], d_query_keys[:, COUNT:wide]
    att_t = heads(product(w_value[...], z0, FIRST), product(w_value[...], z1, FIRST))
    dq_t = heads(product(w_key[...], y0, FIRST), product(w_key[...], y1, FIRST)) * SCALE
    q, a = query_t[...], d_att_t[...]
    g_query = product(normed_t[...], dq_t, BOTH)
    g_key = heads(product(y0, q, BOTH), product(y1, q, BOTH), left) * SCALE
    g_value = heads(product(z0, a, BOTH), product(z1, a, BOTH), left)
    g_out = product(att_t, grad_t[...], BOTH)
    att_out[...] = att_t
    dq_out[...] = dq_t
    ring_out[...] = d_query_keys[:, wide:]
    first = core[0] == 0
    by_core = ((g_query, g_key), (g_value, g_out))
    for half in range(2):
        at = half * CHANNELS
        zero, one = by_core[0][half], by_core[1][half]
        own_out[at : at + CHANNELS, 2 * CHANNELS :] = jnp.where(first, zero, one)
        mate_out[at : at + CHANNELS, 2 * CHANNELS :] = jnp.where(first, one, zero)
    own_out[:, :CHANNELS] = sums[:quarter]
    own_out[:, CHANNELS : 2 * CHANNELS] = sums[quarter : 2 * quarter]
    mate_out[:, :CHANNELS] = sums[2 * quarter : 3 * quarter]
    mate_out[:, CHANNELS : 2 * CHANNELS] = sums[3 * quarter :]


def middle_kernel(sums, pooled, d_normed, normed, inv, grad, padded, d_mixed_out, message, share):
    window = float(WIN_ROWS * COLS)
    share[...] = jnp.zeros(share.shape, jnp.float32)
    half = WIN_ROWS * COLS
    for cell in range(CELLS):
        part = slice(cell * CHANNELS, (cell + 1) * CHANNELS)
        d_pooled = norm_back(
            sums[:, part], pooled[cell : cell + 1], pooled[CELLS + cell : CELLS + cell + 1]
        )
        d_pooled = d_pooled * (1.0 / window)
        share[cell : cell + 1] = d_pooled
        rows = slice(cell * half, (cell + 1) * half)
        back = norm_back(d_normed[rows] + d_pooled, normed[rows], inv[rows])
        back = grad[rows] + back
        d_mixed_out[cell * WIN_ROWS : (cell + 1) * WIN_ROWS] = back.reshape(
            WIN_ROWS, COLS, CHANNELS
        )
    share[CELLS : CELLS + 1] = sums[:, CELLS * CHANNELS :]
    d_mixed = d_mixed_out[...]
    for i in range(3):
        for j in range(3):
            products = padded[1 + i : 1 + i + ROWS, 1 + j : 1 + j + COLS] * d_mixed
            at = CELLS + 1 + 3 * i + j
            share[at : at + 1] = jnp.sum(jnp.sum(products, 0), 0, keepdims=True)
    message[...] = jnp.broadcast_to(share[...][None], message.shape)


def relay_kernel(place, received, message, share):
    peers = received.shape[0]
    row = place[0]
    for k in range(peers):
        share[k : k + 1] = received[k, CELLS : CELLS + 1]
    total = received[0]
    for k in range(1, peers):
        total = total + received[k]
    share[peers : peers + 9] = total[CELLS + 1 : CELLS + 10]
    for d in range(3):
        at = peers + 9 + d * CELLS
        share[at : at + CELLS] = received[jnp.clip(row + d - 1, 0, peers - 1), 0:CELLS]
    share[31:32] = jnp.zeros((1, CHANNELS), jnp.float32)
    message[...] = jnp.broadcast_to(share[...][None], message.shape)


def end_kernel(
    row_count, col_count, place, near, d_normed, normed, inv, grad, d_mixed, weight,
    d_tokens, g_conv, g_query, g_key, g_value, g_out,
    ring, padded,
):
    row, col = place[0], place[1]
    cores, lines = near.shape[0], near.shape[1]
    first = row_count + 9

    def owner(d_row, d_col, cell):
        k = jnp.clip(col + d_col, 0, col_count - 1)
        at = first + (d_row + 1) * CELLS + cell
        return near[k % 2, k // 2, at : at + 1]

    for start, d_row, cell in ((0, -1, CELLS - 1), (WIDE, 1, 0)):
        ring[start : start + 1] = owner(d_row, -1, cell)
        ring[start + 1 : start + 1 + COLS] = jnp.broadcast_to(
            owner(d_row, 0, cell), (COLS, CHANNELS)
        )
        ring[start + 1 + COLS : start + WIDE] = owner(d_row, 1, cell)
    for start, d_col in ((2 * WIDE, -1), (2 * WIDE + ROWS, 1)):
        for cell in range(CELLS):
            at = start + cell * WIN_ROWS
            ring[at : at + WIN_ROWS] = jnp.broadcast_to(
                owner(0, d_col, cell), (WIN_ROWS, CHANNELS)
            )
    ring[USED:] = jnp.zeros((RING - USED, CHANNELS), jnp.float32)
    back = norm_back(d_normed[...] + ring[...], normed[COUNT:], inv[COUNT:])
    back = grad[COUNT:] + back
    at = lax.broadcasted_iota(jnp.int32, (RING, CHANNELS), 0)
    top, bottom = at < WIDE, (at >= WIDE) & (at < 2 * WIDE)
    left = ((at >= 2 * WIDE) & (at < 2 * WIDE + ROWS)) | (at == 0) | (at == WIDE)
    right = (at >= 2 * WIDE + ROWS) | (at == WIDE - 1) | (at == 2 * WIDE - 1)
    outside = (
        (top & (row == 0))
        | (bottom & (row == row_count - 1))
        | (left & (col == 0))
        | (right & (col == col_count - 1))
    )
    ring[...] = jnp.where(outside, 0.0, back)
    padded[0, 0:WIDE] = ring[0:WIDE]
    padded[ROWS + 1, 0:WIDE] = ring[WIDE : 2 * WIDE]
    for r in range(ROWS):
        k = 2 * WIDE + r
        padded[1 + r, 0:1] = ring[k : k + 1]
        padded[1 + r, WIDE - 1 : WIDE] = ring[k + ROWS : k + ROWS + 1]
    padded[1 : 1 + ROWS, 1 : 1 + COLS] = d_mixed[...]
    total = d_mixed[...]
    for i in range(3):
        for j in range(3):
            total = (
                total
                + weight[i, j : j + 1][None]
                * padded[2 - i : 2 - i + ROWS, 2 - j : 2 - j + COLS]
            )
    d_tokens[...] = total
    root = float(COUNT * row_count * col_count) ** (-0.5)
    conv = near[0, 0, row_count:first]
    for k in range(1, cores * lines):
        conv = conv + near[k // lines, k % lines, row_count:first]
    conv = conv * root
    for k in range(9):
        g_conv[k // 3, k % 3 : k % 3 + 1] = conv[k : k + 1]
    blocks = ((g_query, root), (g_key, 1.0 / POOL), (g_value, 1.0 / POOL), (g_out, root))
    for k in range(cores * lines):
        out, factor = blocks[k * row_count // CHANNELS]
        at = k * row_count % CHANNELS
        out[at : at + row_count] = near[k // lines, k % lines, 0:row_count] * factor


def body(tokens, cotangent, conv_weight, w_query, w_key, w_value, w_out):
    row_count, col_count = lax.axis_size(ROW), lax.axis_size(COL)
    chips, lines = lax.axis_size(CHIPS), lax.axis_size(CHIP_COL)
    place = jnp.stack([lax.axis_index(ROW), lax.axis_index(COL), lax.axis_index("c")])
    tile = (ROWS, COLS, CHANNELS)
    square = (CHANNELS, CHANNELS)
    all_tokens = (COUNT + RING, CHANNELS)

    low = jnp.concatenate([tokens[:2], cotangent[:1]])
    high = jnp.concatenate([tokens[-2:], cotangent[-1:]])
    above, below = neighbours(low, high, ROW)

    def side(first_t, first_g):
        parts = []
        for k in (first_t, first_t + 1):
            parts += [above[:2, k], tokens[:, k], below[:2, k]]
        return jnp.concatenate(
            parts + [above[2:, first_g], cotangent[:, first_g], below[2:, first_g]]
        )

    before, after = neighbours(side(0, 0), side(COLS - 2, COLS - 1), COL)
    message, pooled, padded, mixed, normed, inv_std, grad = call(
        mix_kernel,
        [
            f32(chips, CELLS, CHANNELS),
            f32(2 * CELLS, CHANNELS),
            f32(ROWS + 4, 24, CHANNELS),
            f32(*tile),
            f32(*all_tokens),
            f32(*all_tokens),
            f32(*all_tokens),
        ],
        tokens, cotangent, above, below, before, after, conv_weight,
        scratch=[(ROWS + 2, 24, CHANNELS)] * 3,
    )

    message = lax.all_to_all(message, CHIPS, 0, 0, tiled=True)
    keys = lax.all_gather(message, "c", axis=0, tiled=True).reshape(-1, CHANNELS)

    normed_t, grad_t = normed.T, grad.T
    query_t = product(w_query, normed_t, FIRST)
    d_att_t = product(w_out, grad_t)
    to_keys, to_values = [], []
    for head in range(HEADS):
        part = slice(head * WIDTH, (head + 1) * WIDTH)
        to_keys.append(product(w_key[:, part], query_t[part]) * SCALE)
        to_values.append(product(w_value[:, part], d_att_t[part]))

    def columns(by_head):
        return jnp.concatenate([x[:, :COUNT] for x in by_head] + [x[:, COUNT:] for x in by_head], 1)

    own, mate, att_t, dq_t, ring_keys = call(
        attend_kernel,
        [
            f32(chips, 3 * CHANNELS),
            f32(chips, 3 * CHANNELS),
            f32(*square),
            f32(*square),
            f32(CHANNELS, HEADS * RING),
        ],
        place[2:], keys, columns(to_keys), columns(to_values), query_t[:, :COUNT],
        d_att_t[:, :COUNT], normed_t[:, :COUNT], grad_t[:, :COUNT], w_key, w_value,
        scalars=1, flops=1 << 31,
    )

    received = lax.ppermute(mate, "c", [(0, 1), (1, 0)])
    sums = (own + received).reshape(chips, 1, 3 * CHANNELS)
    sums = jnp.sum(lax.all_to_all(sums, CHIPS, 0, 0, tiled=True), 0)

    output = mixed + product(att_t, w_out, FIRST).reshape(tile)
    d_normed = product(dq_t, w_query, ((0,), (1,)))
    dq_ring = [
        product(
            w_key[:, head * WIDTH : (head + 1) * WIDTH],
            ring_keys[:, head * RING : (head + 1) * RING],
            FIRST,
        )
        for head in range(HEADS)
    ]
    d_ring = product(jnp.concatenate(dq_ring) * SCALE, w_query, ((0,), (1,)))

    d_mixed, message = call(
        middle_kernel,
        [f32(*tile), f32(row_count, 16, CHANNELS)],
        sums, pooled, d_normed, normed, inv_std, grad, padded,
        scratch=[(16, CHANNELS)],
    )
    message = lax.all_to_all(message, ROW, 0, 0, tiled=True)
    (message,) = call(
        relay_kernel,
        [f32(lines, 32, CHANNELS)],
        place, message,
        scratch=[(32, CHANNELS)], scalars=1,
    )
    message = lax.all_to_all(message, CHIP_COL, 0, 0, tiled=True)
    near = lax.all_gather(message, "c", axis=0)
    results = call(
        functools.partial(end_kernel, row_count, col_count),
        [f32(*tile), f32(3, 3, CHANNELS)] + [f32(*square)] * 4,
        place, near, d_ring, normed, inv_std, grad, d_mixed, conv_weight,
        scratch=[(RING, CHANNELS), (ROWS + 2, 24, CHANNELS)], scalars=1,
    )
    return (output, *results)


def solution(mesh):
    fine = Mesh(mesh.devices.reshape(8, 2, 2, 8, 2), ("y", "xl", "xh", "z", "c"))
    tile = P(ROW, COL, None)
    return jax.shard_map(
        body,
        mesh=fine,
        in_specs=(tile, tile, P(), P(), P(), P(), P()),
        out_specs=(tile, tile, P(), P(), P(), P(), P()),
        check_vma=False,
    )
```

```python
import functools

import jax
import jax.numpy as jnp
from jax import lax
from jax.experimental import pallas as pl
from jax.experimental.pallas import tpu as pltpu
from jax.sharding import Mesh, PartitionSpec as P

HEADS = 2
POOL = 32
ROW = ("y", "xl")
COL = ("xh", "z", "c")
CHIP_COL = ("xh", "z")
CHIPS = CHIP_COL + ROW
ROWS, COLS, CHANNELS = 8, 16, 128
CELLS, WIN_ROWS = 2, 4
COUNT = ROWS * COLS
WIDE = COLS + 2
USED = 2 * WIDE + 2 * ROWS
RING = 64
WIDTH = CHANNELS // HEADS
SCALE = WIDTH ** (-0.5)
BOTH = ((1,), (1,))
FIRST = ((0,), (0,))


def product(left, right, dims=((1,), (0,)), precision=lax.Precision.HIGHEST):
    return lax.dot_general(
        left, right, (dims, ((), ())), precision=precision, preferred_element_type=jnp.float32
    )


def normalize(values_in):
    average = jnp.mean(values_in, -1, keepdims=True)
    centered = values_in - average
    inv_std = lax.rsqrt(jnp.mean(centered * centered, -1, keepdims=True) + 1e-06)
    return (centered * inv_std, inv_std)


def norm_back(gradient, normed, inv_std):
    return inv_std * (
        gradient
        - jnp.mean(gradient, -1, keepdims=True)
        - normed * jnp.mean(gradient * normed, -1, keepdims=True)
    )


def f32(*shape):
    return jax.ShapeDtypeStruct(shape, jnp.float32)


def call(kernel, outs, *args, scratch=(), scalars=0, flops=1 << 20):
    in_vmem = pl.BlockSpec(memory_space=pltpu.VMEM)
    specs = [pl.BlockSpec(memory_space=pltpu.SMEM)] * scalars + [in_vmem] * (len(args) - scalars)
    return pl.pallas_call(
        kernel,
        out_shape=outs,
        in_specs=specs,
        out_specs=[in_vmem] * len(outs),
        scratch_shapes=[pltpu.VMEM(shape, jnp.float32) for shape in scratch],
        compiler_params=pltpu.CompilerParams(vmem_limit_bytes=48 << 20),
        cost_estimate=pl.CostEstimate(flops=flops, bytes_accessed=flops, transcendentals=0),
    )(*args)


def neighbours(low_side, high_side, axis):
    peers = lax.axis_size(axis)
    up = [(i, i + 1) for i in range(peers - 1)]
    down = [(i + 1, i) for i in range(peers - 1)]
    return lax.ppermute(high_side, axis, up), lax.ppermute(low_side, axis, down)


def mix_kernel(
    tokens, grad, above, below, before, after, weight,
    message, pooled_out, padded, mixed_out, normed_out, inv_out, grad_out,
    normed_ext, inv_ext, mixed_ext,
):
    padded[2 : 2 + ROWS, 2 : 2 + COLS] = tokens[...]
    padded[0:2, 2 : 2 + COLS] = above[0:2]
    padded[2 + ROWS : 4 + ROWS, 2 : 2 + COLS] = below[0:2]
    tall = ROWS + 4
    for r in range(tall):
        for k in range(2):
            at = k * tall + r
            padded[r, k : k + 1] = before[at : at + 1]
            padded[r, 2 + COLS + k : 3 + COLS + k] = after[at : at + 1]
    mixed = padded[1 : ROWS + 3, 1 : 1 + WIDE]
    for i in range(3):
        for j in range(3):
            mixed = mixed + weight[i, j : j + 1][None] * padded[i : i + ROWS + 2, j : j + WIDE]
    normed, inv_std = normalize(mixed)
    mixed_ext[:, 0:WIDE] = mixed
    normed_ext[:, 0:WIDE] = normed
    inv_ext[:, 0:WIDE] = jnp.broadcast_to(inv_std, normed.shape)
    inner = normed_ext[1 : 1 + ROWS, 1 : 1 + COLS]
    for cell in range(CELLS):
        window = jnp.sum(inner[cell * WIN_ROWS : (cell + 1) * WIN_ROWS], 0)
        pooled = jnp.sum(window, 0, keepdims=True) * (1.0 / (WIN_ROWS * COLS))
        pooled_n, pooled_inv = normalize(pooled)
        pooled_out[cell : cell + 1] = pooled_n
        pooled_out[CELLS + cell : CELLS + cell + 1] = jnp.broadcast_to(pooled_inv, pooled_n.shape)
    message[...] = jnp.broadcast_to(pooled_out[0:CELLS][None], message.shape)
    mixed_out[...] = mixed_ext[1 : 1 + ROWS, 1 : 1 + COLS]
    for ext, out in ((normed_ext, normed_out), (inv_ext, inv_out)):
        out[0:COUNT] = ext[1 : 1 + ROWS, 1 : 1 + COLS].reshape(COUNT, CHANNELS)
        out[COUNT : COUNT + WIDE] = ext[0, 0:WIDE]
        out[COUNT + WIDE : COUNT + 2 * WIDE] = ext[ROWS + 1, 0:WIDE]
        for r in range(ROWS):
            left = COUNT + 2 * WIDE + r
            out[left : left + 1] = ext[1 + r, 0:1]
            out[left + ROWS : left + ROWS + 1] = ext[1 + r, WIDE - 1 : WIDE]
        out[COUNT + USED :] = jnp.zeros((RING - USED, CHANNELS), jnp.float32)
    low = 2 * tall
    high = low + ROWS + 1
    grad_out[0:COUNT] = grad[...].reshape(COUNT, CHANNELS)
    for start, middle, at in ((COUNT, above, low), (COUNT + WIDE, below, high)):
        grad_out[start : start + 1] = before[at : at + 1]
        grad_out[start + 1 : start + 1 + COLS] = middle[2]
        grad_out[start + 1 + COLS : start + WIDE] = after[at : at + 1]
    left = COUNT + 2 * WIDE
    grad_out[left : left + ROWS] = before[low + 1 : high]
    grad_out[left + ROWS : left + 2 * ROWS] = after[low + 1 : high]
    grad_out[COUNT + USED :] = jnp.zeros((RING - USED, CHANNELS), jnp.float32)


def edge_kernel(tokens, grad, low, high):
    low[0:2], low[2] = tokens[0:2], grad[0]
    high[0:2], high[2] = tokens[ROWS - 2 : ROWS], grad[ROWS - 1]


def top_half():
    return lax.broadcasted_iota(jnp.int32, (CHANNELS, CHANNELS), 0) < WIDTH


def before_kernel(
    normed, grad, w_query, w_key, w_value, w_out,
    to_keys, to_values, query_t, d_att_t, normed_t, grad_t,
):
    upper = top_half()

    def by_head(weight, value, ring, out):
        for head, mask in enumerate((upper, ~upper)):
            at = head * COUNT
            out[:, at : at + COUNT] = product(weight, jnp.where(mask, value, 0.0))
        parts = [
            product(weight, jnp.where(mask[:, :RING], ring, 0.0)) for mask in (upper, ~upper)
        ]
        out[:, HEADS * COUNT :] = jnp.concatenate(parts, 1)

    inner, ring = normed[0:COUNT].T, normed[COUNT:].T
    normed_t[...] = inner
    query = product(w_query[...], inner, FIRST)
    query_t[...] = query
    by_head(w_key[...] * SCALE, query, product(w_query[...], ring, FIRST), to_keys)
    inner, ring = grad[0:COUNT].T, grad[COUNT:].T
    grad_t[...] = inner
    d_att = product(w_out[...], inner)
    d_att_t[...] = d_att
    by_head(w_value[...], d_att, product(w_out[...], ring), to_values)


def after_kernel(att_t, dq_t, ring_keys, mixed, w_query, w_key, w_out, output, d_normed, d_ring):
    att_out = product(att_t[...], w_out[...], FIRST)
    output[...] = mixed[...] + att_out.reshape(ROWS, COLS, CHANNELS)
    back = w_query[...].T
    d_normed[...] = product(dq_t[...], back, FIRST)
    ring = product(w_key[...], ring_keys[...], FIRST)
    ring = jnp.where(top_half()[:, :RING], ring[:, :RING], ring[:, RING:]) * SCALE
    d_ring[...] = product(ring, back, FIRST)


def pieces(value, count):
    parts = []
    for _ in range(count - 1):
        parts.append(value.astype(jnp.bfloat16))
        value = value - parts[-1].astype(jnp.float32)
    return parts + [value.astype(jnp.bfloat16)]


def single(left, right, dims=((1,), (0,))):
    return product(left, right, dims, lax.Precision.DEFAULT)


def attend_kernel(
    core, keys_ref, to_keys, to_values, query_t, d_att_t, normed_t, grad_t, w_key, w_value,
    own_out, mate_out, att_out, dq_out, ring_out,
):
    own = core[0] * (keys_ref.shape[0] // 2)
    mate = keys_ref.shape[0] // 2 - own
    quarter = keys_ref.shape[0] // 4
    keys = jnp.concatenate(
        [
            keys_ref[pl.ds(start, quarter, stride=2)]
            for start in (own, own + 1, mate, mate + 1)
        ]
    )
    wide = HEADS * COUNT
    k0, k1, k2 = pieces(keys, 3)
    q0, q1, q2 = pieces(to_keys[...], 3)
    v0, v1 = pieces(to_values[...], 2)
    scores = single(
        jnp.concatenate([k0, k0, k1, k0, k2, k1], 1), jnp.concatenate([q0, q1, q0, q2, q0, q1])
    )
    d_probs = single(jnp.concatenate([k0, k0, k1], 1), jnp.concatenate([v0, v1, v0]))
    weights = jnp.exp(scores - jnp.max(scores, 0, keepdims=True))
    probs = weights * (1.0 / jnp.sum(weights, 0, keepdims=True))
    t0, t1 = pieces(keys.T, 2)
    both_t = jnp.concatenate([t0, t1])

    def by_keys(high, low):
        twice = single(both_t, high)
        return twice[:CHANNELS] + (twice[CHANNELS:] + single(t0, low))

    d_scores = probs * (d_probs - jnp.sum(d_probs * probs, 0, keepdims=True))
    d0, d1 = pieces(d_scores, 2)
    d_query_keys = by_keys(d0, d1)
    p0, p1 = pieces(probs[:, :wide], 2)
    att_keys = by_keys(p0, p1)
    d0, d1 = d0[:, :wide], d1[:, :wide]
    large = jnp.concatenate([q0[:, :wide], v0[:, :wide]], 1)
    small = jnp.concatenate([q1[:, :wide], v1[:, :wide]], 1)
    twice = single(
        jnp.concatenate([d0, p0], 1), jnp.concatenate([large, small]), BOTH
    )
    sums = twice[:, :CHANNELS] + (
        twice[:, CHANNELS:] + single(jnp.concatenate([d1, p1], 1), large, BOTH)
    )
    upper = top_half()
    left = lax.broadcasted_iota(jnp.int32, (CHANNELS, CHANNELS), 1) < WIDTH

    def heads(first, second, mask=upper):
        return jnp.where(mask, first, second)

    z0, z1 = att_keys[:, :COUNT], att_keys[:, COUNT:wide]
    y0, y1 = d_query_keys[:, :COUNT], d_query_keys[:, COUNT:wide]
    att_t = heads(product(w_value[...], z0, FIRST), product(w_value[...], z1, FIRST))
    dq_t = heads(product(w_key[...], y0, FIRST), product(w_key[...], y1, FIRST)) * SCALE
    q, a = query_t[...], d_att_t[...]
    g_query = product(normed_t[...], dq_t, BOTH)
    g_key = heads(product(y0, q, BOTH), product(y1, q, BOTH), left) * SCALE
    g_value = heads(product(z0, a, BOTH), product(z1, a, BOTH), left)
    g_out = product(att_t, grad_t[...], BOTH)
    att_out[...] = att_t
    dq_out[...] = dq_t
    ring_out[...] = d_query_keys[:, wide:]
    first = core[0] == 0
    by_core = ((g_query, g_key), (g_value, g_out))
    for half in range(2):
        at = half * CHANNELS
        zero, one = by_core[0][half], by_core[1][half]
        own_out[at : at + CHANNELS, 2 * CHANNELS :] = jnp.where(first, zero, one)
        mate_out[at : at + CHANNELS, 2 * CHANNELS :] = jnp.where(first, one, zero)
    own_out[:, :CHANNELS] = sums[:quarter]
    own_out[:, CHANNELS : 2 * CHANNELS] = sums[quarter : 2 * quarter]
    mate_out[:, :CHANNELS] = sums[2 * quarter : 3 * quarter]
    mate_out[:, CHANNELS : 2 * CHANNELS] = sums[3 * quarter :]


def middle_kernel(sums, pooled, d_normed, normed, inv, grad, padded, d_mixed_out, message, share):
    window = float(WIN_ROWS * COLS)
    share[...] = jnp.zeros(share.shape, jnp.float32)
    half = WIN_ROWS * COLS
    for cell in range(CELLS):
        part = slice(cell * CHANNELS, (cell + 1) * CHANNELS)
        d_pooled = norm_back(
            sums[:, part], pooled[cell : cell + 1], pooled[CELLS + cell : CELLS + cell + 1]
        )
        d_pooled = d_pooled * (1.0 / window)
        share[cell : cell + 1] = d_pooled
        rows = slice(cell * half, (cell + 1) * half)
        back = norm_back(d_normed[rows] + d_pooled, normed[rows], inv[rows])
        back = grad[rows] + back
        d_mixed_out[cell * WIN_ROWS : (cell + 1) * WIN_ROWS] = back.reshape(
            WIN_ROWS, COLS, CHANNELS
        )
    share[CELLS : CELLS + 1] = sums[:, CELLS * CHANNELS :]
    d_mixed = d_mixed_out[...]
    for i in range(3):
        for j in range(3):
            products = padded[1 + i : 1 + i + ROWS, 1 + j : 1 + j + COLS] * d_mixed
            at = CELLS + 1 + 3 * i + j
            share[at : at + 1] = jnp.sum(jnp.sum(products, 0), 0, keepdims=True)
    message[...] = jnp.broadcast_to(share[...][None], message.shape)


def relay_kernel(place, received, message, share):
    peers = received.shape[0]
    row = place[0]
    for k in range(peers):
        share[k : k + 1] = received[k, CELLS : CELLS + 1]
    total = received[0]
    for k in range(1, peers):
        total = total + received[k]
    share[peers : peers + 9] = total[CELLS + 1 : CELLS + 10]
    for d in range(3):
        at = peers + 9 + d * CELLS
        share[at : at + CELLS] = received[jnp.clip(row + d - 1, 0, peers - 1), 0:CELLS]
    share[31:32] = jnp.zeros((1, CHANNELS), jnp.float32)
    message[...] = jnp.broadcast_to(share[...][None], message.shape)


def end_kernel(
    row_count, col_count, place, near, d_normed, normed, inv, grad, d_mixed, weight,
    d_tokens, g_conv, g_query, g_key, g_value, g_out,
    ring, padded,
):
    row, col = place[0], place[1]
    cores, lines = near.shape[0], near.shape[1]
    first = row_count + 9

    def owner(d_row, d_col, cell):
        k = jnp.clip(col + d_col, 0, col_count - 1)
        at = first + (d_row + 1) * CELLS + cell
        return near[k % 2, k // 2, at : at + 1]

    for start, d_row, cell in ((0, -1, CELLS - 1), (WIDE, 1, 0)):
        ring[start : start + 1] = owner(d_row, -1, cell)
        ring[start + 1 : start + 1 + COLS] = jnp.broadcast_to(
            owner(d_row, 0, cell), (COLS, CHANNELS)
        )
        ring[start + 1 + COLS : start + WIDE] = owner(d_row, 1, cell)
    for start, d_col in ((2 * WIDE, -1), (2 * WIDE + ROWS, 1)):
        for cell in range(CELLS):
            at = start + cell * WIN_ROWS
            ring[at : at + WIN_ROWS] = jnp.broadcast_to(
                owner(0, d_col, cell), (WIN_ROWS, CHANNELS)
            )
    ring[USED:] = jnp.zeros((RING - USED, CHANNELS), jnp.float32)
    back = norm_back(d_normed[...] + ring[...], normed[COUNT:], inv[COUNT:])
    back = grad[COUNT:] + back
    at = lax.broadcasted_iota(jnp.int32, (RING, CHANNELS), 0)
    top, bottom = at < WIDE, (at >= WIDE) & (at < 2 * WIDE)
    left = ((at >= 2 * WIDE) & (at < 2 * WIDE + ROWS)) | (at == 0) | (at == WIDE)
    right = (at >= 2 * WIDE + ROWS) | (at == WIDE - 1) | (at == 2 * WIDE - 1)
    outside = (
        (top & (row == 0))
        | (bottom & (row == row_count - 1))
        | (left & (col == 0))
        | (right & (col == col_count - 1))
    )
    ring[...] = jnp.where(outside, 0.0, back)
    padded[0, 0:WIDE] = ring[0:WIDE]
    padded[ROWS + 1, 0:WIDE] = ring[WIDE : 2 * WIDE]
    for r in range(ROWS):
        k = 2 * WIDE + r
        padded[1 + r, 0:1] = ring[k : k + 1]
        padded[1 + r, WIDE - 1 : WIDE] = ring[k + ROWS : k + ROWS + 1]
    padded[1 : 1 + ROWS, 1 : 1 + COLS] = d_mixed[...]
    total = d_mixed[...]
    for i in range(3):
        for j in range(3):
            total = (
                total
                + weight[i, j : j + 1][None]
                * padded[2 - i : 2 - i + ROWS, 2 - j : 2 - j + COLS]
            )
    d_tokens[...] = total
    root = float(COUNT * row_count * col_count) ** (-0.5)
    conv = near[0, 0, row_count:first]
    for k in range(1, cores * lines):
        conv = conv + near[k // lines, k % lines, row_count:first]
    conv = conv * root
    for k in range(9):
        g_conv[k // 3, k % 3 : k % 3 + 1] = conv[k : k + 1]
    blocks = ((g_query, root), (g_key, 1.0 / POOL), (g_value, 1.0 / POOL), (g_out, root))
    for k in range(cores * lines):
        out, factor = blocks[k * row_count // CHANNELS]
        at = k * row_count % CHANNELS
        out[at : at + row_count] = near[k // lines, k % lines, 0:row_count] * factor


def body(tokens, cotangent, conv_weight, w_query, w_key, w_value, w_out):
    row_count, col_count = lax.axis_size(ROW), lax.axis_size(COL)
    chips, lines = lax.axis_size(CHIPS), lax.axis_size(CHIP_COL)
    place = jnp.stack([lax.axis_index(ROW), lax.axis_index(COL), lax.axis_index("c")])
    tile = (ROWS, COLS, CHANNELS)
    square = (CHANNELS, CHANNELS)
    all_tokens = (COUNT + RING, CHANNELS)

    low, high = call(edge_kernel, [f32(3, COLS, CHANNELS)] * 2, tokens, cotangent)
    above, below = neighbours(low, high, ROW)

    def side(first_t, first_g):
        parts = []
        for k in (first_t, first_t + 1):
            parts += [above[:2, k], tokens[:, k], below[:2, k]]
        return jnp.concatenate(
            parts + [above[2:, first_g], cotangent[:, first_g], below[2:, first_g]]
        )

    before, after = neighbours(side(0, 0), side(COLS - 2, COLS - 1), COL)
    message, pooled, padded, mixed, normed, inv_std, grad = call(
        mix_kernel,
        [
            f32(chips, CELLS, CHANNELS),
            f32(2 * CELLS, CHANNELS),
            f32(ROWS + 4, 24, CHANNELS),
            f32(*tile),
            f32(*all_tokens),
            f32(*all_tokens),
            f32(*all_tokens),
        ],
        tokens, cotangent, above, below, before, after, conv_weight,
        scratch=[(ROWS + 2, 24, CHANNELS)] * 3,
    )

    message = lax.all_to_all(message, CHIPS, 0, 0, tiled=True)
    keys = lax.all_gather(message, "c", axis=0, tiled=True).reshape(-1, CHANNELS)

    columns = HEADS * (COUNT + RING)
    prepared = call(
        before_kernel,
        [f32(CHANNELS, columns)] * 2 + [f32(*square)] * 4,
        normed, grad, w_query, w_key, w_value, w_out,
        flops=1 << 10,
    )
    own, mate, att_t, dq_t, ring_keys = call(
        attend_kernel,
        [
            f32(chips, 3 * CHANNELS),
            f32(chips, 3 * CHANNELS),
            f32(*square),
            f32(*square),
            f32(CHANNELS, HEADS * RING),
        ],
        place[2:], keys, *prepared, w_key, w_value,
        scalars=1, flops=1 << 31,
    )

    received = lax.all_gather(mate, "c", axis=0)
    received = jnp.where(place[2] == 0, received[1], received[0])
    sums = (own + received).reshape(chips, 1, 3 * CHANNELS)
    sums = jnp.sum(lax.all_to_all(sums, CHIPS, 0, 0, tiled=True), 0)
    output, d_normed, d_ring = call(
        after_kernel,
        [f32(*tile), f32(*square), f32(RING, CHANNELS)],
        att_t, dq_t, ring_keys, mixed, w_query, w_key, w_out,
        flops=1 << 10,
    )
    d_mixed, message = call(
        middle_kernel,
        [f32(*tile), f32(row_count, 16, CHANNELS)],
        sums, pooled, d_normed, normed, inv_std, grad, padded,
        scratch=[(16, CHANNELS)],
    )
    message = lax.all_to_all(message, ROW, 0, 0, tiled=True)
    (message,) = call(
        relay_kernel,
        [f32(lines, 32, CHANNELS)],
        place, message,
        scratch=[(32, CHANNELS)], scalars=1,
    )
    message = lax.all_to_all(message, CHIP_COL, 0, 0, tiled=True)
    near = lax.all_gather(message, "c", axis=0)
    results = call(
        functools.partial(end_kernel, row_count, col_count),
        [f32(*tile), f32(3, 3, CHANNELS)] + [f32(*square)] * 4,
        place, near, d_ring, normed, inv_std, grad, d_mixed, conv_weight,
        scratch=[(RING, CHANNELS), (ROWS + 2, 24, CHANNELS)], scalars=1,
    )
    return (output, *results)


def solution(mesh):
    fine = Mesh(mesh.devices.reshape(8, 2, 2, 8, 2), ("y", "xl", "xh", "z", "c"))
    tile = P(ROW, COL, None)
    return jax.shard_map(
        body,
        mesh=fine,
        in_specs=(tile, tile, P(), P(), P(), P(), P()),
        out_specs=(tile, tile, P(), P(), P(), P(), P()),
        check_vma=False,
    )
```

```python
import functools

import jax
import jax.numpy as jnp
from jax import lax
from jax.experimental import pallas as pl
from jax.experimental.pallas import tpu as pltpu
from jax.sharding import Mesh, PartitionSpec as P

HEADS = 2
POOL = 32
ROW = ("y", "xl")
COL = ("xh", "z", "c")
CHIP_COL = ("xh", "z")
CHIPS = CHIP_COL + ROW
ROWS, COLS, CHANNELS = 8, 16, 128
CELLS, WIN_ROWS = 2, 4
COUNT = ROWS * COLS
WIDE = COLS + 2
USED = 2 * WIDE + 2 * ROWS
RING = 64
SIDE = 40
FACING = 6 * COLS
WIDTH = CHANNELS // HEADS
SCALE = WIDTH ** (-0.5)
BOTH = ((1,), (1,))
FIRST = ((0,), (0,))


def product(left, right, dims=((1,), (0,)), precision=lax.Precision.HIGHEST):
    return lax.dot_general(
        left, right, (dims, ((), ())), precision=precision, preferred_element_type=jnp.float32
    )


def normalize(values_in):
    average = jnp.mean(values_in, -1, keepdims=True)
    centered = values_in - average
    inv_std = lax.rsqrt(jnp.mean(centered * centered, -1, keepdims=True) + 1e-06)
    return (centered * inv_std, inv_std)


def norm_back(gradient, normed, inv_std):
    return inv_std * (
        gradient
        - jnp.mean(gradient, -1, keepdims=True)
        - normed * jnp.mean(gradient * normed, -1, keepdims=True)
    )


def f32(*shape):
    return jax.ShapeDtypeStruct(shape, jnp.float32)


def call(kernel, outs, *args, scratch=(), scalars=0, flops=1 << 20):
    in_vmem = pl.BlockSpec(memory_space=pltpu.VMEM)
    specs = [pl.BlockSpec(memory_space=pltpu.SMEM)] * scalars + [in_vmem] * (len(args) - scalars)
    return pl.pallas_call(
        kernel,
        out_shape=outs,
        in_specs=specs,
        out_specs=[in_vmem] * len(outs),
        scratch_shapes=[pltpu.VMEM(shape, jnp.float32) for shape in scratch],
        compiler_params=pltpu.CompilerParams(vmem_limit_bytes=48 << 20),
        cost_estimate=pl.CostEstimate(flops=flops, bytes_accessed=flops, transcendentals=0),
    )(*args)


def seam(axis):
    peers = lax.axis_size(axis)
    return [[k, (k + 1) % peers] for k in range(1, peers, 2)]


def pair_gather(value, axis, groups=None):
    return lax.all_gather(value, axis, axis_index_groups=groups, axis=0)


def edge_kernel(tokens, grad, mine, mates, sems):
    odd, core = lax.axis_index("xl"), lax.axis_index("c")
    copies = []
    for out, last in ((mine, (1 - odd + core) % 2), (mates, (odd + core) % 2)):
        copies += [
            (tokens.at[pl.ds(last * (ROWS - 2), 2)], out.at[0:2]),
            (grad.at[pl.ds(last * (ROWS - 1), 1)], out.at[2:3]),
        ]
    copies = [pltpu.make_async_copy(*copy, sems.at[k]) for k, copy in enumerate(copies)]
    for copy in copies:
        copy.start()
    for copy in copies:
        copy.wait()


def both_kernel(place, mine, shared, strips):
    core = place[2]
    for tile in range(2):
        strips[tile] = jnp.where(core == tile, mine[...], shared[tile])


def reach_kernel(last_row, place, tokens, grad, strips, message):
    row, core = place[0], place[2]
    odd = row % 2
    partner = jnp.where(core == 0, 1 - odd, odd)
    outside = (core == 1) & ((row == 0) | (row == last_row))
    for tile in range(2):
        for r in range(3):
            at = (3 * tile + r) * COLS
            message[at : at + COLS] = jnp.where(outside, 0.0, strips[partner, tile, r])
    right = 1 - core
    for r in range(ROWS):
        for k in range(2):
            message[FACING + k * ROWS + r, :] = tokens[r, right * (COLS - 2) + k]
        message[FACING + 2 * ROWS + r, :] = grad[r, right * (COLS - 1)]


def side_kernel(place, tokens, grad, shared, above, below, beside, beyond):
    row, core = place[0], place[2]
    odd, mate = row % 2, 1 - core
    for r in range(3):
        at = pl.multiple_of((3 * core + r) * COLS, COLS)
        above[r] = shared[1 - odd, pl.ds(at, COLS)]
        below[r] = shared[odd, pl.ds(at, COLS)]
    tall = ROWS + 4
    right = core
    for k in range(2):
        at = right * (COLS - 2) + k
        for r in range(2):
            line = (3 * mate + r) * COLS + at
            beside[k * tall + r, :] = shared[1 - odd, line]
            beside[k * tall + ROWS + 2 + r, :] = shared[odd, line]
            beyond[k * tall + r, :] = above[r, at]
            beyond[k * tall + ROWS + 2 + r, :] = below[r, at]
        for r in range(ROWS):
            beyond[k * tall + 2 + r, :] = tokens[r, at]
        faced = FACING + k * ROWS
        beside[k * tall + 2 : k * tall + 2 + ROWS] = shared[mate, faced : faced + ROWS]
    at = right * (COLS - 1)
    line = (3 * mate + 2) * COLS + at
    beside[2 * tall, :] = shared[1 - odd, line]
    beside[2 * tall + ROWS + 1, :] = shared[odd, line]
    beyond[2 * tall, :] = above[2, at]
    beyond[2 * tall + ROWS + 1, :] = below[2, at]
    faced = FACING + 2 * ROWS
    beside[2 * tall + 1 : 2 * tall + 1 + ROWS] = shared[mate, faced : faced + ROWS]
    for r in range(ROWS):
        beyond[2 * tall + 1 + r, :] = grad[r, at]
    for out in (beside, beyond):
        out[SIDE - 6 :, :] = jnp.zeros((6, CHANNELS), jnp.float32)


def mix_kernel(
    last_col, place, tokens, grad, above, below, beside, beyond, weight,
    message, pooled_out, padded, mixed_out, normed_out, inv_out, grad_out,
    normed_ext, inv_ext, mixed_ext, before, after,
):
    col = place[1]
    even = col % 2 == 0
    before[...] = jnp.where(even, jnp.where(col == 0, 0.0, beyond[0]), beside[...])
    after[...] = jnp.where(even, beside[...], jnp.where(col == last_col, 0.0, beyond[1]))
    padded[2 : 2 + ROWS, 2 : 2 + COLS] = tokens[...]
    padded[0:2, 2 : 2 + COLS] = above[0:2]
    padded[2 + ROWS : 4 + ROWS, 2 : 2 + COLS] = below[0:2]
    tall = ROWS + 4
    for r in range(tall):
        for k in range(2):
            at = k * tall + r
            padded[r, k : k + 1] = before[at : at + 1]
            padded[r, 2 + COLS + k : 3 + COLS + k] = after[at : at + 1]
    mixed = padded[1 : ROWS + 3, 1 : 1 + WIDE]
    for i in range(3):
        for j in range(3):
            mixed = mixed + weight[i, j : j + 1][None] * padded[i : i + ROWS + 2, j : j + WIDE]
    normed, inv_std = normalize(mixed)
    mixed_ext[:, 0:WIDE] = mixed
    normed_ext[:, 0:WIDE] = normed
    inv_ext[:, 0:WIDE] = jnp.broadcast_to(inv_std, normed.shape)
    inner = normed_ext[1 : 1 + ROWS, 1 : 1 + COLS]
    for cell in range(CELLS):
        window = jnp.sum(inner[cell * WIN_ROWS : (cell + 1) * WIN_ROWS], 0)
        pooled = jnp.sum(window, 0, keepdims=True) * (1.0 / (WIN_ROWS * COLS))
        pooled_n, pooled_inv = normalize(pooled)
        pooled_out[cell : cell + 1] = pooled_n
        pooled_out[CELLS + cell : CELLS + cell + 1] = jnp.broadcast_to(pooled_inv, pooled_n.shape)
    message[...] = jnp.broadcast_to(pooled_out[0:CELLS][None], message.shape)
    mixed_out[...] = mixed_ext[1 : 1 + ROWS, 1 : 1 + COLS]
    for ext, out in ((normed_ext, normed_out), (inv_ext, inv_out)):
        out[0:COUNT] = ext[1 : 1 + ROWS, 1 : 1 + COLS].reshape(COUNT, CHANNELS)
        out[COUNT : COUNT + WIDE] = ext[0, 0:WIDE]
        out[COUNT + WIDE : COUNT + 2 * WIDE] = ext[ROWS + 1, 0:WIDE]
        for r in range(ROWS):
            left = COUNT + 2 * WIDE + r
            out[left : left + 1] = ext[1 + r, 0:1]
            out[left + ROWS : left + ROWS + 1] = ext[1 + r, WIDE - 1 : WIDE]
        out[COUNT + USED :] = jnp.zeros((RING - USED, CHANNELS), jnp.float32)
    low = 2 * tall
    high = low + ROWS + 1
    grad_out[0:COUNT] = grad[...].reshape(COUNT, CHANNELS)
    for start, middle, at in ((COUNT, above, low), (COUNT + WIDE, below, high)):
        grad_out[start : start + 1] = before[at : at + 1]
        grad_out[start + 1 : start + 1 + COLS] = middle[2]
        grad_out[start + 1 + COLS : start + WIDE] = after[at : at + 1]
    left = COUNT + 2 * WIDE
    grad_out[left : left + ROWS] = before[low + 1 : high]
    grad_out[left + ROWS : left + 2 * ROWS] = after[low + 1 : high]
    grad_out[COUNT + USED :] = jnp.zeros((RING - USED, CHANNELS), jnp.float32)


def top_half():
    return lax.broadcasted_iota(jnp.int32, (CHANNELS, CHANNELS), 0) < WIDTH


def before_kernel(
    normed, grad, w_query, w_key, w_value, w_out,
    to_keys, to_values, query_t, d_att_t, normed_t, grad_t,
):
    upper = top_half()

    def by_head(weight, value, ring, out):
        for head, mask in enumerate((upper, ~upper)):
            at = head * COUNT
            out[:, at : at + COUNT] = product(weight, jnp.where(mask, value, 0.0))
        parts = [
            product(weight, jnp.where(mask[:, :RING], ring, 0.0)) for mask in (upper, ~upper)
        ]
        out[:, HEADS * COUNT :] = jnp.concatenate(parts, 1)

    inner, ring = normed[0:COUNT].T, normed[COUNT:].T
    normed_t[...] = inner
    query = product(w_query[...], inner, FIRST)
    query_t[...] = query
    by_head(w_key[...] * SCALE, query, product(w_query[...], ring, FIRST), to_keys)
    inner, ring = grad[0:COUNT].T, grad[COUNT:].T
    grad_t[...] = inner
    d_att = product(w_out[...], inner)
    d_att_t[...] = d_att
    by_head(w_value[...], d_att, product(w_out[...], ring), to_values)


def after_kernel(att_t, dq_t, ring_keys, mixed, w_query, w_key, w_out, output, d_normed, d_ring):
    att_out = product(att_t[...], w_out[...], FIRST)
    output[...] = mixed[...] + att_out.reshape(ROWS, COLS, CHANNELS)
    back = w_query[...].T
    d_normed[...] = product(dq_t[...], back, FIRST)
    ring = product(w_key[...], ring_keys[...], FIRST)
    ring = jnp.where(top_half()[:, :RING], ring[:, :RING], ring[:, RING:]) * SCALE
    d_ring[...] = product(ring, back, FIRST)


def pieces(value, count):
    parts = []
    for _ in range(count - 1):
        parts.append(value.astype(jnp.bfloat16))
        value = value - parts[-1].astype(jnp.float32)
    return parts + [value.astype(jnp.bfloat16)]


def single(left, right, dims=((1,), (0,))):
    return product(left, right, dims, lax.Precision.DEFAULT)


def attend_kernel(
    core, keys_ref, to_keys, to_values, query_t, d_att_t, normed_t, grad_t, w_key, w_value,
    own_out, mate_out, att_out, dq_out, ring_out,
):
    own = core[0] * (keys_ref.shape[0] // 2)
    mate = keys_ref.shape[0] // 2 - own
    quarter = keys_ref.shape[0] // 4
    keys = jnp.concatenate(
        [
            keys_ref[pl.ds(start, quarter, stride=2)]
            for start in (own, own + 1, mate, mate + 1)
        ]
    )
    wide = HEADS * COUNT
    k0, k1, k2 = pieces(keys, 3)
    q0, q1, q2 = pieces(to_keys[...], 3)
    v0, v1 = pieces(to_values[...], 2)
    scores = single(
        jnp.concatenate([k0, k0, k1, k0, k2, k1], 1), jnp.concatenate([q0, q1, q0, q2, q0, q1])
    )
    d_probs = single(jnp.concatenate([k0, k0, k1], 1), jnp.concatenate([v0, v1, v0]))
    weights = jnp.exp(scores - jnp.max(scores, 0, keepdims=True))
    probs = weights * (1.0 / jnp.sum(weights, 0, keepdims=True))
    t0, t1 = pieces(keys.T, 2)
    both_t = jnp.concatenate([t0, t1])

    def by_keys(high, low):
        twice = single(both_t, high)
        return twice[:CHANNELS] + (twice[CHANNELS:] + single(t0, low))

    d_scores = probs * (d_probs - jnp.sum(d_probs * probs, 0, keepdims=True))
    d0, d1 = pieces(d_scores, 2)
    d_query_keys = by_keys(d0, d1)
    p0, p1 = pieces(probs[:, :wide], 2)
    att_keys = by_keys(p0, p1)
    d0, d1 = d0[:, :wide], d1[:, :wide]
    large = jnp.concatenate([q0[:, :wide], v0[:, :wide]], 1)
    small = jnp.concatenate([q1[:, :wide], v1[:, :wide]], 1)
    twice = single(
        jnp.concatenate([d0, p0], 1), jnp.concatenate([large, small]), BOTH
    )
    sums = twice[:, :CHANNELS] + (
        twice[:, CHANNELS:] + single(jnp.concatenate([d1, p1], 1), large, BOTH)
    )
    upper = top_half()
    left = lax.broadcasted_iota(jnp.int32, (CHANNELS, CHANNELS), 1) < WIDTH

    def heads(first, second, mask=upper):
        return jnp.where(mask, first, second)

    z0, z1 = att_keys[:, :COUNT], att_keys[:, COUNT:wide]
    y0, y1 = d_query_keys[:, :COUNT], d_query_keys[:, COUNT:wide]
    att_t = heads(product(w_value[...], z0, FIRST), product(w_value[...], z1, FIRST))
    dq_t = heads(product(w_key[...], y0, FIRST), product(w_key[...], y1, FIRST)) * SCALE
    q, a = query_t[...], d_att_t[...]
    g_query = product(normed_t[...], dq_t, BOTH)
    g_key = heads(product(y0, q, BOTH), product(y1, q, BOTH), left) * SCALE
    g_value = heads(product(z0, a, BOTH), product(z1, a, BOTH), left)
    g_out = product(att_t, grad_t[...], BOTH)
    att_out[...] = att_t
    dq_out[...] = dq_t
    ring_out[...] = d_query_keys[:, wide:]
    first = core[0] == 0
    by_core = ((g_query, g_key), (g_value, g_out))
    for half in range(2):
        at = half * CHANNELS
        zero, one = by_core[0][half], by_core[1][half]
        own_out[at : at + CHANNELS, 2 * CHANNELS :] = jnp.where(first, zero, one)
        mate_out[at : at + CHANNELS, 2 * CHANNELS :] = jnp.where(first, one, zero)
    own_out[:, :CHANNELS] = sums[:quarter]
    own_out[:, CHANNELS : 2 * CHANNELS] = sums[quarter : 2 * quarter]
    mate_out[:, :CHANNELS] = sums[2 * quarter : 3 * quarter]
    mate_out[:, CHANNELS : 2 * CHANNELS] = sums[3 * quarter :]


def middle_kernel(sums, pooled, d_normed, normed, inv, grad, padded, d_mixed_out, message, share):
    window = float(WIN_ROWS * COLS)
    share[...] = jnp.zeros(share.shape, jnp.float32)
    half = WIN_ROWS * COLS
    for cell in range(CELLS):
        part = slice(cell * CHANNELS, (cell + 1) * CHANNELS)
        d_pooled = norm_back(
            sums[:, part], pooled[cell : cell + 1], pooled[CELLS + cell : CELLS + cell + 1]
        )
        d_pooled = d_pooled * (1.0 / window)
        share[cell : cell + 1] = d_pooled
        rows = slice(cell * half, (cell + 1) * half)
        back = norm_back(d_normed[rows] + d_pooled, normed[rows], inv[rows])
        back = grad[rows] + back
        d_mixed_out[cell * WIN_ROWS : (cell + 1) * WIN_ROWS] = back.reshape(
            WIN_ROWS, COLS, CHANNELS
        )
    share[CELLS : CELLS + 1] = sums[:, CELLS * CHANNELS :]
    d_mixed = d_mixed_out[...]
    for i in range(3):
        for j in range(3):
            products = padded[1 + i : 1 + i + ROWS, 1 + j : 1 + j + COLS] * d_mixed
            at = CELLS + 1 + 3 * i + j
            share[at : at + 1] = jnp.sum(jnp.sum(products, 0), 0, keepdims=True)
    message[...] = jnp.broadcast_to(share[...][None], message.shape)


def relay_kernel(place, received, message, share):
    peers = received.shape[0]
    row = place[0]
    for k in range(peers):
        share[k : k + 1] = received[k, CELLS : CELLS + 1]
    total = received[0]
    for k in range(1, peers):
        total = total + received[k]
    share[peers : peers + 9] = total[CELLS + 1 : CELLS + 10]
    for d in range(3):
        at = peers + 9 + d * CELLS
        share[at : at + CELLS] = received[jnp.clip(row + d - 1, 0, peers - 1), 0:CELLS]
    share[31:32] = jnp.zeros((1, CHANNELS), jnp.float32)
    message[...] = jnp.broadcast_to(share[...][None], message.shape)


def end_kernel(
    row_count, col_count, place, near, d_normed, normed, inv, grad, d_mixed, weight,
    d_tokens, g_conv, g_query, g_key, g_value, g_out,
    ring, padded,
):
    row, col = place[0], place[1]
    cores, lines = near.shape[0], near.shape[1]
    first = row_count + 9

    def owner(d_row, d_col, cell):
        k = jnp.clip(col + d_col, 0, col_count - 1)
        at = first + (d_row + 1) * CELLS + cell
        return near[k % 2, k // 2, at : at + 1]

    for start, d_row, cell in ((0, -1, CELLS - 1), (WIDE, 1, 0)):
        ring[start : start + 1] = owner(d_row, -1, cell)
        ring[start + 1 : start + 1 + COLS] = jnp.broadcast_to(
            owner(d_row, 0, cell), (COLS, CHANNELS)
        )
        ring[start + 1 + COLS : start + WIDE] = owner(d_row, 1, cell)
    for start, d_col in ((2 * WIDE, -1), (2 * WIDE + ROWS, 1)):
        for cell in range(CELLS):
            at = start + cell * WIN_ROWS
            ring[at : at + WIN_ROWS] = jnp.broadcast_to(
                owner(0, d_col, cell), (WIN_ROWS, CHANNELS)
            )
    ring[USED:] = jnp.zeros((RING - USED, CHANNELS), jnp.float32)
    back = norm_back(d_normed[...] + ring[...], normed[COUNT:], inv[COUNT:])
    back = grad[COUNT:] + back
    at = lax.broadcasted_iota(jnp.int32, (RING, CHANNELS), 0)
    top, bottom = at < WIDE, (at >= WIDE) & (at < 2 * WIDE)
    left = ((at >= 2 * WIDE) & (at < 2 * WIDE + ROWS)) | (at == 0) | (at == WIDE)
    right = (at >= 2 * WIDE + ROWS) | (at == WIDE - 1) | (at == 2 * WIDE - 1)
    outside = (
        (top & (row == 0))
        | (bottom & (row == row_count - 1))
        | (left & (col == 0))
        | (right & (col == col_count - 1))
    )
    ring[...] = jnp.where(outside, 0.0, back)
    padded[0, 0:WIDE] = ring[0:WIDE]
    padded[ROWS + 1, 0:WIDE] = ring[WIDE : 2 * WIDE]
    for r in range(ROWS):
        k = 2 * WIDE + r
        padded[1 + r, 0:1] = ring[k : k + 1]
        padded[1 + r, WIDE - 1 : WIDE] = ring[k + ROWS : k + ROWS + 1]
    padded[1 : 1 + ROWS, 1 : 1 + COLS] = d_mixed[...]
    total = d_mixed[...]
    for i in range(3):
        for j in range(3):
            total = (
                total
                + weight[i, j : j + 1][None]
                * padded[2 - i : 2 - i + ROWS, 2 - j : 2 - j + COLS]
            )
    d_tokens[...] = total
    root = float(COUNT * row_count * col_count) ** (-0.5)
    conv = near[0, 0, row_count:first]
    for k in range(1, cores * lines):
        conv = conv + near[k // lines, k % lines, row_count:first]
    conv = conv * root
    for k in range(9):
        g_conv[k // 3, k % 3 : k % 3 + 1] = conv[k : k + 1]
    blocks = ((g_query, root), (g_key, 1.0 / POOL), (g_value, 1.0 / POOL), (g_out, root))
    for k in range(cores * lines):
        out, factor = blocks[k * row_count // CHANNELS]
        at = k * row_count % CHANNELS
        out[at : at + row_count] = near[k // lines, k % lines, 0:row_count] * factor


def body(tokens, cotangent, conv_weight, w_query, w_key, w_value, w_out):
    row_count, col_count = lax.axis_size(ROW), lax.axis_size(COL)
    chips, lines = lax.axis_size(CHIPS), lax.axis_size(CHIP_COL)
    place = jnp.stack([lax.axis_index(ROW), lax.axis_index(COL), lax.axis_index("c")])
    tile = (ROWS, COLS, CHANNELS)
    square = (CHANNELS, CHANNELS)
    all_tokens = (COUNT + RING, CHANNELS)

    anywhere = pl.BlockSpec(memory_space=pl.ANY)
    mine, mates = pl.pallas_call(
        edge_kernel,
        out_shape=[f32(3, COLS, CHANNELS)] * 2,
        in_specs=[anywhere] * 2,
        out_specs=[pl.BlockSpec(memory_space=pltpu.VMEM)] * 2,
        scratch_shapes=[pltpu.SemaphoreType.DMA((4,))],
    )(tokens, cotangent)
    mates = pair_gather(mates, "c")
    (strips,) = call(both_kernel, [f32(2, 3, COLS, CHANNELS)], place, mine, mates, scalars=1)
    pairs = [[4 * k, 4 * k + 2] for k in range(row_count // 2)]
    pairs += [[2 * j + 1, 2 * k + 1] for j, k in seam(ROW)]
    strips = pair_gather(strips, ROW + ("c",), pairs)
    (shared,) = call(
        functools.partial(reach_kernel, row_count - 1),
        [f32(FACING + 3 * ROWS, CHANNELS)],
        place, tokens, cotangent, strips,
        scalars=1,
    )
    shared = pair_gather(shared, "c")
    above, below, beside, beyond = call(
        side_kernel,
        [f32(3, COLS, CHANNELS)] * 2 + [f32(SIDE, CHANNELS)] * 2,
        place, tokens, cotangent, shared,
        scalars=1,
    )
    beyond = pair_gather(beyond, COL, seam(COL))
    message, pooled, padded, mixed, normed, inv_std, grad = call(
        functools.partial(mix_kernel, col_count - 1),
        [
            f32(chips, CELLS, CHANNELS),
            f32(2 * CELLS, CHANNELS),
            f32(ROWS + 4, 24, CHANNELS),
            f32(*tile),
            f32(*all_tokens),
            f32(*all_tokens),
            f32(*all_tokens),
        ],
        place, tokens, cotangent, above, below, beside, beyond, conv_weight,
        scratch=[(ROWS + 2, 24, CHANNELS)] * 3 + [(SIDE, CHANNELS)] * 2, scalars=1,
    )

    message = lax.all_to_all(message, CHIPS, 0, 0, tiled=True)
    keys = lax.all_gather(message, "c", axis=0, tiled=True).reshape(-1, CHANNELS)

    columns = HEADS * (COUNT + RING)
    prepared = call(
        before_kernel,
        [f32(CHANNELS, columns)] * 2 + [f32(*square)] * 4,
        normed, grad, w_query, w_key, w_value, w_out,
        flops=1 << 10,
    )
    own, mate, att_t, dq_t, ring_keys = call(
        attend_kernel,
        [
            f32(chips, 3 * CHANNELS),
            f32(chips, 3 * CHANNELS),
            f32(*square),
            f32(*square),
            f32(CHANNELS, HEADS * RING),
        ],
        place[2:], keys, *prepared, w_key, w_value,
        scalars=1, flops=1 << 31,
    )

    received = lax.all_gather(mate, "c", axis=0)
    received = jnp.where(place[2] == 0, received[1], received[0])
    sums = (own + received).reshape(chips, 1, 3 * CHANNELS)
    sums = jnp.sum(lax.all_to_all(sums, CHIPS, 0, 0, tiled=True), 0)
    output, d_normed, d_ring = call(
        after_kernel,
        [f32(*tile), f32(*square), f32(RING, CHANNELS)],
        att_t, dq_t, ring_keys, mixed, w_query, w_key, w_out,
        flops=1 << 10,
    )
    d_mixed, message = call(
        middle_kernel,
        [f32(*tile), f32(row_count, 16, CHANNELS)],
        sums, pooled, d_normed, normed, inv_std, grad, padded,
        scratch=[(16, CHANNELS)],
    )
    message = lax.all_to_all(message, ROW, 0, 0, tiled=True)
    (message,) = call(
        relay_kernel,
        [f32(lines, 32, CHANNELS)],
        place, message,
        scratch=[(32, CHANNELS)], scalars=1,
    )
    message = lax.all_to_all(message, CHIP_COL, 0, 0, tiled=True)
    near = lax.all_gather(message, "c", axis=0)
    results = call(
        functools.partial(end_kernel, row_count, col_count),
        [f32(*tile), f32(3, 3, CHANNELS)] + [f32(*square)] * 4,
        place, near, d_ring, normed, inv_std, grad, d_mixed, conv_weight,
        scratch=[(RING, CHANNELS), (ROWS + 2, 24, CHANNELS)], scalars=1,
    )
    return (output, *results)


def solution(mesh):
    fine = Mesh(mesh.devices.reshape(8, 2, 2, 8, 2), ("y", "xl", "xh", "z", "c"))
    tile = P(ROW, COL, None)
    return jax.shard_map(
        body,
        mesh=fine,
        in_specs=(tile, tile, P(), P(), P(), P(), P()),
        out_specs=(tile, tile, P(), P(), P(), P(), P()),
        check_vma=False,
    )
```

```python
import functools

import jax
import jax.numpy as jnp
from jax import lax
from jax.experimental import pallas as pl
from jax.experimental.pallas import tpu as pltpu
from jax.sharding import Mesh, PartitionSpec as P

HEADS = 2
POOL = 32
ROW = ("y", "xl")
COL = ("xh", "z", "c")
CHIP_COL = ("xh", "z")
ROW_GROUP = ("xl", "y")
CHIPS = ("z", "xh") + ROW_GROUP
ROWS, COLS, CHANNELS = 8, 16, 128
CELLS, WIN_ROWS = 2, 4
COUNT = ROWS * COLS
WIDE = COLS + 2
USED = 2 * WIDE + 2 * ROWS
RING = 64
SIDE = 40
FACING = 6 * COLS
WIDTH = CHANNELS // HEADS
SCALE = WIDTH ** (-0.5)
BOTH = ((1,), (1,))
FIRST = ((0,), (0,))


def product(left, right, dims=((1,), (0,)), precision=lax.Precision.HIGHEST):
    return lax.dot_general(
        left, right, (dims, ((), ())), precision=precision, preferred_element_type=jnp.float32
    )


def normalize(values_in):
    average = jnp.mean(values_in, -1, keepdims=True)
    centered = values_in - average
    inv_std = lax.rsqrt(jnp.mean(centered * centered, -1, keepdims=True) + 1e-06)
    return (centered * inv_std, inv_std)


def norm_back(gradient, normed, inv_std):
    return inv_std * (
        gradient
        - jnp.mean(gradient, -1, keepdims=True)
        - normed * jnp.mean(gradient * normed, -1, keepdims=True)
    )


def here():
    core = lax.axis_index("c")
    row = lax.axis_index("y") * lax.axis_size("xl") + lax.axis_index("xl")
    chip = lax.axis_index("xh") * lax.axis_size("z") + lax.axis_index("z")
    return row, chip * lax.axis_size("c") + core, core


def f32(*shape):
    return jax.ShapeDtypeStruct(shape, jnp.float32)


def call(kernel, outs, *args, scratch=(), flops=1 << 20):
    in_vmem = pl.BlockSpec(memory_space=pltpu.VMEM)
    return pl.pallas_call(
        kernel,
        out_shape=outs,
        in_specs=[in_vmem] * len(args),
        out_specs=[in_vmem] * len(outs),
        scratch_shapes=[pltpu.VMEM(shape, jnp.float32) for shape in scratch],
        compiler_params=pltpu.CompilerParams(vmem_limit_bytes=48 << 20),
        cost_estimate=pl.CostEstimate(flops=flops, bytes_accessed=flops, transcendentals=0),
    )(*args)


def seam(axis):
    peers = lax.axis_size(axis)
    return [[k, (k + 1) % peers] for k in range(1, peers, 2)]


def pair_gather(value, axis, groups=None):
    return lax.all_gather(value, axis, axis_index_groups=groups, axis=0)


def edge_kernel(tokens, grad, mine, mates, sems):
    odd, core = lax.axis_index("xl"), lax.axis_index("c")
    copies = []
    for out, last in ((mine, (1 - odd + core) % 2), (mates, (odd + core) % 2)):
        copies += [
            (tokens.at[pl.ds(last * (ROWS - 2), 2)], out.at[0:2]),
            (grad.at[pl.ds(last * (ROWS - 1), 1)], out.at[2:3]),
        ]
    copies = [pltpu.make_async_copy(*copy, sems.at[k]) for k, copy in enumerate(copies)]
    for copy in copies:
        copy.start()
    for copy in copies:
        copy.wait()


def both_kernel(mine, shared, strips):
    core = here()[2]
    for tile in range(2):
        strips[tile] = jnp.where(core == tile, mine[...], shared[tile])


def reach_kernel(last_row, tokens, grad, weight, strips, message, taps):
    row, _, core = here()
    odd = row % 2
    partner = jnp.where(core == 0, 1 - odd, odd)
    outside = (core == 1) & ((row == 0) | (row == last_row))
    for tile in range(2):
        for r in range(3):
            at = (3 * tile + r) * COLS
            message[at : at + COLS] = jnp.where(outside, 0.0, strips[partner, tile, r])
    for k in range(9):
        taps[k : k + 1] = weight[k // 3, k % 3 : k % 3 + 1]
    right = 1 - core
    for r in range(ROWS):
        for k in range(2):
            message[FACING + k * ROWS + r, :] = tokens[r, right * (COLS - 2) + k]
        message[FACING + 2 * ROWS + r, :] = grad[r, right * (COLS - 1)]


def side_kernel(tokens, grad, shared, above, below, beside, beyond):
    row, _, core = here()
    odd, mate = row % 2, 1 - core
    for r in range(3):
        at = pl.multiple_of((3 * core + r) * COLS, COLS)
        above[r] = shared[1 - odd, pl.ds(at, COLS)]
        below[r] = shared[odd, pl.ds(at, COLS)]
    tall = ROWS + 4
    right = core
    for k in range(2):
        at = right * (COLS - 2) + k
        for r in range(2):
            line = (3 * mate + r) * COLS + at
            beside[k * tall + r, :] = shared[1 - odd, line]
            beside[k * tall + ROWS + 2 + r, :] = shared[odd, line]
            beyond[k * tall + r, :] = above[r, at]
            beyond[k * tall + ROWS + 2 + r, :] = below[r, at]
        for r in range(ROWS):
            beyond[k * tall + 2 + r, :] = tokens[r, at]
        faced = FACING + k * ROWS
        beside[k * tall + 2 : k * tall + 2 + ROWS] = shared[mate, faced : faced + ROWS]
    at = right * (COLS - 1)
    line = (3 * mate + 2) * COLS + at
    beside[2 * tall, :] = shared[1 - odd, line]
    beside[2 * tall + ROWS + 1, :] = shared[odd, line]
    beyond[2 * tall, :] = above[2, at]
    beyond[2 * tall + ROWS + 1, :] = below[2, at]
    faced = FACING + 2 * ROWS
    beside[2 * tall + 1 : 2 * tall + 1 + ROWS] = shared[mate, faced : faced + ROWS]
    for r in range(ROWS):
        beyond[2 * tall + 1 + r, :] = grad[r, at]
    for out in (beside, beyond):
        out[SIDE - 6 :, :] = jnp.zeros((6, CHANNELS), jnp.float32)


def mix_kernel(
    last_col, tokens, grad, above, below, beside, beyond, weight,
    message, pooled_out, padded, mixed_out, normed_out, inv_out, grad_out,
    normed_ext, inv_ext, mixed_ext, before, after,
):
    col = here()[1]
    even = col % 2 == 0
    before[...] = jnp.where(even, jnp.where(col == 0, 0.0, beyond[0]), beside[...])
    after[...] = jnp.where(even, beside[...], jnp.where(col == last_col, 0.0, beyond[1]))
    padded[2 : 2 + ROWS, 2 : 2 + COLS] = tokens[...]
    padded[0:2, 2 : 2 + COLS] = above[0:2]
    padded[2 + ROWS : 4 + ROWS, 2 : 2 + COLS] = below[0:2]
    tall = ROWS + 4
    for r in range(tall):
        for k in range(2):
            at = k * tall + r
            padded[r, k : k + 1] = before[at : at + 1]
            padded[r, 2 + COLS + k : 3 + COLS + k] = after[at : at + 1]
    mixed = padded[1 : ROWS + 3, 1 : 1 + WIDE]
    for i in range(3):
        for j in range(3):
            mixed = mixed + weight[3 * i + j : 3 * i + j + 1][None] * padded[i : i + ROWS + 2, j : j + WIDE]
    normed, inv_std = normalize(mixed)
    mixed_ext[:, 0:WIDE] = mixed
    normed_ext[:, 0:WIDE] = normed
    inv_ext[:, 0:WIDE] = jnp.broadcast_to(inv_std, normed.shape)
    inner = normed_ext[1 : 1 + ROWS, 1 : 1 + COLS]
    for cell in range(CELLS):
        window = jnp.sum(inner[cell * WIN_ROWS : (cell + 1) * WIN_ROWS], 0)
        pooled = jnp.sum(window, 0, keepdims=True) * (1.0 / (WIN_ROWS * COLS))
        pooled_n, pooled_inv = normalize(pooled)
        pooled_out[cell : cell + 1] = pooled_n
        pooled_out[CELLS + cell : CELLS + cell + 1] = jnp.broadcast_to(pooled_inv, pooled_n.shape)
    message[...] = jnp.broadcast_to(pooled_out[0:CELLS][None], message.shape)
    mixed_out[...] = mixed_ext[1 : 1 + ROWS, 1 : 1 + COLS]
    for ext, out in ((normed_ext, normed_out), (inv_ext, inv_out)):
        out[0:COUNT] = ext[1 : 1 + ROWS, 1 : 1 + COLS].reshape(COUNT, CHANNELS)
        out[COUNT : COUNT + WIDE] = ext[0, 0:WIDE]
        out[COUNT + WIDE : COUNT + 2 * WIDE] = ext[ROWS + 1, 0:WIDE]
        for r in range(ROWS):
            left = COUNT + 2 * WIDE + r
            out[left : left + 1] = ext[1 + r, 0:1]
            out[left + ROWS : left + ROWS + 1] = ext[1 + r, WIDE - 1 : WIDE]
        out[COUNT + USED :] = jnp.zeros((RING - USED, CHANNELS), jnp.float32)
    low = 2 * tall
    high = low + ROWS + 1
    grad_out[0:COUNT] = grad[...].reshape(COUNT, CHANNELS)
    for start, middle, at in ((COUNT, above, low), (COUNT + WIDE, below, high)):
        grad_out[start : start + 1] = before[at : at + 1]
        grad_out[start + 1 : start + 1 + COLS] = middle[2]
        grad_out[start + 1 + COLS : start + WIDE] = after[at : at + 1]
    left = COUNT + 2 * WIDE
    grad_out[left : left + ROWS] = before[low + 1 : high]
    grad_out[left + ROWS : left + 2 * ROWS] = after[low + 1 : high]
    grad_out[COUNT + USED :] = jnp.zeros((RING - USED, CHANNELS), jnp.float32)


def top_half():
    return lax.broadcasted_iota(jnp.int32, (CHANNELS, CHANNELS), 0) < WIDTH


def by_head(weight, value, ring, out):
    upper = top_half()
    for head, mask in enumerate((upper, ~upper)):
        at = head * COUNT
        out[:, at : at + COUNT] = product(weight, jnp.where(mask, value, 0.0))
    parts = [product(weight, jnp.where(mask[:, :RING], ring, 0.0)) for mask in (upper, ~upper)]
    out[:, HEADS * COUNT :] = jnp.concatenate(parts, 1)


def before_kernel(
    normed, grad, w_query, w_key, w_value, w_out,
    to_keys, to_values, query_t, d_att_t, normed_t, grad_t,
):
    normed_t[...], grad_t[...] = normed[0:COUNT].T, grad[0:COUNT].T
    query_t[...] = product(w_query[...], normed_t[...], FIRST)
    d_att_t[...] = product(w_out[...], grad_t[...])
    ring = product(w_query[...], normed[COUNT:].T, FIRST)
    by_head(w_key[...] * SCALE, query_t[...], ring, to_keys)
    ring = product(w_out[...], grad[COUNT:].T)
    by_head(w_value[...], d_att_t[...], ring, to_values)


def pieces(value, count):
    parts = []
    for _ in range(count - 1):
        parts.append(value.astype(jnp.bfloat16))
        value = value - parts[-1].astype(jnp.float32)
    return parts + [value.astype(jnp.bfloat16)]


def single(left, right, dims=((1,), (0,))):
    return product(left, right, dims, lax.Precision.DEFAULT)


def attend_kernel(
    keys_ref, to_keys, to_values, query_t, d_att_t, normed_t, grad_t,
    w_query, w_key, w_value, w_out,
    own_out, mate_out, att_out, d_normed, d_ring,
):
    core = here()[2]
    own = core * (keys_ref.shape[0] // 2)
    mate = keys_ref.shape[0] // 2 - own
    quarter = keys_ref.shape[0] // 4
    keys = jnp.concatenate(
        [
            keys_ref[pl.ds(start, quarter, stride=2)]
            for start in (own, own + 1, mate, mate + 1)
        ]
    )
    wide = HEADS * COUNT
    k0, k1, k2 = pieces(keys, 3)
    q0, q1, q2 = pieces(to_keys[...], 3)
    v0, v1 = pieces(to_values[...], 2)
    scores = single(
        jnp.concatenate([k0, k0, k1, k0, k2, k1], 1), jnp.concatenate([q0, q1, q0, q2, q0, q1])
    )
    d_probs = single(jnp.concatenate([k0, k0, k1], 1), jnp.concatenate([v0, v1, v0]))
    weights = jnp.exp(scores - jnp.max(scores, 0, keepdims=True))
    probs = weights * (1.0 / jnp.sum(weights, 0, keepdims=True))
    t0, t1 = pieces(keys.T, 2)
    both_t = jnp.concatenate([t0, t1])

    def by_keys(high, low):
        twice = single(both_t, high)
        return twice[:CHANNELS] + (twice[CHANNELS:] + single(t0, low))

    d_scores = probs * (d_probs - jnp.sum(d_probs * probs, 0, keepdims=True))
    d0, d1 = pieces(d_scores, 2)
    d_query_keys = by_keys(d0, d1)
    p0, p1 = pieces(probs[:, :wide], 2)
    att_keys = by_keys(p0, p1)
    d0, d1 = d0[:, :wide], d1[:, :wide]
    large = jnp.concatenate([q0[:, :wide], v0[:, :wide]], 1)
    small = jnp.concatenate([q1[:, :wide], v1[:, :wide]], 1)
    twice = single(
        jnp.concatenate([d0, p0], 1), jnp.concatenate([large, small]), BOTH
    )
    sums = twice[:, :CHANNELS] + (
        twice[:, CHANNELS:] + single(jnp.concatenate([d1, p1], 1), large, BOTH)
    )
    upper = top_half()
    left = lax.broadcasted_iota(jnp.int32, (CHANNELS, CHANNELS), 1) < WIDTH

    def heads(first, second, mask=upper):
        return jnp.where(mask, first, second)

    z0, z1 = att_keys[:, :COUNT], att_keys[:, COUNT:wide]
    y0, y1 = d_query_keys[:, :COUNT], d_query_keys[:, COUNT:wide]
    att_t = heads(product(w_value[...], z0, FIRST), product(w_value[...], z1, FIRST))
    dq_t = heads(product(w_key[...], y0, FIRST), product(w_key[...], y1, FIRST)) * SCALE
    q, a = query_t[...], d_att_t[...]
    g_query = product(normed_t[...], dq_t, BOTH)
    g_key = heads(product(y0, q, BOTH), product(y1, q, BOTH), left) * SCALE
    g_value = heads(product(z0, a, BOTH), product(z1, a, BOTH), left)
    g_out = product(att_t, grad_t[...], BOTH)
    att_out[...] = product(att_t, w_out[...], FIRST)
    back = w_query[...].T
    d_normed[...] = product(dq_t, back, FIRST)
    ring = product(w_key[...], d_query_keys[:, wide:], FIRST)
    ring = jnp.where(upper[:, :RING], ring[:, :RING], ring[:, RING:]) * SCALE
    d_ring[...] = product(ring, back, FIRST)
    first = core == 0
    by_core = ((g_query, g_key), (g_value, g_out))
    for half in range(2):
        at = half * CHANNELS
        zero, one = by_core[0][half], by_core[1][half]
        own_out[at : at + CHANNELS, 2 * CHANNELS :] = jnp.where(first, zero, one)
        mate_out[at : at + CHANNELS, 2 * CHANNELS :] = jnp.where(first, one, zero)
    own_out[:, :CHANNELS] = sums[:quarter]
    own_out[:, CHANNELS : 2 * CHANNELS] = sums[quarter : 2 * quarter]
    mate_out[:, :CHANNELS] = sums[2 * quarter : 3 * quarter]
    mate_out[:, CHANNELS : 2 * CHANNELS] = sums[3 * quarter :]


def middle_kernel(sums, pooled, d_normed, normed, inv, grad, padded, d_mixed_out, message, share):
    window = float(WIN_ROWS * COLS)
    share[...] = jnp.zeros(share.shape, jnp.float32)
    half = WIN_ROWS * COLS
    for cell in range(CELLS):
        part = slice(cell * CHANNELS, (cell + 1) * CHANNELS)
        d_pooled = norm_back(
            sums[:, part], pooled[cell : cell + 1], pooled[CELLS + cell : CELLS + cell + 1]
        )
        d_pooled = d_pooled * (1.0 / window)
        share[cell : cell + 1] = d_pooled
        rows = slice(cell * half, (cell + 1) * half)
        back = norm_back(d_normed[rows] + d_pooled, normed[rows], inv[rows])
        back = grad[rows] + back
        d_mixed_out[cell * WIN_ROWS : (cell + 1) * WIN_ROWS] = back.reshape(
            WIN_ROWS, COLS, CHANNELS
        )
    share[CELLS : CELLS + 1] = sums[:, CELLS * CHANNELS :]
    d_mixed = d_mixed_out[...]
    for i in range(3):
        for j in range(3):
            products = padded[1 + i : 1 + i + ROWS, 1 + j : 1 + j + COLS] * d_mixed
            at = CELLS + 1 + 3 * i + j
            share[at : at + 1] = jnp.sum(jnp.sum(products, 0), 0, keepdims=True)
    message[...] = jnp.broadcast_to(share[...][None], message.shape)


def relay_kernel(received, message, share):
    peers = received.shape[0]
    row = here()[0]
    for k in range(peers):
        share[k : k + 1] = received[k, CELLS : CELLS + 1]
    total = received[0]
    for k in range(1, peers):
        total = total + received[k]
    share[peers : peers + 9] = total[CELLS + 1 : CELLS + 10]
    for d in range(3):
        at = peers + 9 + d * CELLS
        near = jnp.clip(row + d - 1, 0, peers - 1)
        share[at : at + CELLS] = received[near % 2 * (peers // 2) + near // 2, 0:CELLS]
    share[31:32] = jnp.zeros((1, CHANNELS), jnp.float32)
    message[...] = jnp.broadcast_to(share[...][None], message.shape)


def end_kernel(
    row_count, col_count, near, d_normed, normed, inv, grad, d_mixed, weight, mixed, att,
    output, d_tokens, g_conv, g_query, g_key, g_value, g_out,
    ring, padded,
):
    row, col, _ = here()
    cores, lines = near.shape[0], near.shape[1]
    first = row_count + 9

    def owner(d_row, d_col, cell):
        k = jnp.clip(col + d_col, 0, col_count - 1)
        at = first + (d_row + 1) * CELLS + cell
        return near[k % 2, k // 2, at : at + 1]

    for start, d_row, cell in ((0, -1, CELLS - 1), (WIDE, 1, 0)):
        ring[start : start + 1] = owner(d_row, -1, cell)
        ring[start + 1 : start + 1 + COLS] = jnp.broadcast_to(
            owner(d_row, 0, cell), (COLS, CHANNELS)
        )
        ring[start + 1 + COLS : start + WIDE] = owner(d_row, 1, cell)
    for start, d_col in ((2 * WIDE, -1), (2 * WIDE + ROWS, 1)):
        for cell in range(CELLS):
            at = start + cell * WIN_ROWS
            ring[at : at + WIN_ROWS] = jnp.broadcast_to(
                owner(0, d_col, cell), (WIN_ROWS, CHANNELS)
            )
    ring[USED:] = jnp.zeros((RING - USED, CHANNELS), jnp.float32)
    back = norm_back(d_normed[...] + ring[...], normed[COUNT:], inv[COUNT:])
    back = grad[COUNT:] + back
    at = lax.broadcasted_iota(jnp.int32, (RING, CHANNELS), 0)
    top, bottom = at < WIDE, (at >= WIDE) & (at < 2 * WIDE)
    left = ((at >= 2 * WIDE) & (at < 2 * WIDE + ROWS)) | (at == 0) | (at == WIDE)
    right = (at >= 2 * WIDE + ROWS) | (at == WIDE - 1) | (at == 2 * WIDE - 1)
    outside = (
        (top & (row == 0))
        | (bottom & (row == row_count - 1))
        | (left & (col == 0))
        | (right & (col == col_count - 1))
    )
    ring[...] = jnp.where(outside, 0.0, back)
    padded[0, 0:WIDE] = ring[0:WIDE]
    padded[ROWS + 1, 0:WIDE] = ring[WIDE : 2 * WIDE]
    for r in range(ROWS):
        k = 2 * WIDE + r
        padded[1 + r, 0:1] = ring[k : k + 1]
        padded[1 + r, WIDE - 1 : WIDE] = ring[k + ROWS : k + ROWS + 1]
    padded[1 : 1 + ROWS, 1 : 1 + COLS] = d_mixed[...]
    total = d_mixed[...]
    for i in range(3):
        for j in range(3):
            total = (
                total
                + weight[3 * i + j : 3 * i + j + 1][None]
                * padded[2 - i : 2 - i + ROWS, 2 - j : 2 - j + COLS]
            )
    d_tokens[...] = total
    output[...] = mixed[...] + att[...].reshape(ROWS, COLS, CHANNELS)
    root = float(COUNT * row_count * col_count) ** (-0.5)
    conv = near[0, 0, row_count:first]
    for k in range(1, cores * lines):
        conv = conv + near[k // lines, k % lines, row_count:first]
    conv = conv * root
    for k in range(9):
        g_conv[k // 3, k % 3 : k % 3 + 1] = conv[k : k + 1]
    blocks = ((g_query, root), (g_key, 1.0 / POOL), (g_value, 1.0 / POOL), (g_out, root))
    for k in range(cores * lines):
        line = k % lines
        place_of = k - line + line % (lines // 2) * 2 + line // (lines // 2)
        out, factor = blocks[place_of * row_count // CHANNELS]
        at = place_of * row_count % CHANNELS
        out[at : at + row_count] = near[k // lines, k % lines, 0:row_count] * factor


def body(tokens, cotangent, conv_weight, w_query, w_key, w_value, w_out):
    row_count, col_count = lax.axis_size(ROW), lax.axis_size(COL)
    chips, lines = lax.axis_size(CHIPS), lax.axis_size(CHIP_COL)
    core = lax.axis_index("c")
    tile = (ROWS, COLS, CHANNELS)
    square = (CHANNELS, CHANNELS)
    all_tokens = (COUNT + RING, CHANNELS)

    anywhere = pl.BlockSpec(memory_space=pl.ANY)
    mine, mates = pl.pallas_call(
        edge_kernel,
        out_shape=[f32(3, COLS, CHANNELS)] * 2,
        in_specs=[anywhere] * 2,
        out_specs=[pl.BlockSpec(memory_space=pltpu.VMEM)] * 2,
        scratch_shapes=[pltpu.SemaphoreType.DMA((4,))],
    )(tokens, cotangent)
    mates = pair_gather(mates, "c")
    (strips,) = call(both_kernel, [f32(2, 3, COLS, CHANNELS)], mine, mates)
    pairs = [[4 * k, 4 * k + 2] for k in range(row_count // 2)]
    pairs += [[2 * j + 1, 2 * k + 1] for j, k in seam(ROW)]
    strips = pair_gather(strips, ROW + ("c",), pairs)
    shared, taps = call(
        functools.partial(reach_kernel, row_count - 1),
        [f32(FACING + 3 * ROWS, CHANNELS), f32(9, CHANNELS)],
        tokens, cotangent, conv_weight, strips,
    )
    shared = pair_gather(shared, "c")
    above, below, beside, beyond = call(
        side_kernel,
        [f32(3, COLS, CHANNELS)] * 2 + [f32(SIDE, CHANNELS)] * 2,
        tokens, cotangent, shared,
    )
    beyond = pair_gather(beyond, COL, seam(COL))
    message, pooled, padded, mixed, normed, inv_std, grad = call(
        functools.partial(mix_kernel, col_count - 1),
        [
            f32(chips, CELLS, CHANNELS),
            f32(2 * CELLS, CHANNELS),
            f32(ROWS + 4, 24, CHANNELS),
            f32(*tile),
            f32(*all_tokens),
            f32(*all_tokens),
            f32(*all_tokens),
        ],
        tokens, cotangent, above, below, beside, beyond, taps,
        scratch=[(ROWS + 2, 24, CHANNELS)] * 3 + [(SIDE, CHANNELS)] * 2,
    )

    message = lax.all_to_all(message, CHIPS, 0, 0, tiled=True)
    keys = lax.all_gather(message, "c", axis=0, tiled=True).reshape(-1, CHANNELS)

    columns = HEADS * (COUNT + RING)
    prepared = call(
        before_kernel,
        [f32(CHANNELS, columns)] * 2 + [f32(*square)] * 4,
        normed, grad, w_query, w_key, w_value, w_out,
        flops=1 << 10,
    )
    own, mate, att_out, d_normed, d_ring = call(
        attend_kernel,
        [
            f32(chips, 3 * CHANNELS),
            f32(chips, 3 * CHANNELS),
            f32(*square),
            f32(*square),
            f32(RING, CHANNELS),
        ],
        keys, *prepared, w_query, w_key, w_value, w_out,
        flops=1 << 31,
    )

    received = lax.all_gather(mate, "c", axis=0)
    received = jnp.where(core == 0, received[1], received[0])
    sums = (own + received).reshape(chips, 1, 3 * CHANNELS)
    sums = jnp.sum(lax.all_to_all(sums, CHIPS, 0, 0, tiled=True), 0)
    d_mixed, message = call(
        middle_kernel,
        [f32(*tile), f32(row_count, 16, CHANNELS)],
        sums, pooled, d_normed, normed, inv_std, grad, padded,
        scratch=[(16, CHANNELS)],
    )
    message = lax.all_to_all(message, ROW_GROUP, 0, 0, tiled=True)
    (message,) = call(
        relay_kernel,
        [f32(lines, 32, CHANNELS)],
        message,
        scratch=[(32, CHANNELS)],
    )
    message = lax.all_to_all(message, CHIP_COL, 0, 0, tiled=True)
    near = lax.all_gather(message, "c", axis=0)
    return call(
        functools.partial(end_kernel, row_count, col_count),
        [f32(*tile)] * 2 + [f32(3, 3, CHANNELS)] + [f32(*square)] * 4,
        near, d_ring, normed, inv_std, grad, d_mixed, taps, mixed, att_out,
        scratch=[(RING, CHANNELS), (ROWS + 2, 24, CHANNELS)],
    )


def solution(mesh):
    fine = Mesh(mesh.devices.reshape(8, 2, 2, 8, 2), ("y", "xl", "xh", "z", "c"))
    tile = P(ROW, COL, None)
    return jax.shard_map(
        body,
        mesh=fine,
        in_specs=(tile, tile, P(), P(), P(), P(), P()),
        out_specs=(tile, tile, P(), P(), P(), P(), P()),
        check_vma=False,
    )
```

```python
import functools

import jax
import jax.numpy as jnp
from jax import lax
from jax.experimental import pallas as pl
from jax.experimental.pallas import tpu as pltpu
from jax.sharding import Mesh, PartitionSpec as P

HEADS = 2
POOL = 32
ROW = ("y", "xl")
COL = ("xh", "z", "c")
CHIP_COL = ("xh", "z")
ROW_GROUP = ("xl", "y")
CHIPS = ("z", "xh") + ROW_GROUP
ROWS, COLS, CHANNELS = 8, 16, 128
CELLS, WIN_ROWS = 2, 4
COUNT = ROWS * COLS
WIDE = COLS + 2
USED = 2 * WIDE + 2 * ROWS
RING = 64
SIDE = 40
FACING = 6 * COLS
WIDTH = CHANNELS // HEADS
SCALE = WIDTH ** (-0.5)
BOTH = ((1,), (1,))
FIRST = ((0,), (0,))


def product(left, right, dims=((1,), (0,)), precision=lax.Precision.HIGHEST):
    return lax.dot_general(
        left, right, (dims, ((), ())), precision=precision, preferred_element_type=jnp.float32
    )


def normalize(values_in):
    average = jnp.mean(values_in, -1, keepdims=True)
    centered = values_in - average
    inv_std = lax.rsqrt(jnp.mean(centered * centered, -1, keepdims=True) + 1e-06)
    return (centered * inv_std, inv_std)


def norm_back(gradient, normed, inv_std):
    return inv_std * (
        gradient
        - jnp.mean(gradient, -1, keepdims=True)
        - normed * jnp.mean(gradient * normed, -1, keepdims=True)
    )


def here():
    core = lax.axis_index("c")
    row = lax.axis_index("y") * lax.axis_size("xl") + lax.axis_index("xl")
    chip = lax.axis_index("xh") * lax.axis_size("z") + lax.axis_index("z")
    return row, chip * lax.axis_size("c") + core, core


def f32(*shape):
    return jax.ShapeDtypeStruct(shape, jnp.float32)


def call(kernel, outs, *args, scratch=(), flops=1 << 20):
    in_vmem = pl.BlockSpec(memory_space=pltpu.VMEM)
    return pl.pallas_call(
        kernel,
        out_shape=outs,
        in_specs=[in_vmem] * len(args),
        out_specs=[in_vmem] * len(outs),
        scratch_shapes=[pltpu.VMEM(shape, jnp.float32) for shape in scratch],
        compiler_params=pltpu.CompilerParams(vmem_limit_bytes=48 << 20),
        cost_estimate=pl.CostEstimate(flops=flops, bytes_accessed=flops, transcendentals=0),
    )(*args)


def seam(axis):
    peers = lax.axis_size(axis)
    return [[k, (k + 1) % peers] for k in range(1, peers, 2)]


def column_seam():
    rows, columns = lax.axis_size(ROW), lax.axis_size(COL)
    pairs = []
    for row in range(rows):
        at = row * columns
        pairs += [[at + k, at + k + 1] for k in range(1, columns - 1, 2)]
        if row % 2 == 0:
            pairs += [[k, k + columns] for k in (at, at + columns - 1)]
    return pairs


def pair_gather(value, axis, groups=None):
    return lax.all_gather(value, axis, axis_index_groups=groups, axis=0)


def edge_kernel(tokens, grad, mine, mates, sems):
    odd, core = lax.axis_index("xl"), lax.axis_index("c")
    copies = []
    for out, last in ((mine, (1 - odd + core) % 2), (mates, (odd + core) % 2)):
        copies += [
            (tokens.at[pl.ds(last * (ROWS - 2), 2)], out.at[0:2]),
            (grad.at[pl.ds(last * (ROWS - 1), 1)], out.at[2:3]),
        ]
    copies = [pltpu.make_async_copy(*copy, sems.at[k]) for k, copy in enumerate(copies)]
    for copy in copies:
        copy.start()
    for copy in copies:
        copy.wait()


def both_kernel(mine, shared, strips):
    core = here()[2]
    for tile in range(2):
        strips[tile] = jnp.where(core == tile, mine[...], shared[tile])


def reach_kernel(last_row, tokens, grad, weight, strips, message, taps):
    row, _, core = here()
    odd = row % 2
    partner = jnp.where(core == 0, 1 - odd, odd)
    outside = (core == 1) & ((row == 0) | (row == last_row))
    for tile in range(2):
        for r in range(3):
            at = (3 * tile + r) * COLS
            message[at : at + COLS] = jnp.where(outside, 0.0, strips[partner, tile, r])
    for k in range(9):
        taps[k : k + 1] = weight[k // 3, k % 3 : k % 3 + 1]
    right = 1 - core
    for r in range(ROWS):
        for k in range(2):
            message[FACING + k * ROWS + r, :] = tokens[r, right * (COLS - 2) + k]
        message[FACING + 2 * ROWS + r, :] = grad[r, right * (COLS - 1)]


def side_kernel(tokens, grad, shared, above, below, beside, beyond):
    row, _, core = here()
    odd, mate = row % 2, 1 - core
    for r in range(3):
        at = pl.multiple_of((3 * core + r) * COLS, COLS)
        above[r] = shared[1 - odd, pl.ds(at, COLS)]
        below[r] = shared[odd, pl.ds(at, COLS)]
    tall = ROWS + 4
    right = core
    for k in range(2):
        at = right * (COLS - 2) + k
        for r in range(2):
            line = (3 * mate + r) * COLS + at
            beside[k * tall + r, :] = shared[1 - odd, line]
            beside[k * tall + ROWS + 2 + r, :] = shared[odd, line]
            beyond[k * tall + r, :] = above[r, at]
            beyond[k * tall + ROWS + 2 + r, :] = below[r, at]
        for r in range(ROWS):
            beyond[k * tall + 2 + r, :] = tokens[r, at]
        faced = FACING + k * ROWS
        beside[k * tall + 2 : k * tall + 2 + ROWS] = shared[mate, faced : faced + ROWS]
    at = right * (COLS - 1)
    line = (3 * mate + 2) * COLS + at
    beside[2 * tall, :] = shared[1 - odd, line]
    beside[2 * tall + ROWS + 1, :] = shared[odd, line]
    beyond[2 * tall, :] = above[2, at]
    beyond[2 * tall + ROWS + 1, :] = below[2, at]
    faced = FACING + 2 * ROWS
    beside[2 * tall + 1 : 2 * tall + 1 + ROWS] = shared[mate, faced : faced + ROWS]
    for r in range(ROWS):
        beyond[2 * tall + 1 + r, :] = grad[r, at]
    for out in (beside, beyond):
        out[SIDE - 6 :, :] = jnp.zeros((6, CHANNELS), jnp.float32)


def mix_kernel(
    last_col, tokens, grad, above, below, beside, beyond, weight,
    message, pooled_out, padded, mixed_out, normed_out, inv_out, grad_out,
    normed_ext, inv_ext, mixed_ext, before, after,
):
    col = here()[1]
    even = col % 2 == 0
    before[...] = jnp.where(even, jnp.where(col == 0, 0.0, beyond[0]), beside[...])
    after[...] = jnp.where(even, beside[...], jnp.where(col == last_col, 0.0, beyond[1]))
    padded[2 : 2 + ROWS, 2 : 2 + COLS] = tokens[...]
    padded[0:2, 2 : 2 + COLS] = above[0:2]
    padded[2 + ROWS : 4 + ROWS, 2 : 2 + COLS] = below[0:2]
    tall = ROWS + 4
    for r in range(tall):
        for k in range(2):
            at = k * tall + r
            padded[r, k : k + 1] = before[at : at + 1]
            padded[r, 2 + COLS + k : 3 + COLS + k] = after[at : at + 1]
    mixed = padded[1 : ROWS + 3, 1 : 1 + WIDE]
    for i in range(3):
        for j in range(3):
            mixed = mixed + weight[3 * i + j : 3 * i + j + 1][None] * padded[i : i + ROWS + 2, j : j + WIDE]
    normed, inv_std = normalize(mixed)
    mixed_ext[:, 0:WIDE] = mixed
    normed_ext[:, 0:WIDE] = normed
    inv_ext[:, 0:WIDE] = jnp.broadcast_to(inv_std, normed.shape)
    inner = normed_ext[1 : 1 + ROWS, 1 : 1 + COLS]
    for cell in range(CELLS):
        window = jnp.sum(inner[cell * WIN_ROWS : (cell + 1) * WIN_ROWS], 0)
        pooled = jnp.sum(window, 0, keepdims=True) * (1.0 / (WIN_ROWS * COLS))
        pooled_n, pooled_inv = normalize(pooled)
        pooled_out[cell : cell + 1] = pooled_n
        pooled_out[CELLS + cell : CELLS + cell + 1] = jnp.broadcast_to(pooled_inv, pooled_n.shape)
    message[...] = jnp.broadcast_to(pooled_out[0:CELLS][None], message.shape)
    mixed_out[...] = mixed_ext[1 : 1 + ROWS, 1 : 1 + COLS]
    for ext, out in ((normed_ext, normed_out), (inv_ext, inv_out)):
        out[0:COUNT] = ext[1 : 1 + ROWS, 1 : 1 + COLS].reshape(COUNT, CHANNELS)
        out[COUNT : COUNT + WIDE] = ext[0, 0:WIDE]
        out[COUNT + WIDE : COUNT + 2 * WIDE] = ext[ROWS + 1, 0:WIDE]
        for r in range(ROWS):
            left = COUNT + 2 * WIDE + r
            out[left : left + 1] = ext[1 + r, 0:1]
            out[left + ROWS : left + ROWS + 1] = ext[1 + r, WIDE - 1 : WIDE]
        out[COUNT + USED :] = jnp.zeros((RING - USED, CHANNELS), jnp.float32)
    low = 2 * tall
    high = low + ROWS + 1
    grad_out[0:COUNT] = grad[...].reshape(COUNT, CHANNELS)
    for start, middle, at in ((COUNT, above, low), (COUNT + WIDE, below, high)):
        grad_out[start : start + 1] = before[at : at + 1]
        grad_out[start + 1 : start + 1 + COLS] = middle[2]
        grad_out[start + 1 + COLS : start + WIDE] = after[at : at + 1]
    left = COUNT + 2 * WIDE
    grad_out[left : left + ROWS] = before[low + 1 : high]
    grad_out[left + ROWS : left + 2 * ROWS] = after[low + 1 : high]
    grad_out[COUNT + USED :] = jnp.zeros((RING - USED, CHANNELS), jnp.float32)


def top_half():
    return lax.broadcasted_iota(jnp.int32, (CHANNELS, CHANNELS), 0) < WIDTH


def by_head(weight, value, ring, out):
    upper = top_half()
    for head, mask in enumerate((upper, ~upper)):
        at = head * COUNT
        out[:, at : at + COUNT] = product(weight, jnp.where(mask, value, 0.0))
    parts = [product(weight, jnp.where(mask[:, :RING], ring, 0.0)) for mask in (upper, ~upper)]
    out[:, HEADS * COUNT :] = jnp.concatenate(parts, 1)


def before_kernel(
    normed, grad, w_query, w_key, w_value, w_out,
    to_keys, to_values, query_t, d_att_t, normed_t, grad_t,
):
    normed_t[...], grad_t[...] = normed[0:COUNT].T, grad[0:COUNT].T
    query_t[...] = product(w_query[...], normed_t[...], FIRST)
    d_att_t[...] = product(w_out[...], grad_t[...])
    ring = product(w_query[...], normed[COUNT:].T, FIRST)
    by_head(w_key[...] * SCALE, query_t[...], ring, to_keys)
    ring = product(w_out[...], grad[COUNT:].T)
    by_head(w_value[...], d_att_t[...], ring, to_values)


def pieces(value, count):
    parts = []
    for _ in range(count - 1):
        parts.append(value.astype(jnp.bfloat16))
        value = value - parts[-1].astype(jnp.float32)
    return parts + [value.astype(jnp.bfloat16)]


def single(left, right, dims=((1,), (0,))):
    return product(left, right, dims, lax.Precision.DEFAULT)


def three(left, right, dims=((1,), (0,))):
    (left_high, left_low), (right_high, right_low) = pieces(left, 2), pieces(right, 2)
    (left_axis,), (right_axis,) = dims
    return single(
        jnp.concatenate([left_high, left_high, left_low], left_axis),
        jnp.concatenate([right_high, right_low, right_high], right_axis),
        dims,
    )


def attend_kernel(
    keys_ref, to_keys, to_values, query_t, d_att_t, normed_t, grad_t,
    w_query, w_key, w_value, w_out,
    own_out, mate_out, att_out, d_normed, d_ring,
):
    core = here()[2]
    own = core * (keys_ref.shape[0] // 2)
    mate = keys_ref.shape[0] // 2 - own
    quarter = keys_ref.shape[0] // 4
    keys = jnp.concatenate(
        [
            keys_ref[pl.ds(start, quarter, stride=2)]
            for start in (own, own + 1, mate, mate + 1)
        ]
    )
    wide = HEADS * COUNT
    k0, k1, k2 = pieces(keys, 3)
    q0, q1, q2 = pieces(to_keys[...], 3)
    v0, v1 = pieces(to_values[...], 2)
    scores = single(
        jnp.concatenate([k0, k0, k1, k0, k2, k1], 1), jnp.concatenate([q0, q1, q0, q2, q0, q1])
    )
    d_probs = single(jnp.concatenate([k0, k0, k1], 1), jnp.concatenate([v0, v1, v0]))
    weights = jnp.exp(scores - jnp.max(scores, 0, keepdims=True))
    probs = weights * (1.0 / jnp.sum(weights, 0, keepdims=True))
    t0, t1 = pieces(keys.T, 2)
    both_t = jnp.concatenate([t0, t1])

    def by_keys(high, low):
        twice = single(both_t, high)
        return twice[:CHANNELS] + (twice[CHANNELS:] + single(t0, low))

    d_scores = probs * (d_probs - jnp.sum(d_probs * probs, 0, keepdims=True))
    d0, d1 = pieces(d_scores, 2)
    d_query_keys = by_keys(d0, d1)
    p0, p1 = pieces(probs[:, :wide], 2)
    att_keys = by_keys(p0, p1)
    d0, d1 = d0[:, :wide], d1[:, :wide]
    large = jnp.concatenate([q0[:, :wide], v0[:, :wide]], 1)
    small = jnp.concatenate([q1[:, :wide], v1[:, :wide]], 1)
    twice = single(
        jnp.concatenate([d0, p0], 1), jnp.concatenate([large, small]), BOTH
    )
    sums = twice[:, :CHANNELS] + (
        twice[:, CHANNELS:] + single(jnp.concatenate([d1, p1], 1), large, BOTH)
    )
    upper = top_half()
    left = lax.broadcasted_iota(jnp.int32, (CHANNELS, CHANNELS), 1) < WIDTH

    def heads(first, second, mask=upper):
        return jnp.where(mask, first, second)

    def rows(value):
        return jnp.concatenate([value[:, :COUNT], value[:, COUNT:wide]])

    att = three(w_value[...], att_keys, FIRST)
    att_t = heads(att[:, :COUNT], att[:, COUNT:])
    d_query = three(w_key[...] * SCALE, d_query_keys, FIRST)
    dq_t = heads(d_query[:, :COUNT], d_query[:, COUNT:wide])
    ring = d_query[:, wide:]
    ring = jnp.where(upper[:, :RING], ring[:, :RING], ring[:, RING:])
    g_query = three(normed_t[...], dq_t, BOTH)
    g_out = three(att_t, grad_t[...], BOTH)
    g_key = three(rows(d_query_keys), query_t[...], BOTH)
    g_key = heads(g_key[:CHANNELS], g_key[CHANNELS:], left) * SCALE
    g_value = three(rows(att_keys), d_att_t[...], BOTH)
    g_value = heads(g_value[:CHANNELS], g_value[CHANNELS:], left)
    att_out[...] = three(att_t, w_out[...], FIRST)
    back = w_query[...].T
    d_normed[...] = three(dq_t, back, FIRST)
    d_ring[...] = three(ring, back, FIRST)
    first = core == 0
    by_core = ((g_query, g_key), (g_value, g_out))
    for half in range(2):
        at = half * CHANNELS
        zero, one = by_core[0][half], by_core[1][half]
        own_out[at : at + CHANNELS, 2 * CHANNELS :] = jnp.where(first, zero, one)
        mate_out[at : at + CHANNELS, 2 * CHANNELS :] = jnp.where(first, one, zero)
    own_out[:, :CHANNELS] = sums[:quarter]
    own_out[:, CHANNELS : 2 * CHANNELS] = sums[quarter : 2 * quarter]
    mate_out[:, :CHANNELS] = sums[2 * quarter : 3 * quarter]
    mate_out[:, CHANNELS : 2 * CHANNELS] = sums[3 * quarter :]


def middle_kernel(sums, pooled, d_normed, normed, inv, grad, padded, d_mixed_out, message, share):
    window = float(WIN_ROWS * COLS)
    share[...] = jnp.zeros(share.shape, jnp.float32)
    half = WIN_ROWS * COLS
    for cell in range(CELLS):
        part = slice(cell * CHANNELS, (cell + 1) * CHANNELS)
        d_pooled = norm_back(
            sums[:, part], pooled[cell : cell + 1], pooled[CELLS + cell : CELLS + cell + 1]
        )
        d_pooled = d_pooled * (1.0 / window)
        share[cell : cell + 1] = d_pooled
        rows = slice(cell * half, (cell + 1) * half)
        back = norm_back(d_normed[rows] + d_pooled, normed[rows], inv[rows])
        back = grad[rows] + back
        d_mixed_out[cell * WIN_ROWS : (cell + 1) * WIN_ROWS] = back.reshape(
            WIN_ROWS, COLS, CHANNELS
        )
    share[CELLS : CELLS + 1] = sums[:, CELLS * CHANNELS :]
    d_mixed = d_mixed_out[...]
    for i in range(3):
        for j in range(3):
            products = padded[1 + i : 1 + i + ROWS, 1 + j : 1 + j + COLS] * d_mixed
            at = CELLS + 1 + 3 * i + j
            share[at : at + 1] = jnp.sum(jnp.sum(products, 0), 0, keepdims=True)
    message[...] = jnp.broadcast_to(share[...][None], message.shape)


def relay_kernel(received, message, share):
    peers = received.shape[0]
    row = here()[0]
    for k in range(peers):
        share[k : k + 1] = received[k, CELLS : CELLS + 1]
    total = received[0]
    for k in range(1, peers):
        total = total + received[k]
    share[peers : peers + 9] = total[CELLS + 1 : CELLS + 10]
    for d in range(3):
        at = peers + 9 + d * CELLS
        near = jnp.clip(row + d - 1, 0, peers - 1)
        share[at : at + CELLS] = received[near % 2 * (peers // 2) + near // 2, 0:CELLS]
    share[31:32] = jnp.zeros((1, CHANNELS), jnp.float32)
    message[...] = jnp.broadcast_to(share[...][None], message.shape)


def end_kernel(
    row_count, col_count, near, d_normed, normed, inv, grad, d_mixed, weight, mixed, att,
    output, d_tokens, g_conv, g_query, g_key, g_value, g_out,
    ring, padded,
):
    row, col, _ = here()
    cores, lines = near.shape[0], near.shape[1]
    first = row_count + 9

    def owner(d_row, d_col, cell):
        k = jnp.clip(col + d_col, 0, col_count - 1)
        at = first + (d_row + 1) * CELLS + cell
        return near[k % 2, k // 2, at : at + 1]

    for start, d_row, cell in ((0, -1, CELLS - 1), (WIDE, 1, 0)):
        ring[start : start + 1] = owner(d_row, -1, cell)
        ring[start + 1 : start + 1 + COLS] = jnp.broadcast_to(
            owner(d_row, 0, cell), (COLS, CHANNELS)
        )
        ring[start + 1 + COLS : start + WIDE] = owner(d_row, 1, cell)
    for start, d_col in ((2 * WIDE, -1), (2 * WIDE + ROWS, 1)):
        for cell in range(CELLS):
            at = start + cell * WIN_ROWS
            ring[at : at + WIN_ROWS] = jnp.broadcast_to(
                owner(0, d_col, cell), (WIN_ROWS, CHANNELS)
            )
    ring[USED:] = jnp.zeros((RING - USED, CHANNELS), jnp.float32)
    back = norm_back(d_normed[...] + ring[...], normed[COUNT:], inv[COUNT:])
    back = grad[COUNT:] + back
    at = lax.broadcasted_iota(jnp.int32, (RING, CHANNELS), 0)
    top, bottom = at < WIDE, (at >= WIDE) & (at < 2 * WIDE)
    left = ((at >= 2 * WIDE) & (at < 2 * WIDE + ROWS)) | (at == 0) | (at == WIDE)
    right = (at >= 2 * WIDE + ROWS) | (at == WIDE - 1) | (at == 2 * WIDE - 1)
    outside = (
        (top & (row == 0))
        | (bottom & (row == row_count - 1))
        | (left & (col == 0))
        | (right & (col == col_count - 1))
    )
    ring[...] = jnp.where(outside, 0.0, back)
    padded[0, 0:WIDE] = ring[0:WIDE]
    padded[ROWS + 1, 0:WIDE] = ring[WIDE : 2 * WIDE]
    for r in range(ROWS):
        k = 2 * WIDE + r
        padded[1 + r, 0:1] = ring[k : k + 1]
        padded[1 + r, WIDE - 1 : WIDE] = ring[k + ROWS : k + ROWS + 1]
    padded[1 : 1 + ROWS, 1 : 1 + COLS] = d_mixed[...]
    total = d_mixed[...]
    for i in range(3):
        for j in range(3):
            total = (
                total
                + weight[3 * i + j : 3 * i + j + 1][None]
                * padded[2 - i : 2 - i + ROWS, 2 - j : 2 - j + COLS]
            )
    d_tokens[...] = total
    output[...] = mixed[...] + att[...].reshape(ROWS, COLS, CHANNELS)
    root = float(COUNT * row_count * col_count) ** (-0.5)
    conv = near[0, 0, row_count:first]
    for k in range(1, cores * lines):
        conv = conv + near[k // lines, k % lines, row_count:first]
    conv = conv * root
    for k in range(9):
        g_conv[k // 3, k % 3 : k % 3 + 1] = conv[k : k + 1]
    blocks = ((g_query, root), (g_key, 1.0 / POOL), (g_value, 1.0 / POOL), (g_out, root))
    for k in range(cores * lines):
        line = k % lines
        place_of = k - line + line % (lines // 2) * 2 + line // (lines // 2)
        out, factor = blocks[place_of * row_count // CHANNELS]
        at = place_of * row_count % CHANNELS
        out[at : at + row_count] = near[k // lines, k % lines, 0:row_count] * factor


def body(tokens, cotangent, conv_weight, w_query, w_key, w_value, w_out):
    row_count, col_count = lax.axis_size(ROW), lax.axis_size(COL)
    chips, lines = lax.axis_size(CHIPS), lax.axis_size(CHIP_COL)
    core = lax.axis_index("c")
    tile = (ROWS, COLS, CHANNELS)
    square = (CHANNELS, CHANNELS)
    all_tokens = (COUNT + RING, CHANNELS)

    anywhere = pl.BlockSpec(memory_space=pl.ANY)
    mine, mates = pl.pallas_call(
        edge_kernel,
        out_shape=[f32(3, COLS, CHANNELS)] * 2,
        in_specs=[anywhere] * 2,
        out_specs=[pl.BlockSpec(memory_space=pltpu.VMEM)] * 2,
        scratch_shapes=[pltpu.SemaphoreType.DMA((4,))],
    )(tokens, cotangent)
    mates = pair_gather(mates, "c")
    (strips,) = call(both_kernel, [f32(2, 3, COLS, CHANNELS)], mine, mates)
    pairs = [[4 * k, 4 * k + 2] for k in range(row_count // 2)]
    pairs += [[2 * j + 1, 2 * k + 1] for j, k in seam(ROW)]
    strips = pair_gather(strips, ROW + ("c",), pairs)
    shared, taps = call(
        functools.partial(reach_kernel, row_count - 1),
        [f32(FACING + 3 * ROWS, CHANNELS), f32(9, CHANNELS)],
        tokens, cotangent, conv_weight, strips,
    )
    shared = pair_gather(shared, "c")
    above, below, beside, beyond = call(
        side_kernel,
        [f32(3, COLS, CHANNELS)] * 2 + [f32(SIDE, CHANNELS)] * 2,
        tokens, cotangent, shared,
    )
    beyond = pair_gather(beyond, ROW + COL, column_seam())
    message, pooled, padded, mixed, normed, inv_std, grad = call(
        functools.partial(mix_kernel, col_count - 1),
        [
            f32(chips, CELLS, CHANNELS),
            f32(2 * CELLS, CHANNELS),
            f32(ROWS + 4, 24, CHANNELS),
            f32(*tile),
            f32(*all_tokens),
            f32(*all_tokens),
            f32(*all_tokens),
        ],
        tokens, cotangent, above, below, beside, beyond, taps,
        scratch=[(ROWS + 2, 24, CHANNELS)] * 3 + [(SIDE, CHANNELS)] * 2,
    )

    message = lax.all_to_all(message, CHIPS, 0, 0, tiled=True)
    keys = lax.all_gather(message, "c", axis=0, tiled=True).reshape(-1, CHANNELS)

    columns = HEADS * (COUNT + RING)
    prepared = call(
        before_kernel,
        [f32(CHANNELS, columns)] * 2 + [f32(*square)] * 4,
        normed, grad, w_query, w_key, w_value, w_out,
        flops=1 << 10,
    )
    own, mate, att_out, d_normed, d_ring = call(
        attend_kernel,
        [
            f32(chips, 3 * CHANNELS),
            f32(chips, 3 * CHANNELS),
            f32(*square),
            f32(*square),
            f32(RING, CHANNELS),
        ],
        keys, *prepared, w_query, w_key, w_value, w_out,
        flops=1 << 31,
    )

    received = lax.all_gather(mate, "c", axis=0)
    received = jnp.where(core == 0, received[1], received[0])
    sums = (own + received).reshape(chips, 1, 3 * CHANNELS)
    sums = jnp.sum(lax.all_to_all(sums, CHIPS, 0, 0, tiled=True), 0)
    d_mixed, message = call(
        middle_kernel,
        [f32(*tile), f32(row_count, 16, CHANNELS)],
        sums, pooled, d_normed, normed, inv_std, grad, padded,
        scratch=[(16, CHANNELS)],
    )
    message = lax.all_to_all(message, ROW_GROUP, 0, 0, tiled=True)
    (message,) = call(
        relay_kernel,
        [f32(lines, 32, CHANNELS)],
        message,
        scratch=[(32, CHANNELS)],
    )
    message = lax.all_to_all(message, CHIP_COL, 0, 0, tiled=True)
    near = lax.all_gather(message, "c", axis=0)
    return call(
        functools.partial(end_kernel, row_count, col_count),
        [f32(*tile)] * 2 + [f32(3, 3, CHANNELS)] + [f32(*square)] * 4,
        near, d_ring, normed, inv_std, grad, d_mixed, taps, mixed, att_out,
        scratch=[(RING, CHANNELS), (ROWS + 2, 24, CHANNELS)],
    )


def solution(mesh):
    fine = Mesh(mesh.devices.reshape(8, 2, 2, 8, 2), ("y", "xl", "xh", "z", "c"))
    tile = P(ROW, COL, None)
    return jax.shard_map(
        body,
        mesh=fine,
        in_specs=(tile, tile, P(), P(), P(), P(), P()),
        out_specs=(tile, tile, P(), P(), P(), P(), P()),
        check_vma=False,
    )
```

```python
import functools

import jax
import jax.numpy as jnp
from jax import lax
from jax.experimental import pallas as pl
from jax.experimental.pallas import tpu as pltpu
from jax.sharding import Mesh, PartitionSpec as P

HEADS = 2
POOL = 32
ROW = ("y", "xl")
COL = ("xh", "z", "c")
CHIP_COL = ("xh", "z")
ROW_GROUP = ("xl", "y")
CHIPS = ("z", "xh") + ROW_GROUP
ROWS, COLS, CHANNELS = 8, 16, 128
CELLS, WIN_ROWS = 2, 4
COUNT = ROWS * COLS
WIDE = COLS + 2
USED = 2 * WIDE + 2 * ROWS
RING = 64
SIDE = 40
FACING = 6 * COLS
WIDTH = CHANNELS // HEADS
SCALE = WIDTH ** (-0.5)
BOTH = ((1,), (1,))
FIRST = ((0,), (0,))


def product(left, right, dims=((1,), (0,)), precision=lax.Precision.HIGHEST):
    return lax.dot_general(
        left, right, (dims, ((), ())), precision=precision, preferred_element_type=jnp.float32
    )


def normalize(values_in):
    average = jnp.mean(values_in, -1, keepdims=True)
    centered = values_in - average
    inv_std = lax.rsqrt(jnp.mean(centered * centered, -1, keepdims=True) + 1e-06)
    return (centered * inv_std, inv_std)


def norm_back(gradient, normed, inv_std):
    return inv_std * (
        gradient
        - jnp.mean(gradient, -1, keepdims=True)
        - normed * jnp.mean(gradient * normed, -1, keepdims=True)
    )


def here():
    core = lax.axis_index("c")
    row = lax.axis_index("y") * lax.axis_size("xl") + lax.axis_index("xl")
    chip = lax.axis_index("xh") * lax.axis_size("z") + lax.axis_index("z")
    return row, chip * lax.axis_size("c") + core, core


def f32(*shape):
    return jax.ShapeDtypeStruct(shape, jnp.float32)


def call(kernel, outs, *args, scratch=(), flops=1 << 20):
    in_vmem = pl.BlockSpec(memory_space=pltpu.VMEM)
    return pl.pallas_call(
        kernel,
        out_shape=outs,
        in_specs=[in_vmem] * len(args),
        out_specs=[in_vmem] * len(outs),
        scratch_shapes=[pltpu.VMEM(shape, jnp.float32) for shape in scratch],
        compiler_params=pltpu.CompilerParams(vmem_limit_bytes=48 << 20),
        cost_estimate=pl.CostEstimate(flops=flops, bytes_accessed=flops, transcendentals=0),
    )(*args)


def seam(axis):
    peers = lax.axis_size(axis)
    return [[k, (k + 1) % peers] for k in range(1, peers, 2)]


def column_seam():
    rows, columns = lax.axis_size(ROW), lax.axis_size(COL)
    pairs = []
    for row in range(rows):
        at = row * columns
        pairs += [[at + k, at + k + 1] for k in range(1, columns - 1, 2)]
        if row % 2 == 0:
            pairs += [[k, k + columns] for k in (at, at + columns - 1)]
    return pairs


def pair_gather(value, axis, groups=None):
    return lax.all_gather(value, axis, axis_index_groups=groups, axis=0)


def edge_kernel(tokens, grad, mine, mates, sems):
    odd, core = lax.axis_index("xl"), lax.axis_index("c")
    copies = []
    for out, last in ((mine, (1 - odd + core) % 2), (mates, (odd + core) % 2)):
        copies += [
            (tokens.at[pl.ds(last * (ROWS - 2), 2)], out.at[0:2]),
            (grad.at[pl.ds(last * (ROWS - 1), 1)], out.at[2:3]),
        ]
    copies = [pltpu.make_async_copy(*copy, sems.at[k]) for k, copy in enumerate(copies)]
    for copy in copies:
        copy.start()
    for copy in copies:
        copy.wait()


def both_kernel(mine, shared, strips):
    core = here()[2]
    for tile in range(2):
        strips[tile] = jnp.where(core == tile, mine[...], shared[tile])


def reach_kernel(last_row, tokens, grad, weight, strips, message, taps):
    row, _, core = here()
    odd = row % 2
    partner = jnp.where(core == 0, 1 - odd, odd)
    outside = (core == 1) & ((row == 0) | (row == last_row))
    for tile in range(2):
        for r in range(3):
            at = (3 * tile + r) * COLS
            message[at : at + COLS] = jnp.where(outside, 0.0, strips[partner, tile, r])
    for k in range(9):
        taps[k : k + 1] = weight[k // 3, k % 3 : k % 3 + 1]
    right = 1 - core
    for r in range(ROWS):
        for k in range(2):
            message[FACING + k * ROWS + r, :] = tokens[r, right * (COLS - 2) + k]
        message[FACING + 2 * ROWS + r, :] = grad[r, right * (COLS - 1)]


def side_kernel(tokens, grad, shared, above, below, beside, beyond):
    row, _, core = here()
    odd, mate = row % 2, 1 - core
    for r in range(3):
        at = pl.multiple_of((3 * core + r) * COLS, COLS)
        above[r] = shared[1 - odd, pl.ds(at, COLS)]
        below[r] = shared[odd, pl.ds(at, COLS)]
    tall = ROWS + 4
    right = core
    for k in range(2):
        at = right * (COLS - 2) + k
        for r in range(2):
            line = (3 * mate + r) * COLS + at
            beside[k * tall + r, :] = shared[1 - odd, line]
            beside[k * tall + ROWS + 2 + r, :] = shared[odd, line]
            beyond[k * tall + r, :] = above[r, at]
            beyond[k * tall + ROWS + 2 + r, :] = below[r, at]
        for r in range(ROWS):
            beyond[k * tall + 2 + r, :] = tokens[r, at]
        faced = FACING + k * ROWS
        beside[k * tall + 2 : k * tall + 2 + ROWS] = shared[mate, faced : faced + ROWS]
    at = right * (COLS - 1)
    line = (3 * mate + 2) * COLS + at
    beside[2 * tall, :] = shared[1 - odd, line]
    beside[2 * tall + ROWS + 1, :] = shared[odd, line]
    beyond[2 * tall, :] = above[2, at]
    beyond[2 * tall + ROWS + 1, :] = below[2, at]
    faced = FACING + 2 * ROWS
    beside[2 * tall + 1 : 2 * tall + 1 + ROWS] = shared[mate, faced : faced + ROWS]
    for r in range(ROWS):
        beyond[2 * tall + 1 + r, :] = grad[r, at]
    for out in (beside, beyond):
        out[SIDE - 6 :, :] = jnp.zeros((6, CHANNELS), jnp.float32)


def mix_kernel(
    last_col, tokens, grad, above, below, beside, beyond, weight,
    message, pooled_out, padded, mixed_out, normed_out, inv_out, grad_out,
    normed_ext, inv_ext, mixed_ext, before, after, rows,
):
    col = here()[1]
    even = col % 2 == 0
    before[...] = jnp.where(even, jnp.where(col == 0, 0.0, beyond[0]), beside[...])
    after[...] = jnp.where(even, beside[...], jnp.where(col == last_col, 0.0, beyond[1]))
    padded[2 : 2 + ROWS, 2 : 2 + COLS] = tokens[...]
    padded[0:2, 2 : 2 + COLS] = above[0:2]
    padded[2 + ROWS : 4 + ROWS, 2 : 2 + COLS] = below[0:2]
    tall = ROWS + 4
    for r in range(tall):
        for k in range(2):
            at = k * tall + r
            padded[r, k : k + 1] = before[at : at + 1]
            padded[r, 2 + COLS + k : 3 + COLS + k] = after[at : at + 1]
    mixed = padded[1 : ROWS + 3, 1 : 1 + WIDE]
    for i in range(3):
        for j in range(3):
            mixed = mixed + weight[3 * i + j : 3 * i + j + 1][None] * padded[i : i + ROWS + 2, j : j + WIDE]
    normed, inv_std = normalize(mixed)
    mixed_ext[:, 0:WIDE] = mixed
    normed_ext[:, 0:WIDE] = normed
    inv_ext[:, 0:WIDE] = jnp.broadcast_to(inv_std, normed.shape)
    inner = normed_ext[1 : 1 + ROWS, 1 : 1 + COLS]
    for cell in range(CELLS):
        window = jnp.sum(inner[cell * WIN_ROWS : (cell + 1) * WIN_ROWS], 0)
        pooled = jnp.sum(window, 0, keepdims=True) * (1.0 / (WIN_ROWS * COLS))
        pooled_n, pooled_inv = normalize(pooled)
        pooled_out[cell : cell + 1] = pooled_n
        pooled_out[CELLS + cell : CELLS + cell + 1] = jnp.broadcast_to(pooled_inv, pooled_n.shape)
    for k in range(8):
        rows[k : k + 1] = pooled_out[k % CELLS : k % CELLS + 1]
    tiles = jnp.broadcast_to(rows[...][None], (message.shape[0] // 8, 8, CHANNELS))
    message[...] = tiles.reshape(message.shape)
    mixed_out[...] = mixed_ext[1 : 1 + ROWS, 1 : 1 + COLS]
    for ext, out in ((normed_ext, normed_out), (inv_ext, inv_out)):
        out[0:COUNT] = ext[1 : 1 + ROWS, 1 : 1 + COLS].reshape(COUNT, CHANNELS)
        out[COUNT : COUNT + WIDE] = ext[0, 0:WIDE]
        out[COUNT + WIDE : COUNT + 2 * WIDE] = ext[ROWS + 1, 0:WIDE]
        for r in range(ROWS):
            left = COUNT + 2 * WIDE + r
            out[left : left + 1] = ext[1 + r, 0:1]
            out[left + ROWS : left + ROWS + 1] = ext[1 + r, WIDE - 1 : WIDE]
        out[COUNT + USED :] = jnp.zeros((RING - USED, CHANNELS), jnp.float32)
    low = 2 * tall
    high = low + ROWS + 1
    grad_out[0:COUNT] = grad[...].reshape(COUNT, CHANNELS)
    for start, middle, at in ((COUNT, above, low), (COUNT + WIDE, below, high)):
        grad_out[start : start + 1] = before[at : at + 1]
        grad_out[start + 1 : start + 1 + COLS] = middle[2]
        grad_out[start + 1 + COLS : start + WIDE] = after[at : at + 1]
    left = COUNT + 2 * WIDE
    grad_out[left : left + ROWS] = before[low + 1 : high]
    grad_out[left + ROWS : left + 2 * ROWS] = after[low + 1 : high]
    grad_out[COUNT + USED :] = jnp.zeros((RING - USED, CHANNELS), jnp.float32)


def top_half():
    return lax.broadcasted_iota(jnp.int32, (CHANNELS, CHANNELS), 0) < WIDTH


def by_head(weight, value, ring, out):
    upper = top_half()
    for head, mask in enumerate((upper, ~upper)):
        at = head * COUNT
        out[:, at : at + COUNT] = product(weight, jnp.where(mask, value, 0.0))
    parts = [product(weight, jnp.where(mask[:, :RING], ring, 0.0)) for mask in (upper, ~upper)]
    out[:, HEADS * COUNT :] = jnp.concatenate(parts, 1)


def before_kernel(
    normed, grad, w_query, w_key, w_value, w_out,
    to_keys, to_values, query_t, d_att_t, normed_t, grad_t,
):
    normed_t[...], grad_t[...] = normed[0:COUNT].T, grad[0:COUNT].T
    query_t[...] = product(w_query[...], normed_t[...], FIRST)
    d_att_t[...] = product(w_out[...], grad_t[...])
    ring = product(w_query[...], normed[COUNT:].T, FIRST)
    by_head(w_key[...] * SCALE, query_t[...], ring, to_keys)
    ring = product(w_out[...], grad[COUNT:].T)
    by_head(w_value[...], d_att_t[...], ring, to_values)


def pieces(value, count):
    parts = []
    for _ in range(count - 1):
        parts.append(value.astype(jnp.bfloat16))
        value = value - parts[-1].astype(jnp.float32)
    return parts + [value.astype(jnp.bfloat16)]


def single(left, right, dims=((1,), (0,))):
    return product(left, right, dims, lax.Precision.DEFAULT)


def three(left, right, dims=((1,), (0,))):
    (left_high, left_low), (right_high, right_low) = pieces(left, 2), pieces(right, 2)
    (left_axis,), (right_axis,) = dims
    return single(
        jnp.concatenate([left_high, left_high, left_low], left_axis),
        jnp.concatenate([right_high, right_low, right_high], right_axis),
        dims,
    )


def attend_kernel(
    keys_ref, to_keys, to_values, query_t, d_att_t, normed_t, grad_t,
    w_query, w_key, w_value, w_out,
    own_out, mate_out, att_out, d_normed, d_ring,
):
    core = here()[2]
    own = core * (keys_ref.shape[0] // 2)
    mate = keys_ref.shape[0] // 2 - own
    quarter = keys_ref.shape[0] // 4
    keys = jnp.concatenate(
        [
            keys_ref[pl.ds(start, quarter, stride=2)]
            for start in (own, own + 1, mate, mate + 1)
        ]
    )
    wide = HEADS * COUNT
    k0, k1, k2 = pieces(keys, 3)
    q0, q1, q2 = pieces(to_keys[...], 3)
    v0, v1 = pieces(to_values[...], 2)
    scores = single(
        jnp.concatenate([k0, k0, k1, k0, k2, k1], 1), jnp.concatenate([q0, q1, q0, q2, q0, q1])
    )
    d_probs = single(jnp.concatenate([k0, k0, k1], 1), jnp.concatenate([v0, v1, v0]))
    weights = jnp.exp(scores - jnp.max(scores, 0, keepdims=True))
    probs = weights * (1.0 / jnp.sum(weights, 0, keepdims=True))
    t0, t1 = pieces(keys.T, 2)
    both_t = jnp.concatenate([t0, t1])

    def by_keys(high, low):
        twice = single(both_t, high)
        return twice[:CHANNELS] + (twice[CHANNELS:] + single(t0, low))

    d_scores = probs * (d_probs - jnp.sum(d_probs * probs, 0, keepdims=True))
    d0, d1 = pieces(d_scores, 2)
    d_query_keys = by_keys(d0, d1)
    p0, p1 = pieces(probs[:, :wide], 2)
    att_keys = by_keys(p0, p1)
    d0, d1 = d0[:, :wide], d1[:, :wide]
    large = jnp.concatenate([q0[:, :wide], v0[:, :wide]], 1)
    small = jnp.concatenate([q1[:, :wide], v1[:, :wide]], 1)
    twice = single(
        jnp.concatenate([d0, p0], 1), jnp.concatenate([large, small]), BOTH
    )
    sums = twice[:, :CHANNELS] + (
        twice[:, CHANNELS:] + single(jnp.concatenate([d1, p1], 1), large, BOTH)
    )
    upper = top_half()
    left = lax.broadcasted_iota(jnp.int32, (CHANNELS, CHANNELS), 1) < WIDTH

    def heads(first, second, mask=upper):
        return jnp.where(mask, first, second)

    def rows(value):
        return jnp.concatenate([value[:, :COUNT], value[:, COUNT:wide]])

    att = three(w_value[...], att_keys, FIRST)
    att_t = heads(att[:, :COUNT], att[:, COUNT:])
    d_query = three(w_key[...] * SCALE, d_query_keys, FIRST)
    dq_t = heads(d_query[:, :COUNT], d_query[:, COUNT:wide])
    ring = d_query[:, wide:]
    ring = jnp.where(upper[:, :RING], ring[:, :RING], ring[:, RING:])
    g_query = three(normed_t[...], dq_t, BOTH)
    g_out = three(att_t, grad_t[...], BOTH)
    g_key = three(rows(d_query_keys), query_t[...], BOTH)
    g_key = heads(g_key[:CHANNELS], g_key[CHANNELS:], left) * SCALE
    g_value = three(rows(att_keys), d_att_t[...], BOTH)
    g_value = heads(g_value[:CHANNELS], g_value[CHANNELS:], left)
    att_out[...] = three(att_t, w_out[...], FIRST)
    back = w_query[...].T
    d_normed[...] = three(dq_t, back, FIRST)
    d_ring[...] = three(ring, back, FIRST)
    first = core == 0
    by_core = ((g_query, g_key), (g_value, g_out))
    for half in range(2):
        at = half * CHANNELS
        zero, one = by_core[0][half], by_core[1][half]
        own_out[at : at + CHANNELS, 2 * CHANNELS :] = jnp.where(first, zero, one)
        mate_out[at : at + CHANNELS, 2 * CHANNELS :] = jnp.where(first, one, zero)
    own_out[:, :CHANNELS] = sums[:quarter]
    own_out[:, CHANNELS : 2 * CHANNELS] = sums[quarter : 2 * quarter]
    mate_out[:, :CHANNELS] = sums[2 * quarter : 3 * quarter]
    mate_out[:, CHANNELS : 2 * CHANNELS] = sums[3 * quarter :]


def middle_kernel(sums, pooled, d_normed, normed, inv, grad, padded, d_mixed_out, message, share):
    window = float(WIN_ROWS * COLS)
    share[...] = jnp.zeros(share.shape, jnp.float32)
    half = WIN_ROWS * COLS
    for cell in range(CELLS):
        part = slice(cell * CHANNELS, (cell + 1) * CHANNELS)
        d_pooled = norm_back(
            sums[:, part], pooled[cell : cell + 1], pooled[CELLS + cell : CELLS + cell + 1]
        )
        d_pooled = d_pooled * (1.0 / window)
        share[cell : cell + 1] = d_pooled
        rows = slice(cell * half, (cell + 1) * half)
        back = norm_back(d_normed[rows] + d_pooled, normed[rows], inv[rows])
        back = grad[rows] + back
        d_mixed_out[cell * WIN_ROWS : (cell + 1) * WIN_ROWS] = back.reshape(
            WIN_ROWS, COLS, CHANNELS
        )
    share[CELLS : CELLS + 1] = sums[:, CELLS * CHANNELS :]
    d_mixed = d_mixed_out[...]
    for i in range(3):
        for j in range(3):
            products = padded[1 + i : 1 + i + ROWS, 1 + j : 1 + j + COLS] * d_mixed
            at = CELLS + 1 + 3 * i + j
            share[at : at + 1] = jnp.sum(jnp.sum(products, 0), 0, keepdims=True)
    message[...] = jnp.broadcast_to(share[...][None], message.shape)


def relay_kernel(received, message, share):
    peers = received.shape[0]
    row = here()[0]
    for k in range(peers):
        share[k : k + 1] = received[k, CELLS : CELLS + 1]
    total = received[0]
    for k in range(1, peers):
        total = total + received[k]
    share[peers : peers + 9] = total[CELLS + 1 : CELLS + 10]
    for d in range(3):
        at = peers + 9 + d * CELLS
        near = jnp.clip(row + d - 1, 0, peers - 1)
        share[at : at + CELLS] = received[near % 2 * (peers // 2) + near // 2, 0:CELLS]
    share[31:32] = jnp.zeros((1, CHANNELS), jnp.float32)
    message[...] = jnp.broadcast_to(share[...][None], message.shape)


def end_kernel(
    row_count, col_count, near, d_normed, normed, inv, grad, d_mixed, weight, mixed, att,
    output, d_tokens, g_conv, g_query, g_key, g_value, g_out,
    ring, padded,
):
    row, col, _ = here()
    cores, lines = near.shape[0], near.shape[1]
    first = row_count + 9

    def owner(d_row, d_col, cell):
        k = jnp.clip(col + d_col, 0, col_count - 1)
        at = first + (d_row + 1) * CELLS + cell
        return near[k % 2, k // 2, at : at + 1]

    for start, d_row, cell in ((0, -1, CELLS - 1), (WIDE, 1, 0)):
        ring[start : start + 1] = owner(d_row, -1, cell)
        ring[start + 1 : start + 1 + COLS] = jnp.broadcast_to(
            owner(d_row, 0, cell), (COLS, CHANNELS)
        )
        ring[start + 1 + COLS : start + WIDE] = owner(d_row, 1, cell)
    for start, d_col in ((2 * WIDE, -1), (2 * WIDE + ROWS, 1)):
        for cell in range(CELLS):
            at = start + cell * WIN_ROWS
            ring[at : at + WIN_ROWS] = jnp.broadcast_to(
                owner(0, d_col, cell), (WIN_ROWS, CHANNELS)
            )
    ring[USED:] = jnp.zeros((RING - USED, CHANNELS), jnp.float32)
    back = norm_back(d_normed[...] + ring[...], normed[COUNT:], inv[COUNT:])
    back = grad[COUNT:] + back
    at = lax.broadcasted_iota(jnp.int32, (RING, CHANNELS), 0)
    top, bottom = at < WIDE, (at >= WIDE) & (at < 2 * WIDE)
    left = ((at >= 2 * WIDE) & (at < 2 * WIDE + ROWS)) | (at == 0) | (at == WIDE)
    right = (at >= 2 * WIDE + ROWS) | (at == WIDE - 1) | (at == 2 * WIDE - 1)
    outside = (
        (top & (row == 0))
        | (bottom & (row == row_count - 1))
        | (left & (col == 0))
        | (right & (col == col_count - 1))
    )
    ring[...] = jnp.where(outside, 0.0, back)
    padded[0, 0:WIDE] = ring[0:WIDE]
    padded[ROWS + 1, 0:WIDE] = ring[WIDE : 2 * WIDE]
    for r in range(ROWS):
        k = 2 * WIDE + r
        padded[1 + r, 0:1] = ring[k : k + 1]
        padded[1 + r, WIDE - 1 : WIDE] = ring[k + ROWS : k + ROWS + 1]
    padded[1 : 1 + ROWS, 1 : 1 + COLS] = d_mixed[...]
    total = d_mixed[...]
    for i in range(3):
        for j in range(3):
            total = (
                total
                + weight[3 * i + j : 3 * i + j + 1][None]
                * padded[2 - i : 2 - i + ROWS, 2 - j : 2 - j + COLS]
            )
    d_tokens[...] = total
    output[...] = mixed[...] + att[...].reshape(ROWS, COLS, CHANNELS)
    root = float(COUNT * row_count * col_count) ** (-0.5)
    conv = near[0, 0, row_count:first]
    for k in range(1, cores * lines):
        conv = conv + near[k // lines, k % lines, row_count:first]
    conv = conv * root
    for k in range(9):
        g_conv[k // 3, k % 3 : k % 3 + 1] = conv[k : k + 1]
    blocks = ((g_query, root), (g_key, 1.0 / POOL), (g_value, 1.0 / POOL), (g_out, root))
    for k in range(cores * lines):
        line = k % lines
        place_of = k - line + line % (lines // 2) * 2 + line // (lines // 2)
        out, factor = blocks[place_of * row_count // CHANNELS]
        at = place_of * row_count % CHANNELS
        out[at : at + row_count] = near[k // lines, k % lines, 0:row_count] * factor


def body(tokens, cotangent, conv_weight, w_query, w_key, w_value, w_out):
    row_count, col_count = lax.axis_size(ROW), lax.axis_size(COL)
    chips, lines = lax.axis_size(CHIPS), lax.axis_size(CHIP_COL)
    core = lax.axis_index("c")
    tile = (ROWS, COLS, CHANNELS)
    square = (CHANNELS, CHANNELS)
    all_tokens = (COUNT + RING, CHANNELS)

    anywhere = pl.BlockSpec(memory_space=pl.ANY)
    mine, mates = pl.pallas_call(
        edge_kernel,
        out_shape=[pltpu.VMEM((3, COLS, CHANNELS), jnp.float32)] * 2,
        in_specs=[anywhere] * 2,
        out_specs=[pl.BlockSpec(memory_space=pltpu.VMEM)] * 2,
        scratch_shapes=[pltpu.SemaphoreType.DMA((4,))],
    )(tokens, cotangent)
    mates = pair_gather(mates, "c")
    (strips,) = call(both_kernel, [f32(2, 3, COLS, CHANNELS)], mine, mates)
    pairs = [[4 * k, 4 * k + 2] for k in range(row_count // 2)]
    pairs += [[2 * j + 1, 2 * k + 1] for j, k in seam(ROW)]
    strips = pair_gather(strips, ROW + ("c",), pairs)
    shared, taps = call(
        functools.partial(reach_kernel, row_count - 1),
        [f32(FACING + 3 * ROWS, CHANNELS), f32(9, CHANNELS)],
        tokens, cotangent, conv_weight, strips,
    )
    shared = pair_gather(shared, "c")
    above, below, beside, beyond = call(
        side_kernel,
        [f32(3, COLS, CHANNELS)] * 2 + [f32(SIDE, CHANNELS)] * 2,
        tokens, cotangent, shared,
    )
    beyond = pair_gather(beyond, ROW + COL, column_seam())
    message, pooled, padded, mixed, normed, inv_std, grad = call(
        functools.partial(mix_kernel, col_count - 1),
        [
            pltpu.VMEM((chips * CELLS, CHANNELS), jnp.float32),
            f32(2 * CELLS, CHANNELS),
            f32(ROWS + 4, 24, CHANNELS),
            f32(*tile),
            f32(*all_tokens),
            f32(*all_tokens),
            f32(*all_tokens),
        ],
        tokens, cotangent, above, below, beside, beyond, taps,
        scratch=[(ROWS + 2, 24, CHANNELS)] * 3 + [(SIDE, CHANNELS)] * 2 + [(8, CHANNELS)],
    )

    message = message.reshape(chips, CELLS, CHANNELS)
    message = lax.all_to_all(message, CHIPS, 0, 0, tiled=True)
    keys = lax.all_gather(message, "c", axis=0, tiled=True).reshape(-1, CHANNELS)

    columns = HEADS * (COUNT + RING)
    prepared = call(
        before_kernel,
        [f32(CHANNELS, columns)] * 2 + [f32(*square)] * 4,
        normed, grad, w_query, w_key, w_value, w_out,
        flops=1 << 10,
    )
    own, mate, att_out, d_normed, d_ring = call(
        attend_kernel,
        [
            f32(chips, 3 * CHANNELS),
            f32(chips, 3 * CHANNELS),
            f32(*square),
            f32(*square),
            f32(RING, CHANNELS),
        ],
        keys, *prepared, w_query, w_key, w_value, w_out,
        flops=1 << 31,
    )

    received = lax.all_gather(mate, "c", axis=0)
    received = jnp.where(core == 0, received[1], received[0])
    sums = (own + received).reshape(chips, 1, 3 * CHANNELS)
    sums = jnp.sum(lax.all_to_all(sums, CHIPS, 0, 0, tiled=True), 0)
    d_mixed, message = call(
        middle_kernel,
        [f32(*tile), f32(row_count, 16, CHANNELS)],
        sums, pooled, d_normed, normed, inv_std, grad, padded,
        scratch=[(16, CHANNELS)],
    )
    message = lax.all_to_all(message, ROW_GROUP, 0, 0, tiled=True)
    (message,) = call(
        relay_kernel,
        [f32(lines, 32, CHANNELS)],
        message,
        scratch=[(32, CHANNELS)],
    )
    message = lax.all_to_all(message, CHIP_COL, 0, 0, tiled=True)
    near = lax.all_gather(message, "c", axis=0)
    return call(
        functools.partial(end_kernel, row_count, col_count),
        [f32(*tile)] * 2 + [f32(3, 3, CHANNELS)] + [f32(*square)] * 4,
        near, d_ring, normed, inv_std, grad, d_mixed, taps, mixed, att_out,
        scratch=[(RING, CHANNELS), (ROWS + 2, 24, CHANNELS)],
    )


def solution(mesh):
    fine = Mesh(mesh.devices.reshape(8, 2, 2, 8, 2), ("y", "xl", "xh", "z", "c"))
    tile = P(ROW, COL, None)
    return jax.shard_map(
        body,
        mesh=fine,
        in_specs=(tile, tile, P(), P(), P(), P(), P()),
        out_specs=(tile, tile, P(), P(), P(), P(), P()),
        check_vma=False,
    )
```

```python
import functools

import jax
import jax.numpy as jnp
from jax import lax
from jax.experimental import pallas as pl
from jax.experimental.pallas import tpu as pltpu
from jax.sharding import Mesh, PartitionSpec as P

HEADS = 2
POOL = 32
ROW = ("y", "xl")
COL = ("xh", "z", "c")
CHIP_COL = ("xh", "z")
ROW_GROUP = ("xl", "y")
CHIPS = CHIP_COL + ROW_GROUP
ROWS, COLS, CHANNELS = 8, 16, 128
CELLS, WIN_ROWS = 2, 4
COUNT = ROWS * COLS
WIDE = COLS + 2
USED = 2 * WIDE + 2 * ROWS
RING = 64
SIDE = 40
FACING = 6 * COLS
WIDTH = CHANNELS // HEADS
SCALE = WIDTH ** (-0.5)
BOTH = ((1,), (1,))
FIRST = ((0,), (0,))


def product(left, right, dims=((1,), (0,)), precision=lax.Precision.HIGHEST):
    return lax.dot_general(
        left, right, (dims, ((), ())), precision=precision, preferred_element_type=jnp.float32
    )


def normalize(values_in):
    average = jnp.mean(values_in, -1, keepdims=True)
    centered = values_in - average
    inv_std = lax.rsqrt(jnp.mean(centered * centered, -1, keepdims=True) + 1e-06)
    return (centered * inv_std, inv_std)


def norm_back(gradient, normed, inv_std):
    return inv_std * (
        gradient
        - jnp.mean(gradient, -1, keepdims=True)
        - normed * jnp.mean(gradient * normed, -1, keepdims=True)
    )


def here():
    core = lax.axis_index("c")
    row = lax.axis_index("y") * lax.axis_size("xl") + lax.axis_index("xl")
    chip = lax.axis_index("xh") * lax.axis_size("z") + lax.axis_index("z")
    return row, chip * lax.axis_size("c") + core, core


def f32(*shape):
    return jax.ShapeDtypeStruct(shape, jnp.float32)


def call(kernel, outs, *args, scratch=(), flops=1 << 20, copied=0, sems=()):
    in_vmem = pl.BlockSpec(memory_space=pltpu.VMEM)
    return pl.pallas_call(
        kernel,
        out_shape=outs,
        in_specs=[in_vmem] * len(args),
        out_specs=[pl.BlockSpec(memory_space=pl.ANY)] * copied + [in_vmem] * (len(outs) - copied),
        scratch_shapes=[pltpu.VMEM(shape, jnp.float32) for shape in scratch] + list(sems),
        compiler_params=pltpu.CompilerParams(vmem_limit_bytes=48 << 20),
        cost_estimate=pl.CostEstimate(flops=flops, bytes_accessed=flops, transcendentals=0),
    )(*args)


def seam(axis):
    peers = lax.axis_size(axis)
    return [[k, (k + 1) % peers] for k in range(1, peers, 2)]


def column_seam():
    rows, columns = lax.axis_size(ROW), lax.axis_size(COL)
    pairs = []
    for row in range(rows):
        at = row * columns
        pairs += [[at + k, at + k + 1] for k in range(1, columns - 1, 2)]
        if row % 2 == 0:
            pairs += [[k, k + columns] for k in (at, at + columns - 1)]
    return pairs


def pair_gather(value, axis, groups=None):
    return lax.all_gather(value, axis, axis_index_groups=groups, axis=0)


def edge_kernel(tokens, grad, mine, mates, sems):
    odd, core = lax.axis_index("xl"), lax.axis_index("c")
    copies = []
    for out, last in ((mine, (1 - odd + core) % 2), (mates, (odd + core) % 2)):
        copies += [
            (tokens.at[pl.ds(last * (ROWS - 2), 2)], out.at[0:2]),
            (grad.at[pl.ds(last * (ROWS - 1), 1)], out.at[2:3]),
        ]
    copies = [pltpu.make_async_copy(*copy, sems.at[k]) for k, copy in enumerate(copies)]
    for copy in copies:
        copy.start()
    for copy in copies:
        copy.wait()


def both_kernel(mine, shared, strips):
    core = here()[2]
    for tile in range(2):
        strips[tile] = jnp.where(core == tile, mine[...], shared[tile])


def reach_kernel(last_row, tokens, grad, weight, strips, message, taps):
    row, _, core = here()
    odd = row % 2
    partner = jnp.where(core == 0, 1 - odd, odd)
    outside = (core == 1) & ((row == 0) | (row == last_row))
    for tile in range(2):
        for r in range(3):
            at = (3 * tile + r) * COLS
            message[at : at + COLS] = jnp.where(outside, 0.0, strips[partner, tile, r])
    for k in range(9):
        taps[k : k + 1] = weight[k // 3, k % 3 : k % 3 + 1]
    right = 1 - core
    for r in range(ROWS):
        for k in range(2):
            message[FACING + k * ROWS + r, :] = tokens[r, right * (COLS - 2) + k]
        message[FACING + 2 * ROWS + r, :] = grad[r, right * (COLS - 1)]


def side_kernel(tokens, grad, shared, above, below, beside, beyond):
    row, _, core = here()
    odd, mate = row % 2, 1 - core
    for r in range(3):
        at = pl.multiple_of((3 * core + r) * COLS, COLS)
        above[r] = shared[1 - odd, pl.ds(at, COLS)]
        below[r] = shared[odd, pl.ds(at, COLS)]
    tall = ROWS + 4
    right = core
    for k in range(2):
        at = right * (COLS - 2) + k
        for r in range(2):
            line = (3 * mate + r) * COLS + at
            beside[k * tall + r, :] = shared[1 - odd, line]
            beside[k * tall + ROWS + 2 + r, :] = shared[odd, line]
            beyond[k * tall + r, :] = above[r, at]
            beyond[k * tall + ROWS + 2 + r, :] = below[r, at]
        for r in range(ROWS):
            beyond[k * tall + 2 + r, :] = tokens[r, at]
        faced = FACING + k * ROWS
        beside[k * tall + 2 : k * tall + 2 + ROWS] = shared[mate, faced : faced + ROWS]
    at = right * (COLS - 1)
    line = (3 * mate + 2) * COLS + at
    beside[2 * tall, :] = shared[1 - odd, line]
    beside[2 * tall + ROWS + 1, :] = shared[odd, line]
    beyond[2 * tall, :] = above[2, at]
    beyond[2 * tall + ROWS + 1, :] = below[2, at]
    faced = FACING + 2 * ROWS
    beside[2 * tall + 1 : 2 * tall + 1 + ROWS] = shared[mate, faced : faced + ROWS]
    for r in range(ROWS):
        beyond[2 * tall + 1 + r, :] = grad[r, at]
    for out in (beside, beyond):
        out[SIDE - 6 :, :] = jnp.zeros((6, CHANNELS), jnp.float32)


def mix_kernel(
    last_col, tokens, grad, above, below, beside, beyond, weight,
    message, pooled_out, padded, mixed_out, normed_out, inv_out, grad_out,
    normed_ext, inv_ext, mixed_ext, before, after, rows, tiles, sem,
):
    col = here()[1]
    even = col % 2 == 0
    before[...] = jnp.where(even, jnp.where(col == 0, 0.0, beyond[0]), beside[...])
    after[...] = jnp.where(even, beside[...], jnp.where(col == last_col, 0.0, beyond[1]))
    padded[2 : 2 + ROWS, 2 : 2 + COLS] = tokens[...]
    padded[0:2, 2 : 2 + COLS] = above[0:2]
    padded[2 + ROWS : 4 + ROWS, 2 : 2 + COLS] = below[0:2]
    tall = ROWS + 4
    for r in range(tall):
        for k in range(2):
            at = k * tall + r
            padded[r, k : k + 1] = before[at : at + 1]
            padded[r, 2 + COLS + k : 3 + COLS + k] = after[at : at + 1]
    mixed = padded[1 : ROWS + 3, 1 : 1 + WIDE]
    for i in range(3):
        for j in range(3):
            mixed = mixed + weight[3 * i + j : 3 * i + j + 1][None] * padded[i : i + ROWS + 2, j : j + WIDE]
    normed, inv_std = normalize(mixed)
    mixed_ext[:, 0:WIDE] = mixed
    normed_ext[:, 0:WIDE] = normed
    inv_ext[:, 0:WIDE] = jnp.broadcast_to(inv_std, normed.shape)
    inner = normed_ext[1 : 1 + ROWS, 1 : 1 + COLS]
    for cell in range(CELLS):
        window = jnp.sum(inner[cell * WIN_ROWS : (cell + 1) * WIN_ROWS], 0)
        pooled = jnp.sum(window, 0, keepdims=True) * (1.0 / (WIN_ROWS * COLS))
        pooled_n, pooled_inv = normalize(pooled)
        pooled_out[cell : cell + 1] = pooled_n
        pooled_out[CELLS + cell : CELLS + cell + 1] = jnp.broadcast_to(pooled_inv, pooled_n.shape)
    for k in range(8):
        rows[k : k + 1] = pooled_out[k % CELLS : k % CELLS + 1]
    filled = jnp.broadcast_to(rows[...][None], (message.shape[0] // 8, 8, CHANNELS))
    tiles[...] = filled.reshape(message.shape)
    copy = pltpu.make_async_copy(tiles, message, sem)
    copy.start()
    mixed_out[...] = mixed_ext[1 : 1 + ROWS, 1 : 1 + COLS]
    for ext, out in ((normed_ext, normed_out), (inv_ext, inv_out)):
        out[0:COUNT] = ext[1 : 1 + ROWS, 1 : 1 + COLS].reshape(COUNT, CHANNELS)
        out[COUNT : COUNT + WIDE] = ext[0, 0:WIDE]
        out[COUNT + WIDE : COUNT + 2 * WIDE] = ext[ROWS + 1, 0:WIDE]
        for r in range(ROWS):
            left = COUNT + 2 * WIDE + r
            out[left : left + 1] = ext[1 + r, 0:1]
            out[left + ROWS : left + ROWS + 1] = ext[1 + r, WIDE - 1 : WIDE]
        out[COUNT + USED :] = jnp.zeros((RING - USED, CHANNELS), jnp.float32)
    low = 2 * tall
    high = low + ROWS + 1
    grad_out[0:COUNT] = grad[...].reshape(COUNT, CHANNELS)
    for start, middle, at in ((COUNT, above, low), (COUNT + WIDE, below, high)):
        grad_out[start : start + 1] = before[at : at + 1]
        grad_out[start + 1 : start + 1 + COLS] = middle[2]
        grad_out[start + 1 + COLS : start + WIDE] = after[at : at + 1]
    left = COUNT + 2 * WIDE
    grad_out[left : left + ROWS] = before[low + 1 : high]
    grad_out[left + ROWS : left + 2 * ROWS] = after[low + 1 : high]
    grad_out[COUNT + USED :] = jnp.zeros((RING - USED, CHANNELS), jnp.float32)
    copy.wait()


def top_half():
    return lax.broadcasted_iota(jnp.int32, (CHANNELS, CHANNELS), 0) < WIDTH


def by_head(weight, value, ring, out):
    upper = top_half()
    for head, mask in enumerate((upper, ~upper)):
        at = head * COUNT
        out[:, at : at + COUNT] = product(weight, jnp.where(mask, value, 0.0))
    parts = [product(weight, jnp.where(mask[:, :RING], ring, 0.0)) for mask in (upper, ~upper)]
    out[:, HEADS * COUNT :] = jnp.concatenate(parts, 1)


def before_kernel(
    normed, grad, w_query, w_key, w_value, w_out,
    to_keys, to_values, query_t, d_att_t, normed_t, grad_t,
):
    normed_t[...], grad_t[...] = normed[0:COUNT].T, grad[0:COUNT].T
    query_t[...] = product(w_query[...], normed_t[...], FIRST)
    d_att_t[...] = product(w_out[...], grad_t[...])
    ring = product(w_query[...], normed[COUNT:].T, FIRST)
    by_head(w_key[...] * SCALE, query_t[...], ring, to_keys)
    ring = product(w_out[...], grad[COUNT:].T)
    by_head(w_value[...], d_att_t[...], ring, to_values)


def pieces(value, count):
    parts = []
    for _ in range(count - 1):
        parts.append(value.astype(jnp.bfloat16))
        value = value - parts[-1].astype(jnp.float32)
    return parts + [value.astype(jnp.bfloat16)]


def single(left, right, dims=((1,), (0,))):
    return product(left, right, dims, lax.Precision.DEFAULT)


def three(left, right, dims=((1,), (0,))):
    (left_high, left_low), (right_high, right_low) = pieces(left, 2), pieces(right, 2)
    (left_axis,), (right_axis,) = dims
    return single(
        jnp.concatenate([left_high, left_high, left_low], left_axis),
        jnp.concatenate([right_high, right_low, right_high], right_axis),
        dims,
    )


def attend_kernel(
    keys_ref, to_keys, to_values, query_t, d_att_t, normed_t, grad_t,
    w_query, w_key, w_value, w_out,
    own_out, mate_out, att_out, d_normed, d_ring,
):
    core = here()[2]
    own = core * (keys_ref.shape[0] // 2)
    mate = keys_ref.shape[0] // 2 - own
    quarter = keys_ref.shape[0] // 4
    keys = jnp.concatenate(
        [
            keys_ref[pl.ds(start, quarter, stride=2)]
            for start in (own, own + 1, mate, mate + 1)
        ]
    )
    wide = HEADS * COUNT
    k0, k1, k2 = pieces(keys, 3)
    q0, q1, q2 = pieces(to_keys[...], 3)
    v0, v1 = pieces(to_values[...], 2)
    scores = single(
        jnp.concatenate([k0, k0, k1, k0, k2, k1], 1), jnp.concatenate([q0, q1, q0, q2, q0, q1])
    )
    d_probs = single(jnp.concatenate([k0, k0, k1], 1), jnp.concatenate([v0, v1, v0]))
    weights = jnp.exp(scores - jnp.max(scores, 0, keepdims=True))
    probs = weights * (1.0 / jnp.sum(weights, 0, keepdims=True))
    t0, t1 = pieces(keys.T, 2)
    both_t = jnp.concatenate([t0, t1])

    def by_keys(high, low):
        twice = single(both_t, high)
        return twice[:CHANNELS] + (twice[CHANNELS:] + single(t0, low))

    d_scores = probs * (d_probs - jnp.sum(d_probs * probs, 0, keepdims=True))
    d0, d1 = pieces(d_scores, 2)
    p0, p1 = pieces(probs[:, :wide], 2)
    keyed = by_keys(jnp.concatenate([d0, p0], 1), jnp.concatenate([d1, p1], 1))
    d_query_keys, att_keys = keyed[:, : d0.shape[1]], keyed[:, d0.shape[1] :]
    d0, d1 = d0[:, :wide], d1[:, :wide]
    large = jnp.concatenate([q0[:, :wide], v0[:, :wide]], 1)
    small = jnp.concatenate([q1[:, :wide], v1[:, :wide]], 1)
    twice = single(
        jnp.concatenate([d0, p0], 1), jnp.concatenate([large, small]), BOTH
    )
    sums = twice[:, :CHANNELS] + (
        twice[:, CHANNELS:] + single(jnp.concatenate([d1, p1], 1), large, BOTH)
    )
    upper = top_half()
    left = lax.broadcasted_iota(jnp.int32, (CHANNELS, CHANNELS), 1) < WIDTH

    def heads(first, second, mask=upper):
        return jnp.where(mask, first, second)

    def rows(value):
        return jnp.concatenate([value[:, :COUNT], value[:, COUNT:wide]])

    att = three(w_value[...], att_keys, FIRST)
    att_t = heads(att[:, :COUNT], att[:, COUNT:])
    d_query = three(w_key[...] * SCALE, d_query_keys, FIRST)
    dq_t = heads(d_query[:, :COUNT], d_query[:, COUNT:wide])
    ring = d_query[:, wide:]
    ring = jnp.where(upper[:, :RING], ring[:, :RING], ring[:, RING:])
    g_query = three(normed_t[...], dq_t, BOTH)
    g_out = three(att_t, grad_t[...], BOTH)
    g_key = three(rows(d_query_keys), query_t[...], BOTH)
    g_key = heads(g_key[:CHANNELS], g_key[CHANNELS:], left) * SCALE
    g_value = three(rows(att_keys), d_att_t[...], BOTH)
    g_value = heads(g_value[:CHANNELS], g_value[CHANNELS:], left)
    att_out[...] = three(att_t, w_out[...], FIRST)
    back = w_query[...].T
    d_normed[...] = three(dq_t, back, FIRST)
    d_ring[...] = three(ring, back, FIRST)
    first = core == 0
    by_core = ((g_query, g_key), (g_value, g_out))
    for half in range(2):
        at = half * CHANNELS
        zero, one = by_core[0][half], by_core[1][half]
        own_out[at : at + CHANNELS, 2 * CHANNELS :] = jnp.where(first, zero, one)
        mate_out[at : at + CHANNELS, 2 * CHANNELS :] = jnp.where(first, one, zero)
    own_out[:, :CHANNELS] = sums[:quarter]
    own_out[:, CHANNELS : 2 * CHANNELS] = sums[quarter : 2 * quarter]
    mate_out[:, :CHANNELS] = sums[2 * quarter : 3 * quarter]
    mate_out[:, CHANNELS : 2 * CHANNELS] = sums[3 * quarter :]


def middle_kernel(sums, pooled, d_normed, normed, inv, grad, padded, d_mixed_out, message, share):
    window = float(WIN_ROWS * COLS)
    share[...] = jnp.zeros(share.shape, jnp.float32)
    half = WIN_ROWS * COLS
    for cell in range(CELLS):
        part = slice(cell * CHANNELS, (cell + 1) * CHANNELS)
        d_pooled = norm_back(
            sums[:, part], pooled[cell : cell + 1], pooled[CELLS + cell : CELLS + cell + 1]
        )
        d_pooled = d_pooled * (1.0 / window)
        share[cell : cell + 1] = d_pooled
        rows = slice(cell * half, (cell + 1) * half)
        back = norm_back(d_normed[rows] + d_pooled, normed[rows], inv[rows])
        back = grad[rows] + back
        d_mixed_out[cell * WIN_ROWS : (cell + 1) * WIN_ROWS] = back.reshape(
            WIN_ROWS, COLS, CHANNELS
        )
    share[CELLS : CELLS + 1] = sums[:, CELLS * CHANNELS :]
    d_mixed = d_mixed_out[...]
    for i in range(3):
        for j in range(3):
            products = padded[1 + i : 1 + i + ROWS, 1 + j : 1 + j + COLS] * d_mixed
            at = CELLS + 1 + 3 * i + j
            share[at : at + 1] = jnp.sum(jnp.sum(products, 0), 0, keepdims=True)
    message[...] = jnp.broadcast_to(share[...][None], message.shape)


def relay_kernel(received, message, share):
    peers = received.shape[0]
    row = here()[0]
    for k in range(peers):
        share[k : k + 1] = received[k, CELLS : CELLS + 1]
    total = received[0]
    for k in range(1, peers):
        total = total + received[k]
    share[peers : peers + 9] = total[CELLS + 1 : CELLS + 10]
    for d in range(3):
        at = peers + 9 + d * CELLS
        near = jnp.clip(row + d - 1, 0, peers - 1)
        share[at : at + CELLS] = received[near % 2 * (peers // 2) + near // 2, 0:CELLS]
    share[31:32] = jnp.zeros((1, CHANNELS), jnp.float32)
    message[...] = jnp.broadcast_to(share[...][None], message.shape)


def end_kernel(
    row_count, col_count, near, d_normed, normed, inv, grad, d_mixed, weight, mixed, att,
    output, d_tokens, g_conv, g_query, g_key, g_value, g_out,
    ring, padded,
):
    row, col, _ = here()
    cores, lines = near.shape[0], near.shape[1]
    first = row_count + 9

    def owner(d_row, d_col, cell):
        k = jnp.clip(col + d_col, 0, col_count - 1)
        at = first + (d_row + 1) * CELLS + cell
        return near[k % 2, k // 2, at : at + 1]

    for start, d_row, cell in ((0, -1, CELLS - 1), (WIDE, 1, 0)):
        ring[start : start + 1] = owner(d_row, -1, cell)
        ring[start + 1 : start + 1 + COLS] = jnp.broadcast_to(
            owner(d_row, 0, cell), (COLS, CHANNELS)
        )
        ring[start + 1 + COLS : start + WIDE] = owner(d_row, 1, cell)
    for start, d_col in ((2 * WIDE, -1), (2 * WIDE + ROWS, 1)):
        for cell in range(CELLS):
            at = start + cell * WIN_ROWS
            ring[at : at + WIN_ROWS] = jnp.broadcast_to(
                owner(0, d_col, cell), (WIN_ROWS, CHANNELS)
            )
    ring[USED:] = jnp.zeros((RING - USED, CHANNELS), jnp.float32)
    back = norm_back(d_normed[...] + ring[...], normed[COUNT:], inv[COUNT:])
    back = grad[COUNT:] + back
    at = lax.broadcasted_iota(jnp.int32, (RING, CHANNELS), 0)
    top, bottom = at < WIDE, (at >= WIDE) & (at < 2 * WIDE)
    left = ((at >= 2 * WIDE) & (at < 2 * WIDE + ROWS)) | (at == 0) | (at == WIDE)
    right = (at >= 2 * WIDE + ROWS) | (at == WIDE - 1) | (at == 2 * WIDE - 1)
    outside = (
        (top & (row == 0))
        | (bottom & (row == row_count - 1))
        | (left & (col == 0))
        | (right & (col == col_count - 1))
    )
    ring[...] = jnp.where(outside, 0.0, back)
    padded[0, 0:WIDE] = ring[0:WIDE]
    padded[ROWS + 1, 0:WIDE] = ring[WIDE : 2 * WIDE]
    for r in range(ROWS):
        k = 2 * WIDE + r
        padded[1 + r, 0:1] = ring[k : k + 1]
        padded[1 + r, WIDE - 1 : WIDE] = ring[k + ROWS : k + ROWS + 1]
    padded[1 : 1 + ROWS, 1 : 1 + COLS] = d_mixed[...]
    total = d_mixed[...]
    for i in range(3):
        for j in range(3):
            total = (
                total
                + weight[3 * i + j : 3 * i + j + 1][None]
                * padded[2 - i : 2 - i + ROWS, 2 - j : 2 - j + COLS]
            )
    d_tokens[...] = total
    output[...] = mixed[...] + att[...].reshape(ROWS, COLS, CHANNELS)
    root = float(COUNT * row_count * col_count) ** (-0.5)
    conv = near[0, 0, row_count:first]
    for k in range(1, cores * lines):
        conv = conv + near[k // lines, k % lines, row_count:first]
    conv = conv * root
    for k in range(9):
        g_conv[k // 3, k % 3 : k % 3 + 1] = conv[k : k + 1]
    blocks = ((g_query, root), (g_key, 1.0 / POOL), (g_value, 1.0 / POOL), (g_out, root))
    for k in range(cores * lines):
        out, factor = blocks[k * row_count // CHANNELS]
        at = k * row_count % CHANNELS
        out[at : at + row_count] = near[k // lines, k % lines, 0:row_count] * factor


def body(tokens, cotangent, conv_weight, w_query, w_key, w_value, w_out):
    row_count, col_count = lax.axis_size(ROW), lax.axis_size(COL)
    chips, lines = lax.axis_size(CHIPS), lax.axis_size(CHIP_COL)
    core = lax.axis_index("c")
    tile = (ROWS, COLS, CHANNELS)
    square = (CHANNELS, CHANNELS)
    all_tokens = (COUNT + RING, CHANNELS)

    anywhere = pl.BlockSpec(memory_space=pl.ANY)
    mine, mates = pl.pallas_call(
        edge_kernel,
        out_shape=[pltpu.VMEM((3, COLS, CHANNELS), jnp.float32)] * 2,
        in_specs=[anywhere] * 2,
        out_specs=[pl.BlockSpec(memory_space=pltpu.VMEM)] * 2,
        scratch_shapes=[pltpu.SemaphoreType.DMA((4,))],
    )(tokens, cotangent)
    mates = pair_gather(mates, "c")
    (strips,) = call(both_kernel, [f32(2, 3, COLS, CHANNELS)], mine, mates)
    pairs = [[4 * k, 4 * k + 2] for k in range(row_count // 2)]
    pairs += [[2 * j + 1, 2 * k + 1] for j, k in seam(ROW)]
    strips = pair_gather(strips, ROW + ("c",), pairs)
    shared, taps = call(
        functools.partial(reach_kernel, row_count - 1),
        [f32(FACING + 3 * ROWS, CHANNELS), f32(9, CHANNELS)],
        tokens, cotangent, conv_weight, strips,
    )
    shared = pair_gather(shared, "c")
    above, below, beside, beyond = call(
        side_kernel,
        [f32(3, COLS, CHANNELS)] * 2 + [f32(SIDE, CHANNELS)] * 2,
        tokens, cotangent, shared,
    )
    beyond = pair_gather(beyond, ROW + COL, column_seam())
    message, pooled, padded, mixed, normed, inv_std, grad = call(
        functools.partial(mix_kernel, col_count - 1),
        [
            f32(chips * CELLS, CHANNELS),
            f32(2 * CELLS, CHANNELS),
            f32(ROWS + 4, 24, CHANNELS),
            f32(*tile),
            f32(*all_tokens),
            f32(*all_tokens),
            f32(*all_tokens),
        ],
        tokens, cotangent, above, below, beside, beyond, taps,
        scratch=[(ROWS + 2, 24, CHANNELS)] * 3 + [(SIDE, CHANNELS)] * 2 + [(8, CHANNELS), (chips * CELLS, CHANNELS)],
        copied=1, sems=[pltpu.SemaphoreType.DMA],
    )

    message = message.reshape(chips, CELLS, CHANNELS)
    message = lax.all_to_all(message, CHIPS, 0, 0, tiled=True)
    keys = lax.all_gather(message, "c", axis=0, tiled=True).reshape(-1, CHANNELS)

    columns = HEADS * (COUNT + RING)
    prepared = call(
        before_kernel,
        [f32(CHANNELS, columns)] * 2 + [f32(*square)] * 4,
        normed, grad, w_query, w_key, w_value, w_out,
        flops=1 << 10,
    )
    own, mate, att_out, d_normed, d_ring = call(
        attend_kernel,
        [
            f32(chips, 3 * CHANNELS),
            f32(chips, 3 * CHANNELS),
            f32(*square),
            f32(*square),
            f32(RING, CHANNELS),
        ],
        keys, *prepared, w_query, w_key, w_value, w_out,
        flops=1 << 31,
    )

    received = lax.all_gather(mate, "c", axis=0)
    received = jnp.where(core == 0, received[1], received[0])
    sums = (own + received).reshape(chips, 1, 3 * CHANNELS)
    sums = jnp.sum(lax.all_to_all(sums, CHIPS, 0, 0, tiled=True), 0)
    d_mixed, message = call(
        middle_kernel,
        [f32(*tile), f32(row_count, 16, CHANNELS)],
        sums, pooled, d_normed, normed, inv_std, grad, padded,
        scratch=[(16, CHANNELS)],
    )
    message = lax.all_to_all(message, ROW_GROUP, 0, 0, tiled=True)
    (message,) = call(
        relay_kernel,
        [f32(lines, 32, CHANNELS)],
        message,
        scratch=[(32, CHANNELS)],
    )
    message = lax.all_to_all(message, CHIP_COL, 0, 0, tiled=True)
    near = lax.all_gather(message, "c", axis=0)
    return call(
        functools.partial(end_kernel, row_count, col_count),
        [f32(*tile)] * 2 + [f32(3, 3, CHANNELS)] + [f32(*square)] * 4,
        near, d_ring, normed, inv_std, grad, d_mixed, taps, mixed, att_out,
        scratch=[(RING, CHANNELS), (ROWS + 2, 24, CHANNELS)],
    )


def solution(mesh):
    fine = Mesh(mesh.devices.reshape(8, 2, 2, 8, 2), ("y", "xl", "xh", "z", "c"))
    tile = P(ROW, COL, None)
    return jax.shard_map(
        body,
        mesh=fine,
        in_specs=(tile, tile, P(), P(), P(), P(), P()),
        out_specs=(tile, tile, P(), P(), P(), P(), P()),
        check_vma=False,
    )
```
